32 devices in a mesh: energy: 8 (over y, x, core), orb: 4 (over z).
Axes of the slice: x: 2, y: 2, z: 4, core: 2. Of those that a mesh axis runs over, the one named last changes fastest.
Arguments:
- green: float32 [8, 2, 2048, 2048], P('energy', None, 'orb'), may hold values from -0.75 to 0.75
- sigma: float32 [8, 16, 2, 128, 128], P('energy', 'orb'), may hold values from -0.375 to 0.375
- neighbours: int32 [256, 16], P('orb'), may hold values from 0 to 255, as said below
- phonon_shift: int32 [6], replicated, may hold values from 1 to 4
- phonon_weight: float32 [2, 6], replicated, may hold values from 0.1 to 0.6
- dham: float32 [4096, 3, 8, 8], P('orb'), may hold values from -2 to 2
Outputs:
- scattering: float32 [8, 4096, 128], P('energy', 'orb')
The draws below stay inside these ranges and needn't reach their ends.
Inputs may be any that keep to these rules, and one draw needn't show every extreme that they name: neighbours[a, k] is an atom other than a within 8 atoms of a; every atom has a neighbour exactly 8 atoms away.
All inputs are finite; a program needn't handle non-finite values.
Results may differ from the reference program's by a relative error of at most 0.0003.
Values sent between devices are 32-bit elements; how exact they have to be, the bound alone decides.
No kernel may reach another device: no remote copies, remote signals or barrier semaphores. Data moves between devices by JAX's collectives and lax.ppermute only.
A program may use at most 128 MiB of HBM per device.

```python
import math
import jax
import jax.numpy as jnp
from jax import lax

N = 2048
W = 8
BS = 128
K = 16
REACH = 8
Q = 6
NE = 8
NA = 256
PAIRS = 4096
SHIFT_MAX = 4


def draw_neighbours(key, part):
    atom_ids = jnp.arange(NA, dtype=jnp.int32)
    partner = atom_ids + 1 - 2 * (atom_ids % 2)
    distant = jnp.where(atom_ids + REACH < NA, atom_ids + REACH, atom_ids - REACH)
    key_step, key_side = jax.random.split(jax.random.fold_in(key, 11))
    stride = jax.random.randint(key_step, (NA, K - 2), 1, REACH + 1, dtype=jnp.int32)
    direction = 2 * jax.random.randint(key_side, (NA, K - 2), 0, 2, dtype=jnp.int32) - 1
    ahead = atom_ids[:, None] + direction * stride
    inside = (ahead >= 0) & (ahead < NA)
    chosen = jnp.where(inside, ahead, atom_ids[:, None] - direction * stride)
    return jnp.concatenate([partner[:, None], distant[:, None], chosen], axis=1).astype(jnp.int32)


def draw_phonon_shift(key, part):
    key_values, key_order = jax.random.split(jax.random.fold_in(key, 23))
    others = jax.random.randint(key_values, (Q - 2,), 1, SHIFT_MAX + 1, dtype=jnp.int32)
    fixed_ends = jnp.array([SHIFT_MAX, 1], dtype=jnp.int32)
    joined = jnp.concatenate([fixed_ends, others]).astype(jnp.int32)
    return jax.random.permutation(key_order, joined).astype(jnp.int32)


def level_of(stream_key, extent, pieces, low, largest):
    gain, own = 1.0, jax.random.fold_in(stream_key, 6)
    for dim, shards_of in pieces:
        steps = jnp.exp(jax.random.uniform(jax.random.fold_in(own, dim), (shards_of,), jnp.float32, low / len(pieces), largest / len(pieces)))
        gain = gain * jnp.repeat(steps, extent[dim] // shards_of).reshape([-1 if axis == dim else 1 for axis in range(len(extent))])
    return gain


def normal_values(key, extent, spread, limit, pieces=(), held_as=jnp.bfloat16):
    drawn = spread * jax.random.normal(key, extent, jnp.float32)
    if pieces:
        drawn = drawn * level_of(key, extent, pieces, -0.22, 0.18)
    return jnp.clip(drawn, -limit, limit).astype(held_as)


def setup_inputs(seed: int = 0) -> dict:
    arg_keys = jax.random.split(jax.random.key(seed), 7)
    return {
        "green": normal_values(arg_keys[0], (NE, 2, N, N), ((2 * N) ** -0.25), 0.75, ((0, 8), (2, 4)), jnp.float32),
        "sigma": normal_values(arg_keys[1], (NE, N // BS, 2, BS, BS), (2 * BS) ** -0.5, 0.375, ((0, 8), (1, 4)), jnp.float32),
        "neighbours": draw_neighbours(jax.random.fold_in(arg_keys[6], 71), 0),
        "phonon_shift": draw_phonon_shift(jax.random.fold_in(arg_keys[6], 71), 0),
        "phonon_weight": jnp.clip(jnp.exp(jax.random.uniform(arg_keys[4], (2, Q), jnp.float32, math.log(0.1), math.log(0.6))), 0.1, 0.6),
        "dham": normal_values(arg_keys[5], (PAIRS, 3, W, W), W ** -0.5, 2.0, ((0, 4),), jnp.float32),
    }


HIGHEST = lax.Precision.HIGHEST


def multiply(left, right, form):
    return jnp.einsum(form, left, right, precision=HIGHEST)


def self_energy_product(green_energy, sigma_energy):
    row_count = green_energy.shape[1]
    block_count = sigma_energy.shape[0]
    columns = green_energy.reshape(2, row_count, block_count, BS)
    form = 'rmi,mij->rmj'
    real_part = multiply(columns[0], sigma_energy[:, 0], form) - multiply(columns[1], sigma_energy[:, 1], form)
    imag_part = multiply(columns[0], sigma_energy[:, 1], form) + multiply(columns[1], sigma_energy[:, 0], form)
    return jnp.stack([real_part, imag_part]).reshape(2, row_count, block_count * BS)


def lesser_blocks(green_energy, product, neighbours):
    offsets = jnp.arange(W, dtype=jnp.int32)

    def one_atom(atom):
        mine = lax.dynamic_slice_in_dim(product, atom * W, W, 1)
        wanted = (neighbours[atom][:, None] * W + offsets[None, :]).reshape(-1).astype(jnp.int32)
        nearby = jnp.take(green_energy, wanted, axis=1)
        form = 'wn,vn->wv'
        real_part = multiply(mine[0], nearby[0], form) + multiply(mine[1], nearby[1], form)
        imag_part = multiply(mine[1], nearby[0], form) - multiply(mine[0], nearby[1], form)
        block = jnp.stack([real_part, imag_part]).reshape(2, W, K, W).transpose(2, 0, 1, 3)
        return block.reshape(K, 2 * W * W)

    return lax.map(one_atom, jnp.arange(NA, dtype=jnp.int32)).reshape(NA * K, 2 * W * W)


def build_kernel(phonon_shift, phonon_weight, energies):
    rows_e = jnp.arange(energies, dtype=jnp.int32)[None, :, None]
    cols_f = jnp.arange(energies, dtype=jnp.int32)[None, None, :]
    shifts = phonon_shift[:, None, None]
    emission = (cols_f == rows_e + shifts).astype(jnp.float32)
    absorption = (cols_f == rows_e - shifts).astype(jnp.float32)
    terms = phonon_weight[0][:, None, None] * emission + phonon_weight[1][:, None, None] * absorption
    return jnp.sum(terms, axis=0)


def scatter_blocks(smeared, dham):
    energies, pair_count = smeared.shape[0], smeared.shape[1]
    split = smeared.reshape(energies, pair_count, 2, W, W)
    halfway = jnp.einsum('pcij,epzjk->epczik', dham, split, precision=HIGHEST)
    result = jnp.einsum('epczik,pclk->epzil', halfway, dham, precision=HIGHEST)
    return result.reshape(energies, pair_count, 2 * W * W)


def reference(green, sigma, neighbours, phonon_shift, phonon_weight, dham):
    def per_energy(index):
        green_energy = green[index]
        product = self_energy_product(green_energy, sigma[index])
        return lesser_blocks(green_energy, product, neighbours)

    lesser = lax.map(per_energy, jnp.arange(NE, dtype=jnp.int32))
    kernel = build_kernel(phonon_shift, phonon_weight, NE)
    smeared = jnp.einsum('ef,fpx->epx', kernel, lesser, precision=HIGHEST)
    return scatter_blocks(smeared, dham)
```

```python
import functools

import jax
import jax.numpy as jnp
from jax import lax
from jax.experimental import pallas as pl
from jax.experimental.pallas import tpu as pltpu
from jax.sharding import PartitionSpec as P

W = 8
BS = 128
REACH = 8
MARGIN = REACH * W
HALF = MARGIN // 2
TILE = 128
LANES = 128
F32, BF16 = jnp.float32, jnp.bfloat16

NT = (((1,), (1,)), ((), ()))
NN = (((1,), (0,)), ((), ()))


def halves(x):
    hi = x.astype(BF16)
    return hi, (x - hi.astype(F32)).astype(BF16)


def dot(a, b, dims):
    return lax.dot_general(a, b, dims, preferred_element_type=F32)


def dot3(a, b, dims):
    return dot(a[0], b[0], dims) + dot(a[0], b[1], dims) + dot(a[1], b[0], dims)


def one_block(real, imag, self_real, self_imag, hi_ref, lo_ref, acc_ref, tiles, pad):
    rows = real.shape[0]
    hi, lo = halves(jnp.concatenate([real, imag], axis=1))
    hi_ref[pad : pad + rows, :] = hi
    lo_ref[pad : pad + rows, :] = lo
    weight = halves(
        jnp.concatenate(
            [
                jnp.concatenate([self_real, self_imag], axis=1),
                jnp.concatenate([-self_imag, self_real], axis=1),
            ],
            axis=0,
        )
    )
    for t, (row, window, width) in enumerate(tiles):
        left = (hi_ref[row : row + TILE, :], lo_ref[row : row + TILE, :])
        product = dot3(left, weight, NN)
        turned = jnp.concatenate([product[:, BS:], -product[:, :BS]], axis=1)
        both = halves(jnp.concatenate([product, turned], axis=0))
        near = (hi_ref[window : window + width, :], lo_ref[window : window + width, :])
        acc_ref[t] = acc_ref[t] + dot3(both, near, NT)


def main_tiles(rows):
    return [(MARGIN + t * TILE, t * TILE, TILE + 2 * MARGIN) for t in range(rows // TILE)]


def lesser_kernel(count, first, idx_ref, green_ref, sigma_ref, *rest):
    if first:
        acc_ref, buf, hi_ref, lo_ref, sem = rest
    else:
        before_ref, acc_ref, buf, hi_ref, lo_ref, sem = rest
    rows = green_ref.shape[2]

    def fetch(s):
        col = pl.multiple_of(idx_ref[1, s] * BS, BS)
        return pltpu.make_async_copy(
            green_ref.at[0, :, :, pl.ds(col, BS)], buf.at[s], sem.at[s]
        )

    for s in range(count):
        fetch(s).start()
    acc_ref[...] = jnp.zeros_like(acc_ref) if first else before_ref[...]
    for ref in (hi_ref, lo_ref):
        ref[:MARGIN, :] = jnp.zeros((MARGIN, 2 * BS), BF16)
        ref[MARGIN + rows :, :] = jnp.zeros((MARGIN, 2 * BS), BF16)

    def step(s, carry):
        fetch(s).wait()
        at = idx_ref[0, s]
        one_block(
            buf[s, 0], buf[s, 1], sigma_ref[0, at, 0], sigma_ref[0, at, 1],
            hi_ref, lo_ref, acc_ref, main_tiles(rows), MARGIN,
        )
        return carry

    lax.fori_loop(0, count, step, 0)


def lesser_part(green, sigma, index, before):
    rows, count = green.shape[2], index.shape[1]
    tiles = rows // TILE
    first = before is None
    acc = jax.ShapeDtypeStruct((tiles, 2 * TILE, TILE + 2 * MARGIN), F32)
    vmem = pl.BlockSpec(memory_space=pltpu.VMEM)
    return pl.pallas_call(
        functools.partial(lesser_kernel, count, first),
        out_shape=acc,
        in_specs=[
            pl.BlockSpec(memory_space=pltpu.SMEM),
            pl.BlockSpec(memory_space=pl.ANY),
            vmem,
        ]
        + ([] if first else [vmem]),
        out_specs=vmem,
        scratch_shapes=[
            pltpu.VMEM((count, 2, rows, BS), F32),
            pltpu.VMEM((rows + 2 * MARGIN, 2 * BS), BF16),
            pltpu.VMEM((rows + 2 * MARGIN, 2 * BS), BF16),
            pltpu.SemaphoreType.DMA((count,)),
        ],
        input_output_aliases={} if first else {3: 0},
        compiler_params=pltpu.CompilerParams(vmem_limit_bytes=24 << 20),
        cost_estimate=pl.CostEstimate(
            flops=count * 6 * rows * 2 * BS * (2 * BS + 4 * TILE),
            bytes_accessed=count * rows * BS * 8 + 8 * tiles * TILE * 512,
            transcendentals=0,
        ),
        name="lesser_own" if first else "lesser_more",
    )(index, green, sigma, *([] if first else [before]))


def edge_kernel(
    blocks, flag_ref, green_ref, a_ref, b_ref, c_ref, sig0_ref, sig1_ref,
    left_ref, right_ref, own_ref, buf, hi_ref, lo_ref, acc_ref, sem,
):
    rows = green_ref.shape[2]
    tiles = [(0, 0, TILE), (TILE, TILE, TILE)]
    size = 2 * TILE

    def fetch(s):
        cols = pl.ds(pl.multiple_of(s * BS, BS), BS)
        slot = lax.rem(s, 2)
        parts = [
            (a_ref.at[:, :, cols], 0),
            (b_ref.at[:, :, cols], HALF),
            (green_ref.at[0, :, pl.ds(0, MARGIN), cols], MARGIN),
            (green_ref.at[0, :, pl.ds(rows - MARGIN, MARGIN), cols], TILE),
            (c_ref.at[:, :, cols], TILE + MARGIN),
            (a_ref.at[:, :, cols], TILE + MARGIN + HALF),
        ]
        return [
            pltpu.make_async_copy(
                src, buf.at[slot, :, pl.ds(at, src.shape[1]), :], sem.at[slot, k]
            )
            for k, (src, at) in enumerate(parts)
        ]

    acc_ref[...] = jnp.zeros_like(acc_ref)

    @pl.when(flag_ref[0] == 1)
    def _():
        for copy in fetch(0):
            copy.start()
        row = lax.broadcasted_iota(jnp.int32, (size, BS), 0)
        keep = (row >= HALF) | (flag_ref[1] == 1)
        keep &= (row < TILE) | (row >= TILE + MARGIN) | (row < TILE + flag_ref[3])
        keep &= (row < size - HALF) | (flag_ref[2] == 1)

        def step(s, carry):
            for copy in fetch(s):
                copy.wait()

            @pl.when(s + 1 < blocks)
            def _():
                for copy in fetch(s + 1):
                    copy.start()

            slot = lax.rem(s, 2)
            real = jnp.where(keep, buf[slot, 0], 0.0)
            imag = jnp.where(keep, buf[slot, 1], 0.0)
            owner, local = s // flag_ref[4], lax.rem(s, flag_ref[4])
            piece = flag_ref[4] // 2
            at = owner * piece + lax.rem(local, piece)
            low = local < piece
            self_real = jnp.where(low, sig0_ref[0, at, 0], sig1_ref[0, at, 0])
            self_imag = jnp.where(low, sig0_ref[0, at, 1], sig1_ref[0, at, 1])
            one_block(real, imag, self_real, self_imag, hi_ref, lo_ref, acc_ref, tiles, 0)
            return carry

        lax.fori_loop(0, blocks, step, 0)

    lane = lax.broadcasted_iota(jnp.int32, (MARGIN, LANES), 1)
    low = lane < MARGIN
    for part in range(2):
        base = part * TILE
        outer_l = acc_ref[0, base : base + MARGIN, :]
        inner_l = acc_ref[0, base + MARGIN : base + TILE, :]
        inner_r = acc_ref[1, base : base + MARGIN, :]
        outer_r = acc_ref[1, base + MARGIN : base + TILE, :]
        left_ref[part] = jnp.where(low, 0.0, outer_l)
        right_ref[part] = jnp.where(low, outer_r, 0.0)
        own_ref[0, part] = jnp.where(low, inner_l, 0.0)
        own_ref[1, part] = jnp.where(low, 0.0, inner_r)


def edge_part(flags, green, a, b, c, sig0, sig1):
    blocks = sig0.shape[1] + sig1.shape[1]
    vmem = pl.BlockSpec(memory_space=pltpu.VMEM)
    hbm = pl.BlockSpec(memory_space=pl.ANY)
    side = jax.ShapeDtypeStruct((2, MARGIN, LANES), F32)
    size = 2 * TILE
    return pl.pallas_call(
        functools.partial(edge_kernel, blocks),
        out_shape=(side, side, jax.ShapeDtypeStruct((2, 2, MARGIN, LANES), F32)),
        in_specs=[pl.BlockSpec(memory_space=pltpu.SMEM), hbm, hbm, hbm, hbm, vmem, vmem],
        out_specs=(vmem, vmem, vmem),
        scratch_shapes=[
            pltpu.VMEM((2, 2, size, BS), F32),
            pltpu.VMEM((size, 2 * BS), BF16),
            pltpu.VMEM((size, 2 * BS), BF16),
            pltpu.VMEM((2, 2 * TILE, TILE), F32),
            pltpu.SemaphoreType.DMA((2, 6)),
        ],
        compiler_params=pltpu.CompilerParams(vmem_limit_bytes=16 << 20),
        cost_estimate=pl.CostEstimate(
            flops=blocks * 6 * size * 2 * BS * (2 * BS + 2 * TILE),
            bytes_accessed=blocks * size * BS * 8 + blocks * BS * BS * 8,
            transcendentals=0,
        ),
        name="edges",
    )(flags, green, a, b, c, sig0, sig1)


def band_kernel(acc_ref, own_ref, from_left_ref, from_right_ref, out_ref, rows_ref):
    tiles = acc_ref.shape[0]
    group = out_ref.shape[2]
    per_tile = TILE // W
    for t in range(tiles):
        for part in range(2):
            base = part * TILE
            x = acc_ref[t, base : base + TILE, :]
            rows_ref[t, part] = x
            if t == 0:
                extra = own_ref[0, part] + from_left_ref[part]
                rows_ref[t, part, :MARGIN, :LANES] = x[:MARGIN, :LANES] + extra
            if t == tiles - 1:
                extra = own_ref[1, part] + from_right_ref[part]
                rows_ref[t, part, MARGIN:, LANES:] = x[MARGIN:, LANES:] + extra
    low = lax.broadcasted_iota(jnp.int32, (W, LANES), 1) < MARGIN
    width = TILE + 2 * MARGIN
    for a in range(per_tile):
        for t in range(tiles):
            atom = t * per_tile + a
            for part in range(2):
                x = rows_ref[t, part, a * W : (a + 1) * W, :]
                before = pltpu.roll(x, (width - a * W) % width, 1)[:, :LANES]
                after = pltpu.roll(x, (width - (a + 1) * W) % width, 1)[:, :LANES]
                out_ref[atom // group, part, atom % group] = jnp.where(low, before, after)


def band(acc, own, from_left, from_right, energies):
    tiles = acc.shape[0]
    atoms = tiles * TILE // W
    vmem = pl.BlockSpec(memory_space=pltpu.VMEM)
    return pl.pallas_call(
        band_kernel,
        out_shape=jax.ShapeDtypeStruct((energies, 2, atoms // energies, W, LANES), F32),
        in_specs=[vmem] * 4,
        out_specs=vmem,
        scratch_shapes=[pltpu.VMEM((tiles, 2, TILE, TILE + 2 * MARGIN), F32)],
        compiler_params=pltpu.CompilerParams(vmem_limit_bytes=16 << 20),
        name="band",
    )(acc, own, from_left, from_right)


def picks_kernel(where_ref, out_ref):
    rows = out_ref.shape[0]
    padded = where_ref.shape[1]
    entry = lax.broadcasted_iota(jnp.int32, (rows, padded), 0)
    first = where_ref[...] * W
    for j in range(W):
        hit = entry == first + j
        out_ref[:, j * padded : (j + 1) * padded] = jnp.where(hit, 1.0, 0.0).astype(BF16)


def picks(where, rows):
    padded = where.shape[1]
    vmem = pl.BlockSpec(memory_space=pltpu.VMEM)
    return pl.pallas_call(
        picks_kernel,
        out_shape=jax.ShapeDtypeStruct((rows, W * padded), BF16),
        in_specs=[vmem],
        out_specs=vmem,
        compiler_params=pltpu.CompilerParams(vmem_limit_bytes=16 << 20),
        name="picks",
    )(where)


def scatter_kernel(recv_ref, pick_ref, mix_ref, dham_ref, out_ref, smeared_ref, result_ref):
    energies, _, group, _, _ = recv_ref.shape
    padded = dham_ref.shape[1]
    pairs = out_ref.shape[1]
    columns = [
        recv_ref[:, :, a, :, :].reshape(energies * 2 * W, LANES) for a in range(group)
    ]
    received = halves(jnp.concatenate(columns, axis=1))
    mixed = halves(dot3(halves(mix_ref[...]), received, NN))
    smeared_ref[...] = dot(mixed[0], pick_ref[...], NN) + dot(mixed[1], pick_ref[...], NN)

    def block(part, j, k):
        row = (part * W + j) * energies
        return smeared_ref[row : row + energies, k * padded : (k + 1) * padded]

    def factor(c, i, j):
        row = (c * W + i) * W + j
        return dham_ref[row : row + 1, :]

    for part in range(2):
        for i in range(W):
            total = [None] * W
            for c in range(3):
                for k in range(W):
                    t = None
                    for j in range(W):
                        term = factor(c, i, j) * block(part, j, k)
                        t = term if t is None else t + term
                    for l in range(W):
                        term = t * factor(c, l, k)
                        total[l] = term if total[l] is None else total[l] + term
            for l in range(W):
                row = ((part * W + i) * W + l) * energies
                result_ref[row : row + energies, :] = total[l]
    for e in range(energies):
        one = result_ref[pl.ds(e, 2 * W * W, stride=energies), :]
        out_ref[e] = one.T[:pairs, :]


def scatter(recv, pick, mix, dham, pairs):
    energies, _, group, _, _ = recv.shape
    padded = dham.shape[1]
    vmem = pl.BlockSpec(memory_space=pltpu.VMEM)
    return pl.pallas_call(
        scatter_kernel,
        out_shape=jax.ShapeDtypeStruct((energies, pairs, 2 * W * W), F32),
        in_specs=[vmem] * 4,
        out_specs=vmem,
        scratch_shapes=[
            pltpu.VMEM((2 * W * energies, W * padded), F32),
            pltpu.VMEM((2 * W * W * energies, padded), F32),
        ],
        compiler_params=pltpu.CompilerParams(vmem_limit_bytes=24 << 20),
        name="scatter",
    )(recv, pick, mix, dham)


def build_kernel(phonon_shift, phonon_weight, energies):
    rows_e = jnp.arange(energies, dtype=jnp.int32)[None, :, None]
    cols_f = jnp.arange(energies, dtype=jnp.int32)[None, None, :]
    shifts = phonon_shift[:, None, None]
    emission = (cols_f == rows_e + shifts).astype(F32)
    absorption = (cols_f == rows_e - shifts).astype(F32)
    terms = (
        phonon_weight[0][:, None, None] * emission + phonon_weight[1][:, None, None] * absorption
    )
    return jnp.sum(terms, axis=0)


def build_mix(phonon_shift, phonon_weight, energies):
    kernel = build_kernel(phonon_shift, phonon_weight, energies)
    same = jnp.eye(2 * W, dtype=F32)
    mix = same[:, None, None, :] * kernel[None, :, :, None]
    return mix.reshape(2 * W * energies, energies * 2 * W)


def send(x, pairs):
    return lax.ppermute(x, "orb", pairs)


def per_device(green, sigma, neighbours, phonon_shift, phonon_weight, dham):
    energies = lax.axis_size("energy")
    peers = lax.axis_size("orb")
    e, z = lax.axis_index("energy"), lax.axis_index("orb")
    rows = green.shape[2]
    atoms = rows // W
    degree = neighbours.shape[1]
    group = atoms // energies
    pairs = group * degree
    padded = -(-pairs // LANES) * LANES
    held = sigma.shape[1]
    piece = held // 2

    sig = [
        lax.all_gather(sigma[:, h * piece : (h + 1) * piece], "orb", axis=1, tiled=True)
        for h in range(2)
    ]

    far = peers >= 4
    up = [(i, i + 1) for i in range(peers - 1)]
    down = [(i + 1, i) for i in range(peers - 1)]
    near_right = send(green[0, :, rows - HALF :], up[:-1] if far else up)
    near_left = send(green[0, :, :HALF], down[1:] if far else down)
    if far:
        more = jnp.where(
            z == 0, green[0, :, rows - MARGIN : rows - HALF], green[0, :, HALF:MARGIN]
        )
        other = send(more, [(0, 1), (peers - 1, peers - 2)])
        from_left, from_right = z == 1, z == peers - 2
        active = (z > 0) & (z < peers - 1)
    else:
        other = jnp.zeros_like(near_left)
        from_left = from_right = jnp.zeros((), bool)
        active = jnp.ones((), bool)
    limit = jnp.where(from_right, MARGIN, HALF)
    flags = jnp.stack(
        [x.astype(jnp.int32) for x in (active, from_left, from_right, limit)]
        + [jnp.int32(held)]
    )

    slot = jnp.arange(held, dtype=jnp.int32)
    acc = lesser_part(green, sigma, jnp.stack([slot, z * held + slot]), None)
    slot = jnp.arange((peers - 1) * piece, dtype=jnp.int32)
    owner = lax.rem(z + 1 + slot // piece, peers)
    at = slot % piece
    for h in range(2):
        index = jnp.stack([owner * piece + at, owner * held + h * piece + at])
        acc = lesser_part(green, sig[h], index, acc)
    to_left, to_right, own = edge_part(
        flags, green, other, near_right, near_left, sig[0], sig[1]
    )
    back_right = send(to_left, down)
    back_left = send(to_right, up)
    lesser = band(acc, own, back_left, back_right, energies)

    mine = lax.dynamic_slice_in_dim(neighbours, e * group, group, axis=0)
    first = z * atoms + e * group
    offset = mine - (first + jnp.arange(group, dtype=jnp.int32))[:, None]
    column = jnp.where(offset < 0, offset + REACH, offset + REACH - 1)
    where = column + 2 * REACH * jnp.arange(group, dtype=jnp.int32)[:, None]
    where = jnp.pad(where.reshape(1, pairs), ((0, 0), (0, padded - pairs)), constant_values=-1)
    pick = picks(where, group * LANES)
    mix = build_mix(phonon_shift, phonon_weight, energies)
    factors = lax.dynamic_slice_in_dim(
        dham.transpose(1, 2, 3, 0).reshape(3 * W * W, -1), e * pairs, pairs, axis=1
    )
    factors = jnp.pad(factors, ((0, 0), (0, padded - pairs)))

    recv = lax.all_to_all(lesser, "energy", split_axis=0, concat_axis=0, tiled=True)
    spread = scatter(recv, pick, mix, factors, pairs)
    result = lax.all_to_all(spread, "energy", split_axis=0, concat_axis=0, tiled=True)
    return result.reshape(1, atoms * degree, 2 * W * W)


def solution(mesh):
    return jax.shard_map(
        per_device,
        mesh=mesh,
        in_specs=(
            P("energy", None, "orb", None),
            P("energy", "orb", None, None, None),
            P("orb", None),
            P(),
            P(),
            P("orb", None, None, None),
        ),
        out_specs=P("energy", "orb", None),
        check_vma=False,
    )
```

```python
import functools

import jax
import jax.numpy as jnp
from jax import lax
from jax.experimental import pallas as pl
from jax.experimental.pallas import tpu as pltpu
from jax.sharding import PartitionSpec as P

W = 8
BS = 128
REACH = 8
MARGIN = REACH * W
HALF = MARGIN // 2
TILE = 128
LANES = 128
F32, BF16 = jnp.float32, jnp.bfloat16

NT = (((1,), (1,)), ((), ()))
NN = (((1,), (0,)), ((), ()))


def halves(x):
    hi = x.astype(BF16)
    return hi, (x - hi.astype(F32)).astype(BF16)


def dot(a, b, dims):
    return lax.dot_general(a, b, dims, preferred_element_type=F32)


def dot3(a, b, dims):
    return dot(a[0], b[0], dims) + dot(a[0], b[1], dims) + dot(a[1], b[0], dims)


def blocks_at_once(held):
    return 2 if held % 2 == 0 else 1


def some_blocks(fields, weights, hi_ref, lo_ref, acc_ref, edges):
    rows = fields[0][0].shape[0]
    wide = 2 * BS
    hi, lo = halves(jnp.concatenate([x for pair in fields for x in pair], axis=1))
    hi_ref[MARGIN : MARGIN + rows, :] = hi
    lo_ref[MARGIN : MARGIN + rows, :] = lo
    split = []
    for real, imag in weights:
        top = jnp.concatenate([real, imag], axis=1)
        split.append(halves(jnp.concatenate([top, jnp.concatenate([-imag, real], axis=1)], axis=0)))
    tiles = rows // TILE
    for t in range(tiles):
        row, window = MARGIN + t * TILE, t * TILE
        both = []
        for n, weight in enumerate(split):
            cols = slice(n * wide, (n + 1) * wide)
            left = (hi_ref[row : row + TILE, cols], lo_ref[row : row + TILE, cols])
            product = dot3(left, weight, NN)
            turned = jnp.concatenate([product[:, BS:], -product[:, :BS]], axis=1)
            both.append(halves(jnp.concatenate([product, turned], axis=0)))
            if edges is not None:
                for ref, part in zip(edges, both[-1]):
                    if t == 0:
                        ref[n, :MARGIN, :] = part[:MARGIN]
                    if t == tiles - 1:
                        ref[n, 3 * MARGIN :, :] = part[TILE - MARGIN : TILE]
        both = [jnp.concatenate(parts, axis=1) for parts in zip(*both)]
        upto = window + TILE + 2 * MARGIN
        acc_ref[t] = acc_ref[t] + dot3(both, (hi_ref[window:upto, :], lo_ref[window:upto, :]), NT)
    if edges is not None:
        for n, weight in enumerate(split):
            cols = slice(n * wide, (n + 1) * wide)
            outer = [
                jnp.concatenate(
                    [ref[MARGIN : 2 * MARGIN, cols], ref[rows : rows + MARGIN, cols]], axis=0
                )
                for ref in (hi_ref, lo_ref)
            ]
            for ref, part in zip(edges, halves(dot3(outer, weight, NT))):
                ref[n, MARGIN : 3 * MARGIN, :] = part


def lesser_kernel(shards, first, idx_ref, green_ref, *rest):
    sigmas, rest = rest[:shards], rest[shards:]
    if not first:
        before_ref, rest = rest[0], rest[1:]
    acc_ref, keep_hi_ref, keep_lo_ref, buf, hi_ref, lo_ref, sem = rest
    rows, held = green_ref.shape[2], sigmas[0].shape[1]
    once = blocks_at_once(held)

    def fetch(shard, s):
        col = pl.multiple_of((idx_ref[shard] * held + s) * BS, BS)
        at = shard * held + s
        return pltpu.make_async_copy(
            green_ref.at[0, :, :, pl.ds(col, BS)], buf.at[at], sem.at[at]
        )

    def valid(shard):
        return idx_ref[shards + shard] == 1

    for shard in range(shards):

        @pl.when(valid(shard))
        def _():
            for s in range(held):
                fetch(shard, s).start()

    acc_ref[...] = jnp.zeros_like(acc_ref) if first else before_ref[...]
    for ref in (hi_ref, lo_ref):
        ref[:MARGIN, :] = jnp.zeros((MARGIN, ref.shape[1]), BF16)
        ref[MARGIN + rows :, :] = jnp.zeros((MARGIN, ref.shape[1]), BF16)

    for shard in range(shards):

        @pl.when(valid(shard))
        def _():
            def step(g, carry):
                fields, weights = [], []
                for n in range(once):
                    s = g * once + n
                    fetch(shard, s).wait()
                    at = shard * held + s
                    fields.append((buf[at, 0], buf[at, 1]))
                    weights.append((sigmas[shard][0, s, 0], sigmas[shard][0, s, 1]))
                slots = pl.ds(shard * held + g * once, once)
                some_blocks(
                    fields, weights, hi_ref, lo_ref, acc_ref,
                    (keep_hi_ref.at[slots], keep_lo_ref.at[slots]),
                )
                return carry

            lax.fori_loop(0, held // once, step, 0)


def lesser_part(green, sigmas, index, before):
    rows, held, shards = green.shape[2], sigmas[0].shape[1], len(sigmas)
    tiles, count = rows // TILE, held * shards
    once = blocks_at_once(held)
    first = before is None
    vmem = pl.BlockSpec(memory_space=pltpu.VMEM)
    keep = jax.ShapeDtypeStruct((count, 4 * MARGIN, 2 * BS), BF16)
    return pl.pallas_call(
        functools.partial(lesser_kernel, shards, first),
        out_shape=(
            jax.ShapeDtypeStruct((tiles, 2 * TILE, TILE + 2 * MARGIN), F32),
            keep,
            keep,
        ),
        in_specs=[
            pl.BlockSpec(memory_space=pltpu.SMEM),
            pl.BlockSpec(memory_space=pltpu.HBM),
        ]
        + [vmem] * (shards if first else shards + 1),
        out_specs=(vmem, vmem, vmem),
        scratch_shapes=[
            pltpu.VMEM((count, 2, rows, BS), F32),
            pltpu.VMEM((rows + 2 * MARGIN, once * 2 * BS), BF16),
            pltpu.VMEM((rows + 2 * MARGIN, once * 2 * BS), BF16),
            pltpu.SemaphoreType.DMA((count,)),
        ],
        input_output_aliases={} if first else {2 + shards: 0},
        compiler_params=pltpu.CompilerParams(vmem_limit_bytes=24 << 20),
        cost_estimate=pl.CostEstimate(
            flops=held * 6 * rows * 2 * BS * (2 * BS + 4 * TILE),
            bytes_accessed=held * rows * BS * 8 + 8 * tiles * TILE * 512,
            transcendentals=0,
        ),
        name="lesser_own" if first else "lesser_more",
    )(index, green, *sigmas, *([] if first else [before]))


def edge_kernel(counts, idx_ref, a_ref, b_ref, c_ref, *rest):
    parts = len(counts)
    keeps, rest = rest[: 2 * parts], rest[2 * parts :]
    left_ref, right_ref, own_ref, acc_ref = rest
    base = 2 * sum(counts)
    active, from_left, from_right = [idx_ref[base + k] == 1 for k in range(3)]
    limit = idx_ref[base + 3]
    acc_ref[...] = jnp.zeros_like(acc_ref)

    def add(col, keep_hi, keep_lo):
        cols = pl.ds(pl.multiple_of(col * BS, BS), BS)
        more = [a_ref[part, :, cols] for part in range(2)]
        near = [b_ref[part, :, cols] for part in range(2)]
        after = [c_ref[part, :, cols] for part in range(2)]
        sides = []
        for part in range(2):
            outer = jnp.where(from_left, more[part], 0.0)
            beyond = jnp.where(from_right, more[part], 0.0)
            sides.append(
                (
                    jnp.concatenate([outer, near[part]], axis=0),
                    jnp.concatenate([after[part], beyond], axis=0),
                )
            )
        for side in range(2):
            real, imag = sides[0][side], sides[1][side]
            halo = jnp.concatenate(
                [
                    jnp.concatenate([real, imag], axis=1),
                    jnp.concatenate([-imag, real], axis=1),
                ],
                axis=0,
            )
            rows = slice(side * TILE, (side + 1) * TILE)
            acc_ref[side] = acc_ref[side] + dot3(
                halves(halo), (keep_hi[rows, :], keep_lo[rows, :]), NT
            )

    @pl.when(active)
    def _():
        shard = 0
        for part, count in enumerate(counts):
            hi, lo = keeps[2 * part], keeps[2 * part + 1]
            held = hi.shape[0] // count
            for k in range(count):
                number, valid = idx_ref[2 * shard], idx_ref[2 * shard + 1]
                shard += 1

                @pl.when(valid == 1)
                def _():
                    def step(s, carry):
                        at = k * held + s
                        add(number * held + s, hi.at[at], lo.at[at])
                        return carry

                    lax.fori_loop(0, held, step, 0)

    lane = lax.broadcasted_iota(jnp.int32, (MARGIN, LANES), 1)
    row = lax.broadcasted_iota(jnp.int32, (MARGIN, LANES), 0)
    low = lane < MARGIN
    left, right = acc_ref[0], acc_ref[1]
    turned_left, turned_right = left.T[:MARGIN], right.T[MARGIN:]
    left_ref[0] = jnp.where(low, 0.0, left[:MARGIN])
    left_ref[1] = jnp.where(low, 0.0, -left[MARGIN:])
    right_ref[0] = jnp.where(lane < limit, right[:MARGIN], 0.0)
    right_ref[1] = jnp.where(lane < limit, -right[MARGIN:], 0.0)
    own_ref[0, 0] = jnp.where(low, turned_left, 0.0)
    own_ref[0, 1] = jnp.where(low, pltpu.roll(turned_left, MARGIN, 1), 0.0)
    mine = jnp.logical_and(row < limit, lane >= MARGIN)
    own_ref[1, 0] = jnp.where(mine, pltpu.roll(turned_right, MARGIN, 1), 0.0)
    own_ref[1, 1] = jnp.where(mine, turned_right, 0.0)


def edge_part(flags, a, b, c, keeps, counts):
    vmem = pl.BlockSpec(memory_space=pltpu.VMEM)
    side = jax.ShapeDtypeStruct((2, MARGIN, LANES), F32)
    return pl.pallas_call(
        functools.partial(edge_kernel, counts),
        out_shape=(side, side, jax.ShapeDtypeStruct((2, 2, MARGIN, LANES), F32)),
        in_specs=[pl.BlockSpec(memory_space=pltpu.SMEM)] + [vmem] * (3 + len(keeps)),
        out_specs=(vmem, vmem, vmem),
        scratch_shapes=[pltpu.VMEM((2, TILE, TILE), F32)],
        compiler_params=pltpu.CompilerParams(vmem_limit_bytes=24 << 20),
        cost_estimate=pl.CostEstimate(
            flops=a.shape[2] * 2 * 12 * TILE * 2 * TILE,
            bytes_accessed=a.shape[2] * 2 * 4 * TILE * 4,
            transcendentals=0,
        ),
        name="edges",
    )(flags, a, b, c, *keeps)


def band_kernel(acc_ref, own_ref, from_left_ref, from_right_ref, out_ref, rows_ref):
    tiles = acc_ref.shape[0]
    group = out_ref.shape[2]
    per_tile = TILE // W
    for t in range(tiles):
        for part in range(2):
            base = part * TILE
            x = acc_ref[t, base : base + TILE, :]
            rows_ref[t, part] = x
            if t == 0:
                extra = own_ref[0, part] + from_left_ref[part]
                rows_ref[t, part, :MARGIN, :LANES] = x[:MARGIN, :LANES] + extra
            if t == tiles - 1:
                extra = own_ref[1, part] + from_right_ref[part]
                rows_ref[t, part, MARGIN:, LANES:] = x[MARGIN:, LANES:] + extra
    low = lax.broadcasted_iota(jnp.int32, (W, LANES), 1) < MARGIN
    width = TILE + 2 * MARGIN
    for a in range(per_tile):
        for t in range(tiles):
            atom = t * per_tile + a
            for part in range(2):
                x = rows_ref[t, part, a * W : (a + 1) * W, :]
                before = pltpu.roll(x, (width - a * W) % width, 1)[:, :LANES]
                after = pltpu.roll(x, (width - (a + 1) * W) % width, 1)[:, :LANES]
                out_ref[atom // group, part, atom % group] = jnp.where(low, before, after)


def band(acc, own, from_left, from_right, energies):
    tiles = acc.shape[0]
    atoms = tiles * TILE // W
    vmem = pl.BlockSpec(memory_space=pltpu.VMEM)
    return pl.pallas_call(
        band_kernel,
        out_shape=jax.ShapeDtypeStruct((energies, 2, atoms // energies, W, LANES), F32),
        in_specs=[vmem] * 4,
        out_specs=vmem,
        scratch_shapes=[pltpu.VMEM((tiles, 2, TILE, TILE + 2 * MARGIN), F32)],
        compiler_params=pltpu.CompilerParams(vmem_limit_bytes=16 << 20),
        name="band",
    )(acc, own, from_left, from_right)


def picks_kernel(where_ref, out_ref):
    rows = out_ref.shape[0]
    padded = where_ref.shape[1]
    entry = lax.broadcasted_iota(jnp.int32, (rows, padded), 0)
    first = where_ref[...] * W
    for j in range(W):
        hit = entry == first + j
        out_ref[:, j * padded : (j + 1) * padded] = jnp.where(hit, 1.0, 0.0).astype(BF16)


def picks(where, rows):
    padded = where.shape[1]
    vmem = pl.BlockSpec(memory_space=pltpu.VMEM)
    return pl.pallas_call(
        picks_kernel,
        out_shape=jax.ShapeDtypeStruct((rows, W * padded), BF16),
        in_specs=[vmem],
        out_specs=vmem,
        compiler_params=pltpu.CompilerParams(vmem_limit_bytes=16 << 20),
        name="picks",
    )(where)


def scatter_kernel(recv_ref, pick_ref, mix_ref, dham_ref, out_ref, smeared_ref, result_ref):
    energies, _, group, _, _ = recv_ref.shape
    padded = dham_ref.shape[1]
    pairs = out_ref.shape[1]
    columns = [
        recv_ref[:, :, a, :, :].reshape(energies * 2 * W, LANES) for a in range(group)
    ]
    received = halves(jnp.concatenate(columns, axis=1))
    mixed = halves(dot3(halves(mix_ref[...]), received, NN))
    smeared_ref[...] = dot(mixed[0], pick_ref[...], NN) + dot(mixed[1], pick_ref[...], NN)

    def block(part, j, k):
        row = (part * W + j) * energies
        return smeared_ref[row : row + energies, k * padded : (k + 1) * padded]

    def factor(c, i, j):
        row = (c * W + i) * W + j
        return dham_ref[row : row + 1, :]

    for part in range(2):
        for i in range(W):
            total = [None] * W
            for c in range(3):
                for k in range(W):
                    t = None
                    for j in range(W):
                        term = factor(c, i, j) * block(part, j, k)
                        t = term if t is None else t + term
                    for l in range(W):
                        term = t * factor(c, l, k)
                        total[l] = term if total[l] is None else total[l] + term
            for l in range(W):
                row = ((part * W + i) * W + l) * energies
                result_ref[row : row + energies, :] = total[l]
    for e in range(energies):
        one = result_ref[pl.ds(e, 2 * W * W, stride=energies), :]
        out_ref[e] = one.T[:pairs, :]


def scatter(recv, pick, mix, dham, pairs):
    energies, _, group, _, _ = recv.shape
    padded = dham.shape[1]
    vmem = pl.BlockSpec(memory_space=pltpu.VMEM)
    return pl.pallas_call(
        scatter_kernel,
        out_shape=jax.ShapeDtypeStruct((energies, pairs, 2 * W * W), F32),
        in_specs=[vmem] * 4,
        out_specs=vmem,
        scratch_shapes=[
            pltpu.VMEM((2 * W * energies, W * padded), F32),
            pltpu.VMEM((2 * W * W * energies, padded), F32),
        ],
        compiler_params=pltpu.CompilerParams(vmem_limit_bytes=24 << 20),
        name="scatter",
    )(recv, pick, mix, dham)


def build_kernel(phonon_shift, phonon_weight, energies):
    rows_e = jnp.arange(energies, dtype=jnp.int32)[None, :, None]
    cols_f = jnp.arange(energies, dtype=jnp.int32)[None, None, :]
    shifts = phonon_shift[:, None, None]
    emission = (cols_f == rows_e + shifts).astype(F32)
    absorption = (cols_f == rows_e - shifts).astype(F32)
    terms = (
        phonon_weight[0][:, None, None] * emission + phonon_weight[1][:, None, None] * absorption
    )
    return jnp.sum(terms, axis=0)


def build_mix(phonon_shift, phonon_weight, energies):
    kernel = build_kernel(phonon_shift, phonon_weight, energies)
    same = jnp.eye(2 * W, dtype=F32)
    mix = same[:, None, None, :] * kernel[None, :, :, None]
    return mix.reshape(2 * W * energies, energies * 2 * W)


def send(x, pairs):
    return lax.ppermute(x, "orb", pairs)


def per_device(green, sigma, neighbours, phonon_shift, phonon_weight, dham):
    energies = lax.axis_size("energy")
    peers = lax.axis_size("orb")
    e, z = lax.axis_index("energy"), lax.axis_index("orb")
    rows = green.shape[2]
    atoms = rows // W
    degree = neighbours.shape[1]
    group = atoms // energies
    pairs = group * degree
    padded = -(-pairs // LANES) * LANES
    held = sigma.shape[1]

    far = peers >= 4
    up = [(i, i + 1) for i in range(peers - 1)]
    down = [(i + 1, i) for i in range(peers - 1)]
    near_right = send(green[0, :, rows - HALF :], up[:-1] if far else up)
    near_left = send(green[0, :, :HALF], down[1:] if far else down)
    if far:
        more = jnp.where(
            z == 0, green[0, :, rows - MARGIN : rows - HALF], green[0, :, HALF:MARGIN]
        )
        other = send(more, [(0, 1), (peers - 1, peers - 2)])
        from_left, from_right = z == 1, z == peers - 2
        active = (z > 0) & (z < peers - 1)
    else:
        other = jnp.zeros_like(near_left)
        from_left = from_right = jnp.zeros((), bool)
        active = jnp.ones((), bool)
    limit = jnp.where(from_right, MARGIN, HALF)

    one = jnp.ones((), jnp.int32)
    acc, *keeps = lesser_part(green, [sigma], jnp.stack([z, one]), None)
    counts, listed = [1], [z, one]
    rightward = leftward = sigma
    for k in range(1, peers):
        rightward = send(rightward, up[k - 1 :])
        leftward = send(leftward, down[: peers - k])
        numbers = [jnp.maximum(z - k, 0), jnp.minimum(z + k, peers - 1)]
        valid = [(z >= k).astype(jnp.int32), (z + k < peers).astype(jnp.int32)]
        acc, *more_keeps = lesser_part(
            green, [rightward, leftward], jnp.stack(numbers + valid), acc
        )
        keeps += more_keeps
        counts.append(2)
        listed += [numbers[0], valid[0], numbers[1], valid[1]]
    listed += [x.astype(jnp.int32) for x in (active, from_left, from_right, limit)]
    to_left, to_right, own = edge_part(
        jnp.stack(listed), other, near_right, near_left, keeps, tuple(counts)
    )
    back_right = send(to_left, down)
    back_left = send(to_right, up)
    lesser = band(acc, own, back_left, back_right, energies)

    mine = lax.dynamic_slice_in_dim(neighbours, e * group, group, axis=0)
    first = z * atoms + e * group
    offset = mine - (first + jnp.arange(group, dtype=jnp.int32))[:, None]
    column = jnp.where(offset < 0, offset + REACH, offset + REACH - 1)
    where = column + 2 * REACH * jnp.arange(group, dtype=jnp.int32)[:, None]
    where = jnp.pad(where.reshape(1, pairs), ((0, 0), (0, padded - pairs)), constant_values=-1)
    pick = picks(where, group * LANES)
    mix = build_mix(phonon_shift, phonon_weight, energies)
    factors = lax.dynamic_slice_in_dim(
        dham.transpose(1, 2, 3, 0).reshape(3 * W * W, -1), e * pairs, pairs, axis=1
    )
    factors = jnp.pad(factors, ((0, 0), (0, padded - pairs)))

    recv = lax.all_to_all(lesser, "energy", split_axis=0, concat_axis=0, tiled=True)
    spread = scatter(recv, pick, mix, factors, pairs)
    result = lax.all_to_all(spread, "energy", split_axis=0, concat_axis=0, tiled=True)
    return result.reshape(1, atoms * degree, 2 * W * W)


def solution(mesh):
    return jax.shard_map(
        per_device,
        mesh=mesh,
        in_specs=(
            P("energy", None, "orb", None),
            P("energy", "orb", None, None, None),
            P("orb", None),
            P(),
            P(),
            P("orb", None, None, None),
        ),
        out_specs=P("energy", "orb", None),
        check_vma=False,
    )
```

```python
import functools

import jax
import jax.numpy as jnp
from jax import lax
from jax.experimental import pallas as pl
from jax.experimental.pallas import tpu as pltpu
from jax.sharding import PartitionSpec as P

W = 8
BS = 128
REACH = 8
MARGIN = REACH * W
HALF = MARGIN // 2
TILE = 128
LANES = 128
F32, BF16 = jnp.float32, jnp.bfloat16

NT = (((1,), (1,)), ((), ()))
NN = (((1,), (0,)), ((), ()))


def halves(x):
    hi = x.astype(BF16)
    return hi, (x - hi.astype(F32)).astype(BF16)


def dot(a, b, dims):
    return lax.dot_general(a, b, dims, preferred_element_type=F32)


def dot3(a, b, dims):
    left = jnp.concatenate([a[0], a[0], a[1]], axis=1)
    right = jnp.concatenate([b[0], b[1], b[0]], axis=dims[0][1][0])
    return dot(left, right, dims)


def blocks_at_once(held):
    return 2 if held % 2 == 0 else 1


def some_blocks(fields, weights, hi_ref, lo_ref, acc_ref, edges):
    rows = fields[0][0].shape[0]
    wide = 2 * BS
    hi, lo = halves(jnp.concatenate([x for pair in fields for x in pair], axis=1))
    hi_ref[MARGIN : MARGIN + rows, :] = hi
    lo_ref[MARGIN : MARGIN + rows, :] = lo
    split = []
    for real, imag in weights:
        top = jnp.concatenate([real, imag], axis=1)
        split.append(halves(jnp.concatenate([top, jnp.concatenate([-imag, real], axis=1)], axis=0)))
    tiles = rows // TILE
    for t in range(tiles):
        row, window = MARGIN + t * TILE, t * TILE
        both = []
        for n, weight in enumerate(split):
            cols = slice(n * wide, (n + 1) * wide)
            left = (hi_ref[row : row + TILE, cols], lo_ref[row : row + TILE, cols])
            product = dot3(left, weight, NN)
            both.append(
                [
                    jnp.concatenate(
                        [x, jnp.concatenate([x[:, BS:], -x[:, :BS]], axis=1)], axis=0
                    )
                    for x in halves(product)
                ]
            )
            if edges is not None:
                for ref, part in zip(edges, both[-1]):
                    if t == 0:
                        ref[n, :MARGIN, :] = part[:MARGIN]
                    if t == tiles - 1:
                        ref[n, 3 * MARGIN :, :] = part[TILE - MARGIN : TILE]
        both = [jnp.concatenate(parts, axis=1) for parts in zip(*both)]
        upto = window + TILE + 2 * MARGIN
        acc_ref[t] = acc_ref[t] + dot3(both, (hi_ref[window:upto, :], lo_ref[window:upto, :]), NT)
    if edges is not None:
        for n, weight in enumerate(split):
            cols = slice(n * wide, (n + 1) * wide)
            outer = [
                jnp.concatenate(
                    [ref[MARGIN : 2 * MARGIN, cols], ref[rows : rows + MARGIN, cols]], axis=0
                )
                for ref in (hi_ref, lo_ref)
            ]
            for ref, part in zip(edges, halves(dot3(outer, weight, NT))):
                ref[n, MARGIN : 3 * MARGIN, :] = part


def lesser_kernel(shards, first, idx_ref, green_ref, *rest):
    sigmas, rest = rest[:shards], rest[shards:]
    if first:
        acc_ref, keep_hi_ref, keep_lo_ref, *sent, buf, hi_ref, lo_ref, sem, self_ref, self_sem = rest
    else:
        before_ref, acc_ref, keep_hi_ref, keep_lo_ref, buf, hi_ref, lo_ref, sem = rest
    rows, held = green_ref.shape[2], sigmas[0].shape[1]
    once = blocks_at_once(held)

    def fetch(shard, s):
        col = pl.multiple_of((idx_ref[shard] + s) * BS, BS)
        at = shard * held + s
        return pltpu.make_async_copy(
            green_ref.at[0, :, :, pl.ds(col, BS)], buf.at[at], sem.at[at]
        )

    def valid(shard):
        return idx_ref[shards + shard] == 1

    if first:
        load = pltpu.make_async_copy(sigmas[0], self_ref, self_sem.at[0])
        load.start()
        sigmas = [self_ref]
    for shard in range(shards):

        @pl.when(valid(shard))
        def _():
            for s in range(held):
                fetch(shard, s).start()

    if first:
        starts = [pl.multiple_of(idx_ref[2], HALF), rows - HALF, 0]
        copies = [
            pltpu.make_async_copy(
                green_ref.at[0, :, pl.ds(row, HALF), :], out, self_sem.at[n + 1]
            )
            for n, (row, out) in enumerate(zip(starts, sent))
        ]
        for copy in copies:
            copy.start()
    acc_ref[...] = jnp.zeros_like(acc_ref) if first else before_ref[...]
    for ref in (hi_ref, lo_ref):
        ref[:MARGIN, :] = jnp.zeros((MARGIN, ref.shape[1]), BF16)
        ref[MARGIN + rows :, :] = jnp.zeros((MARGIN, ref.shape[1]), BF16)
    if first:
        load.wait()

    for shard in range(shards):

        @pl.when(valid(shard))
        def _():
            def step(g, carry):
                fields, weights = [], []
                for n in range(once):
                    s = g * once + n
                    fetch(shard, s).wait()
                    at = shard * held + s
                    fields.append((buf[at, 0], buf[at, 1]))
                    weights.append((sigmas[shard][0, s, 0], sigmas[shard][0, s, 1]))
                slots = pl.ds(shard * held + g * once, once)
                some_blocks(
                    fields, weights, hi_ref, lo_ref, acc_ref,
                    (keep_hi_ref.at[slots], keep_lo_ref.at[slots]),
                )
                return carry

            lax.fori_loop(0, held // once, step, 0)

    if first:
        for copy in copies:
            copy.wait()


def lesser_part(green, sigmas, index, before):
    rows, held, shards = green.shape[2], sigmas[0].shape[1], len(sigmas)
    tiles, count = rows // TILE, held * shards
    once = blocks_at_once(held)
    first = before is None
    vmem = pl.BlockSpec(memory_space=pltpu.VMEM)
    hbm = pl.BlockSpec(memory_space=pl.ANY)
    keep = jax.ShapeDtypeStruct((count, 4 * MARGIN, 2 * BS), BF16)
    sent = jax.ShapeDtypeStruct((2, HALF, green.shape[3]), F32)
    more = [sent] * 3 if first else []
    extra = [pltpu.VMEM(sigmas[0].shape, F32), pltpu.SemaphoreType.DMA((4,))] if first else []
    return pl.pallas_call(
        functools.partial(lesser_kernel, shards, first),
        out_shape=[
            jax.ShapeDtypeStruct((tiles, 2 * TILE, TILE + 2 * MARGIN), F32),
            keep,
            keep,
        ]
        + more,
        in_specs=[pl.BlockSpec(memory_space=pltpu.SMEM), hbm]
        + ([hbm] * shards if first else [vmem] * (shards + 1)),
        out_specs=[vmem] * 3 + [hbm] * len(more),
        scratch_shapes=[
            pltpu.VMEM((count, 2, rows, BS), F32),
            pltpu.VMEM((rows + 2 * MARGIN, once * 2 * BS), BF16),
            pltpu.VMEM((rows + 2 * MARGIN, once * 2 * BS), BF16),
            pltpu.SemaphoreType.DMA((count,)),
        ]
        + extra,
        input_output_aliases={} if first else {2 + shards: 0},
        compiler_params=pltpu.CompilerParams(vmem_limit_bytes=24 << 20),
        cost_estimate=pl.CostEstimate(
            flops=held * 6 * rows * 2 * BS * (2 * BS + 4 * TILE),
            bytes_accessed=held * rows * BS * 8 + 8 * tiles * TILE * 512,
            transcendentals=0,
        ),
        name="lesser_own" if first else "lesser_more",
    )(index, green, *sigmas, *([] if first else [before]))


def edge_kernel(counts, idx_ref, a_ref, b_ref, c_ref, *rest):
    parts = len(counts)
    keeps, rest = rest[: 2 * parts], rest[2 * parts :]
    left_ref, right_ref, own_ref, acc_ref = rest
    base = 2 * sum(counts)
    active, from_left, from_right = [idx_ref[base + k] == 1 for k in range(3)]
    limit = idx_ref[base + 3]
    acc_ref[...] = jnp.zeros_like(acc_ref)

    def add(col, hi, lo, at, held):
        cols = pl.ds(pl.multiple_of(col * BS, BS), held * BS)
        wide = [
            [ref[part, :, cols] for part in range(2)] for ref in (a_ref, b_ref, c_ref)
        ]
        for side in range(2):
            fields = []
            for part in range(2):
                more = wide[0][part]
                if side == 0:
                    rows = [jnp.where(from_left, more, 0.0), wide[1][part]]
                else:
                    rows = [wide[2][part], jnp.where(from_right, more, 0.0)]
                fields.append(halves(jnp.concatenate(rows, axis=0)))
            halo = []
            for real, imag in zip(*fields):
                lanes = []
                for s in range(held):
                    one = slice(s * BS, (s + 1) * BS)
                    lanes += [
                        jnp.concatenate([real[:, one], -imag[:, one]], axis=0),
                        jnp.concatenate([imag[:, one], real[:, one]], axis=0),
                    ]
                halo.append(jnp.concatenate(lanes, axis=1))
            rows = slice(side * TILE, (side + 1) * TILE)
            kept = [
                jnp.concatenate([ref[at + s, rows, :] for s in range(held)], axis=1)
                for ref in (hi, lo)
            ]
            acc_ref[side] = acc_ref[side] + dot3(halo, kept, NT)

    @pl.when(active)
    def _():
        shard = 0
        for part, count in enumerate(counts):
            hi, lo = keeps[2 * part], keeps[2 * part + 1]
            held = hi.shape[0] // count
            for k in range(count):
                col, valid = idx_ref[2 * shard], idx_ref[2 * shard + 1]
                shard += 1

                @pl.when(valid == 1)
                def _():
                    add(col, hi, lo, k * held, held)

    lane = lax.broadcasted_iota(jnp.int32, (MARGIN, LANES), 1)
    row = lax.broadcasted_iota(jnp.int32, (MARGIN, LANES), 0)
    low = lane < MARGIN
    left, right = acc_ref[0], acc_ref[1]
    turned_left, turned_right = left.T[:MARGIN], right.T[MARGIN:]
    left_ref[0] = jnp.where(low, 0.0, left[:MARGIN])
    left_ref[1] = jnp.where(low, 0.0, -left[MARGIN:])
    right_ref[0] = jnp.where(lane < limit, right[:MARGIN], 0.0)
    right_ref[1] = jnp.where(lane < limit, -right[MARGIN:], 0.0)
    own_ref[0, 0] = jnp.where(low, turned_left, 0.0)
    own_ref[0, 1] = jnp.where(low, pltpu.roll(turned_left, MARGIN, 1), 0.0)
    mine = jnp.logical_and(row < limit, lane >= MARGIN)
    own_ref[1, 0] = jnp.where(mine, pltpu.roll(turned_right, MARGIN, 1), 0.0)
    own_ref[1, 1] = jnp.where(mine, turned_right, 0.0)


def edge_part(flags, a, b, c, keeps, counts):
    vmem = pl.BlockSpec(memory_space=pltpu.VMEM)
    side = jax.ShapeDtypeStruct((2, MARGIN, LANES), F32)
    return pl.pallas_call(
        functools.partial(edge_kernel, counts),
        out_shape=(side, side, jax.ShapeDtypeStruct((2, 2, MARGIN, LANES), F32)),
        in_specs=[pl.BlockSpec(memory_space=pltpu.SMEM)] + [vmem] * (3 + len(keeps)),
        out_specs=(vmem, vmem, vmem),
        scratch_shapes=[pltpu.VMEM((2, TILE, TILE), F32)],
        compiler_params=pltpu.CompilerParams(vmem_limit_bytes=24 << 20),
        cost_estimate=pl.CostEstimate(
            flops=a.shape[2] * 2 * 12 * TILE * 2 * TILE,
            bytes_accessed=a.shape[2] * 2 * 4 * TILE * 4,
            transcendentals=0,
        ),
        name="edges",
    )(flags, a, b, c, *keeps)


def band_kernel(acc_ref, own_ref, from_left_ref, from_right_ref, out_ref, rows_ref):
    tiles = acc_ref.shape[0]
    group = out_ref.shape[2]
    per_tile = TILE // W
    for t in range(tiles):
        for part in range(2):
            base = part * TILE
            x = acc_ref[t, base : base + TILE, :]
            rows_ref[t, part] = x
            if t == 0:
                extra = own_ref[0, part] + from_left_ref[part]
                rows_ref[t, part, :MARGIN, :LANES] = x[:MARGIN, :LANES] + extra
            if t == tiles - 1:
                extra = own_ref[1, part] + from_right_ref[part]
                rows_ref[t, part, MARGIN:, LANES:] = x[MARGIN:, LANES:] + extra
    low = lax.broadcasted_iota(jnp.int32, (W, LANES), 1) < MARGIN
    width = TILE + 2 * MARGIN
    for a in range(per_tile):
        for t in range(tiles):
            atom = t * per_tile + a
            for part in range(2):
                x = rows_ref[t, part, a * W : (a + 1) * W, :]
                before = pltpu.roll(x, (width - a * W) % width, 1)[:, :LANES]
                after = pltpu.roll(x, (width - (a + 1) * W) % width, 1)[:, :LANES]
                out_ref[atom // group, part, atom % group] = jnp.where(low, before, after)


def band(acc, own, from_left, from_right, energies):
    tiles = acc.shape[0]
    atoms = tiles * TILE // W
    vmem = pl.BlockSpec(memory_space=pltpu.VMEM)
    return pl.pallas_call(
        band_kernel,
        out_shape=jax.ShapeDtypeStruct((energies, 2, atoms // energies, W, LANES), F32),
        in_specs=[vmem] * 4,
        out_specs=vmem,
        scratch_shapes=[pltpu.VMEM((tiles, 2, TILE, TILE + 2 * MARGIN), F32)],
        compiler_params=pltpu.CompilerParams(vmem_limit_bytes=16 << 20),
        name="band",
    )(acc, own, from_left, from_right)


def picks_kernel(where_ref, out_ref):
    rows = out_ref.shape[0]
    padded = where_ref.shape[1]
    entry = lax.broadcasted_iota(jnp.int32, (rows, padded), 0)
    first = where_ref[...] * W
    for j in range(W):
        hit = entry == first + j
        out_ref[:, j * padded : (j + 1) * padded] = jnp.where(hit, 1.0, 0.0).astype(BF16)


def picks(where, rows):
    padded = where.shape[1]
    vmem = pl.BlockSpec(memory_space=pltpu.VMEM)
    return pl.pallas_call(
        picks_kernel,
        out_shape=jax.ShapeDtypeStruct((rows, W * padded), BF16),
        in_specs=[vmem],
        out_specs=vmem,
        compiler_params=pltpu.CompilerParams(vmem_limit_bytes=16 << 20),
        name="picks",
    )(where)


def scatter_kernel(recv_ref, pick_ref, mix_ref, dham_ref, out_ref, smeared_ref, result_ref):
    energies, _, group, _, _ = recv_ref.shape
    padded = dham_ref.shape[1]
    pairs = out_ref.shape[1]
    columns = [
        recv_ref[:, :, a, :, :].reshape(energies * 2 * W, LANES) for a in range(group)
    ]
    received = halves(jnp.concatenate(columns, axis=1))
    mixed = halves(dot3(halves(mix_ref[...]), received, NN))
    smeared_ref[...] = dot(mixed[0], pick_ref[...], NN) + dot(mixed[1], pick_ref[...], NN)

    def block(part, j, k):
        row = (part * W + j) * energies
        return smeared_ref[row : row + energies, k * padded : (k + 1) * padded]

    def factor(c, i, j):
        row = (c * W + i) * W + j
        return dham_ref[row : row + 1, :]

    for part in range(2):
        for i in range(W):
            total = [None] * W
            for c in range(3):
                for k in range(W):
                    t = None
                    for j in range(W):
                        term = factor(c, i, j) * block(part, j, k)
                        t = term if t is None else t + term
                    for l in range(W):
                        term = t * factor(c, l, k)
                        total[l] = term if total[l] is None else total[l] + term
            for l in range(W):
                row = ((part * W + i) * W + l) * energies
                result_ref[row : row + energies, :] = total[l]
    for e in range(energies):
        one = result_ref[pl.ds(e, 2 * W * W, stride=energies), :]
        out_ref[e] = one.T[:pairs, :]


def scatter(recv, pick, mix, dham, pairs):
    energies, _, group, _, _ = recv.shape
    padded = dham.shape[1]
    vmem = pl.BlockSpec(memory_space=pltpu.VMEM)
    return pl.pallas_call(
        scatter_kernel,
        out_shape=jax.ShapeDtypeStruct((energies, pairs, 2 * W * W), F32),
        in_specs=[vmem] * 4,
        out_specs=vmem,
        scratch_shapes=[
            pltpu.VMEM((2 * W * energies, W * padded), F32),
            pltpu.VMEM((2 * W * W * energies, padded), F32),
        ],
        compiler_params=pltpu.CompilerParams(vmem_limit_bytes=24 << 20),
        name="scatter",
    )(recv, pick, mix, dham)


def build_kernel(phonon_shift, phonon_weight, energies):
    rows_e = jnp.arange(energies, dtype=jnp.int32)[None, :, None]
    cols_f = jnp.arange(energies, dtype=jnp.int32)[None, None, :]
    shifts = phonon_shift[:, None, None]
    emission = (cols_f == rows_e + shifts).astype(F32)
    absorption = (cols_f == rows_e - shifts).astype(F32)
    terms = (
        phonon_weight[0][:, None, None] * emission + phonon_weight[1][:, None, None] * absorption
    )
    return jnp.sum(terms, axis=0)


def build_mix(phonon_shift, phonon_weight, energies):
    kernel = build_kernel(phonon_shift, phonon_weight, energies)
    same = jnp.eye(2 * W, dtype=F32)
    mix = same[:, None, None, :] * kernel[None, :, :, None]
    return mix.reshape(2 * W * energies, energies * 2 * W)


def send(x, pairs):
    return lax.ppermute(x, "orb", pairs)


def per_device(green, sigma, neighbours, phonon_shift, phonon_weight, dham):
    energies = lax.axis_size("energy")
    peers = lax.axis_size("orb")
    e, z = lax.axis_index("energy"), lax.axis_index("orb")
    rows = green.shape[2]
    atoms = rows // W
    degree = neighbours.shape[1]
    group = atoms // energies
    pairs = group * degree
    padded = -(-pairs // LANES) * LANES
    held = sigma.shape[1]

    far = peers >= 4
    up = [(i, i + 1) for i in range(peers - 1)]
    down = [(i + 1, i) for i in range(peers - 1)]
    one = jnp.ones((), jnp.int32)
    sooner = jnp.where(z == 0, rows - MARGIN, HALF)
    green = pltpu.with_memory_space_constraint(green, pltpu.HBM)
    acc, *keeps, more, last, leading = lesser_part(
        green,
        [pltpu.with_memory_space_constraint(sigma, pltpu.HBM)],
        jnp.stack([z * held, one, sooner]),
        None,
    )
    near_right = send(last, up[:-1] if far else up)
    near_left = send(leading, down[1:] if far else down)
    if far:
        other = send(more, [(0, 1), (peers - 1, peers - 2)])
        from_left, from_right = z == 1, z == peers - 2
        active = (z > 0) & (z < peers - 1)
    else:
        other = jnp.zeros_like(near_left)
        from_left = from_right = jnp.zeros((), bool)
        active = jnp.ones((), bool)
    limit = jnp.where(from_right, MARGIN, HALF)

    counts, listed = [1], [z * held, one]
    cuts = 2 if held % 2 == 0 else 1
    piece = held // cuts
    rightward = [sigma[:, h * piece : (h + 1) * piece] for h in range(cuts)]
    leftward = list(rightward)
    for k in range(1, peers):
        numbers = [jnp.maximum(z - k, 0) * held, jnp.minimum(z + k, peers - 1) * held]
        valid = [(z >= k).astype(jnp.int32), (z + k < peers).astype(jnp.int32)]
        for h in range(cuts):
            rightward[h] = send(rightward[h], up[k - 1 :])
            leftward[h] = send(leftward[h], down[: peers - k])
            firsts = [x + h * piece for x in numbers]
            acc, *more_keeps = lesser_part(
                green, [rightward[h], leftward[h]], jnp.stack(firsts + valid), acc
            )
            keeps += more_keeps
            counts.append(2)
            listed += [firsts[0], valid[0], firsts[1], valid[1]]
    listed += [x.astype(jnp.int32) for x in (active, from_left, from_right, limit)]
    to_left, to_right, own = edge_part(
        jnp.stack(listed), other, near_right, near_left, keeps, tuple(counts)
    )
    back_right = send(to_left, down)
    back_left = send(to_right, up)
    lesser = band(acc, own, back_left, back_right, energies)

    mine = lax.dynamic_slice_in_dim(neighbours, e * group, group, axis=0)
    first = z * atoms + e * group
    offset = mine - (first + jnp.arange(group, dtype=jnp.int32))[:, None]
    column = jnp.where(offset < 0, offset + REACH, offset + REACH - 1)
    where = column + 2 * REACH * jnp.arange(group, dtype=jnp.int32)[:, None]
    where = jnp.pad(where.reshape(1, pairs), ((0, 0), (0, padded - pairs)), constant_values=-1)
    pick = picks(where, group * LANES)
    mix = build_mix(phonon_shift, phonon_weight, energies)
    factors = lax.dynamic_slice_in_dim(
        dham.transpose(1, 2, 3, 0).reshape(3 * W * W, -1), e * pairs, pairs, axis=1
    )
    factors = jnp.pad(factors, ((0, 0), (0, padded - pairs)))

    recv = lax.all_to_all(lesser, "energy", split_axis=0, concat_axis=0, tiled=True)
    spread = scatter(recv, pick, mix, factors, pairs)
    result = lax.all_to_all(spread, "energy", split_axis=0, concat_axis=0, tiled=True)
    return result.reshape(1, atoms * degree, 2 * W * W)


def solution(mesh):
    return jax.shard_map(
        per_device,
        mesh=mesh,
        in_specs=(
            P("energy", None, "orb", None),
            P("energy", "orb", None, None, None),
            P("orb", None),
            P(),
            P(),
            P("orb", None, None, None),
        ),
        out_specs=P("energy", "orb", None),
        check_vma=False,
    )
```

```python
import functools

import jax
import jax.numpy as jnp
from jax import lax
from jax.experimental import pallas as pl
from jax.experimental.pallas import tpu as pltpu
from jax.sharding import PartitionSpec as P

W = 8
BS = 128
REACH = 8
MARGIN = REACH * W
HALF = MARGIN // 2
TILE = 128
LANES = 128
F32, BF16 = jnp.float32, jnp.bfloat16

NT = (((1,), (1,)), ((), ()))
NN = (((1,), (0,)), ((), ()))


def halves(x):
    hi = x.astype(BF16)
    return hi, (x - hi.astype(F32)).astype(BF16)


def dot(a, b, dims):
    return lax.dot_general(a, b, dims, preferred_element_type=F32)


def dot3(a, b, dims):
    left = jnp.concatenate([a[0], a[0], a[1]], axis=1)
    right = jnp.concatenate([b[0], b[1], b[0]], axis=dims[0][1][0])
    return dot(left, right, dims)


def blocks_at_once(held):
    return 2 if held % 2 == 0 else 1


def some_blocks(lane, weights, hi_ref, lo_ref, acc_ref, edges, active):
    rows = hi_ref.shape[0] - 2 * MARGIN
    wide = 2 * BS
    split, products = [], []
    for n, (real, imag) in enumerate(weights):
        top = jnp.concatenate([real, imag], axis=1)
        weight = halves(jnp.concatenate([top, jnp.concatenate([-imag, real], axis=1)], axis=0))
        cols = pl.ds(lane + n * wide, wide)
        own = [ref[MARGIN : MARGIN + rows, cols] for ref in (hi_ref, lo_ref)]
        product = halves(dot3(own, weight, NN))
        for ref, part in zip(edges, product):
            ref[n, :MARGIN, :] = part[:MARGIN]
            ref[n, 3 * MARGIN :, :] = part[rows - MARGIN :]
        split.append(weight)
        products.append(product)
    cols = pl.ds(lane, len(weights) * wide)
    for t in range(rows // TILE):
        both = []
        for part in zip(*products):
            lanes = []
            for x in part:
                x = x[t * TILE : (t + 1) * TILE]
                turned = jnp.concatenate([x[:, BS:], -x[:, :BS]], axis=1)
                lanes.append(jnp.concatenate([x, turned], axis=0))
            both.append(jnp.concatenate(lanes, axis=1))
        near = pl.ds(t * TILE, TILE + 2 * MARGIN)
        acc_ref[t] = acc_ref[t] + dot3(both, (hi_ref[near, cols], lo_ref[near, cols]), NT)

    @pl.when(active)
    def _():
        for n, weight in enumerate(split):
            one = pl.ds(lane + n * wide, wide)
            outer = [
                jnp.concatenate(
                    [ref[MARGIN : 2 * MARGIN, one], ref[rows : rows + MARGIN, one]], axis=0
                )
                for ref in (hi_ref, lo_ref)
            ]
            for ref, part in zip(edges, halves(dot3(outer, weight, NT))):
                ref[n, MARGIN : 3 * MARGIN, :] = part


def shard_loop(first_block, self_ref, hi_ref, lo_ref, acc_ref, keeps, slot, active):
    held = self_ref.shape[1]
    once = blocks_at_once(held)

    def step(g, carry):
        lane = pl.multiple_of((first_block + g * once) * 2 * BS, 2 * BS)
        weights = [
            (self_ref[0, g * once + n, 0], self_ref[0, g * once + n, 1]) for n in range(once)
        ]
        slots = pl.ds(slot + g * once, once)
        kept = tuple(ref.at[slots] for ref in keeps)
        some_blocks(lane, weights, hi_ref, lo_ref, acc_ref, kept, active)
        return carry

    lax.fori_loop(0, held // once, step, 0)


def own_kernel(
    idx_ref, green_ref, sigma_ref, acc_ref, keep_hi_ref, keep_lo_ref, hi_ref, lo_ref,
    buf, self_ref, sem,
):
    rows, held = green_ref.shape[2], sigma_ref.shape[1]
    blocks = green_ref.shape[3] // BS
    begin, active = idx_ref[0], idx_ref[1] == 1

    def block_of(s):
        return lax.rem(begin + s, blocks)

    def fetch(s):
        col = pl.multiple_of(block_of(s) * BS, BS)
        return pltpu.make_async_copy(
            green_ref.at[0, :, :, pl.ds(col, BS)], buf.at[s], sem.at[s]
        )

    def store(s, carry):
        fetch(s).wait()
        lanes = pl.ds(pl.multiple_of(block_of(s) * 2 * BS, 2 * BS), 2 * BS)
        parts = halves(jnp.concatenate([buf[s, 0], buf[s, 1]], axis=1))
        for ref, part in zip((hi_ref, lo_ref), parts):
            ref[MARGIN : MARGIN + rows, lanes] = part
        return carry

    load = pltpu.make_async_copy(sigma_ref, self_ref, sem.at[blocks])
    load.start()
    for s in range(blocks):
        fetch(s).start()
    acc_ref[...] = jnp.zeros_like(acc_ref)
    for ref in (hi_ref, lo_ref):
        ref[:MARGIN, :] = jnp.zeros((MARGIN, ref.shape[1]), BF16)
        ref[MARGIN + rows :, :] = jnp.zeros((MARGIN, ref.shape[1]), BF16)
    lax.fori_loop(0, held, store, 0)
    load.wait()
    shard_loop(begin, self_ref, hi_ref, lo_ref, acc_ref, (keep_hi_ref, keep_lo_ref), 0, active)
    lax.fori_loop(held, blocks, store, 0)


def own_part(green, sigma, index):
    rows, held = green.shape[2], sigma.shape[1]
    tiles, blocks = rows // TILE, green.shape[3] // BS
    vmem = pl.BlockSpec(memory_space=pltpu.VMEM)
    hbm = pl.BlockSpec(memory_space=pl.ANY)
    keep = jax.ShapeDtypeStruct((held, 4 * MARGIN, 2 * BS), BF16)
    whole = jax.ShapeDtypeStruct((rows + 2 * MARGIN, blocks * 2 * BS), BF16)
    return pl.pallas_call(
        own_kernel,
        out_shape=(
            jax.ShapeDtypeStruct((tiles, 2 * TILE, TILE + 2 * MARGIN), F32),
            keep,
            keep,
            whole,
            whole,
        ),
        in_specs=[pl.BlockSpec(memory_space=pltpu.SMEM), hbm, hbm],
        out_specs=(vmem,) * 5,
        scratch_shapes=[
            pltpu.VMEM((blocks, 2, rows, BS), F32),
            pltpu.VMEM(sigma.shape, F32),
            pltpu.SemaphoreType.DMA((blocks + 1,)),
        ],
        compiler_params=pltpu.CompilerParams(vmem_limit_bytes=40 << 20),
        cost_estimate=pl.CostEstimate(
            flops=held * 6 * rows * 2 * BS * (2 * BS + 4 * TILE),
            bytes_accessed=blocks * rows * BS * 8,
            transcendentals=0,
        ),
        name="lesser_own",
    )(index, green, sigma)


def lesser_kernel(
    idx_ref, hi_ref, lo_ref, right_ref, left_ref, before_ref, *rest
):
    acc_ref, keep_hi_ref, keep_lo_ref = rest[-3:]
    held = right_ref.shape[1]
    acc_ref[...] = before_ref[...]
    for k, self_ref in enumerate((right_ref, left_ref)):

        @pl.when(idx_ref[2 + k] == 1)
        def _():
            shard_loop(
                idx_ref[k], self_ref, hi_ref, lo_ref, acc_ref,
                (keep_hi_ref, keep_lo_ref), k * held, idx_ref[4] == 1,
            )


def lesser_part(hi, lo, right, left, index, before, after):
    held = right.shape[1]
    vmem = pl.BlockSpec(memory_space=pltpu.VMEM)
    keep = jax.ShapeDtypeStruct((2 * held, 4 * MARGIN, 2 * BS), BF16)
    return pl.pallas_call(
        lesser_kernel,
        out_shape=(jax.ShapeDtypeStruct(before.shape, F32), keep, keep),
        in_specs=[pl.BlockSpec(memory_space=pltpu.SMEM)]
        + [vmem] * 5
        + [pl.BlockSpec(memory_space=pl.ANY)] * len(after),
        out_specs=(vmem,) * 3,
        input_output_aliases={5: 0},
        compiler_params=pltpu.CompilerParams(vmem_limit_bytes=32 << 20),
        cost_estimate=pl.CostEstimate(
            flops=held * 6 * hi.shape[0] * 2 * BS * (2 * BS + 4 * TILE),
            bytes_accessed=8 * before.size,
            transcendentals=0,
        ),
        name="lesser_more",
    )(index, hi, lo, right, left, before, *after)


def rows_kernel(count, idx_ref, green_ref, *rest):
    outs, sem = rest[-1 - count : -1], rest[-1]
    copies = [
        pltpu.make_async_copy(
            green_ref.at[0, :, pl.ds(pl.multiple_of(idx_ref[n], HALF), HALF), :],
            out,
            sem.at[n],
        )
        for n, out in enumerate(outs)
    ]
    for copy in copies:
        copy.start()
    for copy in copies:
        copy.wait()


def rows_at(green, starts, after):
    count = len(starts)
    hbm = pl.BlockSpec(memory_space=pl.ANY)
    out = jax.ShapeDtypeStruct((2, HALF, green.shape[3]), F32)
    return pl.pallas_call(
        functools.partial(rows_kernel, count),
        out_shape=[out] * count,
        in_specs=[pl.BlockSpec(memory_space=pltpu.SMEM)] + [hbm] * (1 + len(after)),
        out_specs=[pl.BlockSpec(memory_space=pltpu.VMEM)] * count,
        scratch_shapes=[pltpu.SemaphoreType.DMA((count,))],
        compiler_params=pltpu.CompilerParams(vmem_limit_bytes=8 << 20),
        cost_estimate=pl.CostEstimate(
            flops=0, bytes_accessed=4 * count * out.size, transcendentals=0
        ),
        name="rows",
    )(jnp.stack([jnp.asarray(x, jnp.int32) for x in starts]), green, *after)


def gate_kernel(right_ref, left_ref, after_ref, *outs):
    del right_ref, left_ref, after_ref, outs


def gate(right, left, after):
    hbm = pl.BlockSpec(memory_space=pl.ANY)
    return pl.pallas_call(
        gate_kernel,
        out_shape=[jax.ShapeDtypeStruct(x.shape, x.dtype) for x in (right, left)],
        in_specs=[hbm] * 3,
        out_specs=[hbm] * 2,
        input_output_aliases={0: 0, 1: 1},
        cost_estimate=pl.CostEstimate(flops=0, bytes_accessed=0, transcendentals=0),
        name="gate",
    )(right, left, after)


def edge_kernel(counts, idx_ref, a_ref, b_ref, c_ref, *rest):
    parts = len(counts)
    keeps, rest = rest[: 2 * parts], rest[2 * parts :]
    left_ref, right_ref, own_ref, acc_ref = rest
    base = 2 * sum(counts)
    active, from_left, from_right = [idx_ref[base + k] == 1 for k in range(3)]
    limit = idx_ref[base + 3]
    acc_ref[...] = jnp.zeros_like(acc_ref)

    def add(col, hi, lo, at, held):
        cols = pl.ds(pl.multiple_of(col * BS, BS), held * BS)
        wide = [
            [ref[part, :, cols] for part in range(2)] for ref in (a_ref, b_ref, c_ref)
        ]
        for side in range(2):
            fields = []
            for part in range(2):
                more = wide[0][part]
                if side == 0:
                    rows = [jnp.where(from_left, more, 0.0), wide[1][part]]
                else:
                    rows = [wide[2][part], jnp.where(from_right, more, 0.0)]
                fields.append(halves(jnp.concatenate(rows, axis=0)))
            halo = []
            for real, imag in zip(*fields):
                lanes = []
                for s in range(held):
                    one = slice(s * BS, (s + 1) * BS)
                    lanes += [
                        jnp.concatenate([real[:, one], -imag[:, one]], axis=0),
                        jnp.concatenate([imag[:, one], real[:, one]], axis=0),
                    ]
                halo.append(jnp.concatenate(lanes, axis=1))
            rows = slice(side * TILE, (side + 1) * TILE)
            kept = [
                jnp.concatenate([ref[at + s, rows, :] for s in range(held)], axis=1)
                for ref in (hi, lo)
            ]
            acc_ref[side] = acc_ref[side] + dot3(halo, kept, NT)

    @pl.when(active)
    def _():
        shard = 0
        for part, count in enumerate(counts):
            hi, lo = keeps[2 * part], keeps[2 * part + 1]
            held = hi.shape[0] // count
            for k in range(count):
                col, valid = idx_ref[2 * shard], idx_ref[2 * shard + 1]
                shard += 1

                @pl.when(valid == 1)
                def _():
                    add(col, hi, lo, k * held, held)

    lane = lax.broadcasted_iota(jnp.int32, (MARGIN, LANES), 1)
    row = lax.broadcasted_iota(jnp.int32, (MARGIN, LANES), 0)
    low = lane < MARGIN
    left, right = acc_ref[0], acc_ref[1]
    turned_left, turned_right = left.T[:MARGIN], right.T[MARGIN:]
    left_ref[0] = jnp.where(low, 0.0, left[:MARGIN])
    left_ref[1] = jnp.where(low, 0.0, -left[MARGIN:])
    right_ref[0] = jnp.where(lane < limit, right[:MARGIN], 0.0)
    right_ref[1] = jnp.where(lane < limit, -right[MARGIN:], 0.0)
    own_ref[0, 0] = jnp.where(low, turned_left, 0.0)
    own_ref[0, 1] = jnp.where(low, pltpu.roll(turned_left, MARGIN, 1), 0.0)
    mine = jnp.logical_and(row < limit, lane >= MARGIN)
    own_ref[1, 0] = jnp.where(mine, pltpu.roll(turned_right, MARGIN, 1), 0.0)
    own_ref[1, 1] = jnp.where(mine, turned_right, 0.0)


def edge_part(flags, a, b, c, keeps, counts):
    vmem = pl.BlockSpec(memory_space=pltpu.VMEM)
    side = jax.ShapeDtypeStruct((2, MARGIN, LANES), F32)
    return pl.pallas_call(
        functools.partial(edge_kernel, counts),
        out_shape=(side, side, jax.ShapeDtypeStruct((2, 2, MARGIN, LANES), F32)),
        in_specs=[pl.BlockSpec(memory_space=pltpu.SMEM)] + [vmem] * (3 + len(keeps)),
        out_specs=(vmem, vmem, vmem),
        scratch_shapes=[pltpu.VMEM((2, TILE, TILE), F32)],
        compiler_params=pltpu.CompilerParams(vmem_limit_bytes=24 << 20),
        cost_estimate=pl.CostEstimate(
            flops=a.shape[2] * 2 * 12 * TILE * 2 * TILE,
            bytes_accessed=a.shape[2] * 2 * 4 * TILE * 4,
            transcendentals=0,
        ),
        name="edges",
    )(flags, a, b, c, *keeps)


def band_kernel(acc_ref, own_ref, from_left_ref, from_right_ref, out_ref, rows_ref):
    tiles = acc_ref.shape[0]
    group = out_ref.shape[2]
    per_tile = TILE // W
    for t in range(tiles):
        for part in range(2):
            base = part * TILE
            x = acc_ref[t, base : base + TILE, :]
            rows_ref[t, part] = x
            if t == 0:
                extra = own_ref[0, part] + from_left_ref[part]
                rows_ref[t, part, :MARGIN, :LANES] = x[:MARGIN, :LANES] + extra
            if t == tiles - 1:
                extra = own_ref[1, part] + from_right_ref[part]
                rows_ref[t, part, MARGIN:, LANES:] = x[MARGIN:, LANES:] + extra
    low = lax.broadcasted_iota(jnp.int32, (W, LANES), 1) < MARGIN
    width = TILE + 2 * MARGIN
    for a in range(per_tile):
        for t in range(tiles):
            atom = t * per_tile + a
            for part in range(2):
                x = rows_ref[t, part, a * W : (a + 1) * W, :]
                before = pltpu.roll(x, (width - a * W) % width, 1)[:, :LANES]
                after = pltpu.roll(x, (width - (a + 1) * W) % width, 1)[:, :LANES]
                out_ref[atom // group, part, atom % group] = jnp.where(low, before, after)


def band(acc, own, from_left, from_right, energies):
    tiles = acc.shape[0]
    atoms = tiles * TILE // W
    vmem = pl.BlockSpec(memory_space=pltpu.VMEM)
    return pl.pallas_call(
        band_kernel,
        out_shape=jax.ShapeDtypeStruct((energies, 2, atoms // energies, W, LANES), F32),
        in_specs=[vmem] * 4,
        out_specs=vmem,
        scratch_shapes=[pltpu.VMEM((tiles, 2, TILE, TILE + 2 * MARGIN), F32)],
        compiler_params=pltpu.CompilerParams(vmem_limit_bytes=16 << 20),
        name="band",
    )(acc, own, from_left, from_right)


def picks_kernel(where_ref, out_ref):
    rows = out_ref.shape[0]
    padded = where_ref.shape[1]
    entry = lax.broadcasted_iota(jnp.int32, (rows, padded), 0)
    first = where_ref[...] * W
    for j in range(W):
        hit = entry == first + j
        out_ref[:, j * padded : (j + 1) * padded] = jnp.where(hit, 1.0, 0.0).astype(BF16)


def picks(where, rows):
    padded = where.shape[1]
    vmem = pl.BlockSpec(memory_space=pltpu.VMEM)
    return pl.pallas_call(
        picks_kernel,
        out_shape=jax.ShapeDtypeStruct((rows, W * padded), BF16),
        in_specs=[vmem],
        out_specs=vmem,
        compiler_params=pltpu.CompilerParams(vmem_limit_bytes=16 << 20),
        name="picks",
    )(where)


def scatter_kernel(recv_ref, pick_ref, mix_ref, dham_ref, out_ref, smeared_ref, result_ref):
    energies, _, group, _, _ = recv_ref.shape
    padded = dham_ref.shape[1]
    pairs = out_ref.shape[1]
    columns = [
        recv_ref[:, :, a, :, :].reshape(energies * 2 * W, LANES) for a in range(group)
    ]
    received = halves(jnp.concatenate(columns, axis=1))
    mixed = halves(dot3(halves(mix_ref[...]), received, NN))
    smeared_ref[...] = dot(mixed[0], pick_ref[...], NN) + dot(mixed[1], pick_ref[...], NN)

    def block(part, j, k):
        row = (part * W + j) * energies
        return smeared_ref[row : row + energies, k * padded : (k + 1) * padded]

    def factor(c, i, j):
        row = (c * W + i) * W + j
        return dham_ref[row : row + 1, :]

    for part in range(2):
        for i in range(W):
            total = [None] * W
            for c in range(3):
                for k in range(W):
                    t = None
                    for j in range(W):
                        term = factor(c, i, j) * block(part, j, k)
                        t = term if t is None else t + term
                    for l in range(W):
                        term = t * factor(c, l, k)
                        total[l] = term if total[l] is None else total[l] + term
            for l in range(W):
                row = ((part * W + i) * W + l) * energies
                result_ref[row : row + energies, :] = total[l]
    for e in range(energies):
        one = result_ref[pl.ds(e, 2 * W * W, stride=energies), :]
        out_ref[e] = one.T[:pairs, :]


def scatter(recv, pick, mix, dham, pairs):
    energies, _, group, _, _ = recv.shape
    padded = dham.shape[1]
    vmem = pl.BlockSpec(memory_space=pltpu.VMEM)
    return pl.pallas_call(
        scatter_kernel,
        out_shape=jax.ShapeDtypeStruct((energies, pairs, 2 * W * W), F32),
        in_specs=[vmem] * 4,
        out_specs=vmem,
        scratch_shapes=[
            pltpu.VMEM((2 * W * energies, W * padded), F32),
            pltpu.VMEM((2 * W * W * energies, padded), F32),
        ],
        compiler_params=pltpu.CompilerParams(vmem_limit_bytes=24 << 20),
        name="scatter",
    )(recv, pick, mix, dham)


def build_kernel(phonon_shift, phonon_weight, energies):
    rows_e = jnp.arange(energies, dtype=jnp.int32)[None, :, None]
    cols_f = jnp.arange(energies, dtype=jnp.int32)[None, None, :]
    shifts = phonon_shift[:, None, None]
    emission = (cols_f == rows_e + shifts).astype(F32)
    absorption = (cols_f == rows_e - shifts).astype(F32)
    terms = (
        phonon_weight[0][:, None, None] * emission + phonon_weight[1][:, None, None] * absorption
    )
    return jnp.sum(terms, axis=0)


def build_mix(phonon_shift, phonon_weight, energies):
    kernel = build_kernel(phonon_shift, phonon_weight, energies)
    same = jnp.eye(2 * W, dtype=F32)
    mix = same[:, None, None, :] * kernel[None, :, :, None]
    return mix.reshape(2 * W * energies, energies * 2 * W)


def send(x, pairs):
    return lax.ppermute(x, "orb", pairs)


def per_device(green, sigma, neighbours, phonon_shift, phonon_weight, dham):
    energies = lax.axis_size("energy")
    peers = lax.axis_size("orb")
    e, z = lax.axis_index("energy"), lax.axis_index("orb")
    rows = green.shape[2]
    atoms = rows // W
    degree = neighbours.shape[1]
    group = atoms // energies
    pairs = group * degree
    padded = -(-pairs // LANES) * LANES
    held = sigma.shape[1]

    far = peers >= 4
    up = [(i, i + 1) for i in range(peers - 1)]
    down = [(i + 1, i) for i in range(peers - 1)]
    if far:
        from_left, from_right = z == 1, z == peers - 2
        active = (z > 0) & (z < peers - 1)
    else:
        from_left = from_right = jnp.zeros((), bool)
        active = jnp.ones((), bool)
    limit = jnp.where(from_right, MARGIN, HALF)
    one, inner = jnp.ones((), jnp.int32), active.astype(jnp.int32)

    fixed = pltpu.with_memory_space_constraint(green, pltpu.HBM)
    acc, keep_hi, keep_lo, hi, lo = own_part(
        fixed,
        pltpu.with_memory_space_constraint(sigma, pltpu.HBM),
        jnp.stack([z * held, inner]),
    )
    keeps = [keep_hi, keep_lo]
    counts, listed = [1], [z * held, one]
    rightward = leftward = sigma
    other = near_right = near_left = None
    for k in range(1, peers):
        rightward = send(rightward, up[k - 1 :])
        leftward = send(leftward, down[: peers - k])
        if k < peers - 1:
            rightward, leftward = gate(rightward, leftward, keeps[-1])
        after = []
        if far and k == 1:
            sooner = jnp.where(z == 0, rows - MARGIN, HALF)
            (more,) = rows_at(fixed, [sooner], [rightward, leftward])
            other = send(more, [(0, 1), (peers - 1, peers - 2)])
            after = [more]
        if k == min(2, peers - 1):
            last, leading = rows_at(fixed, [rows - HALF, 0], [rightward, leftward])
            near_right = send(last, up[:-1] if far else up)
            near_left = send(leading, down[1:] if far else down)
        firsts = [jnp.maximum(z - k, 0) * held, jnp.minimum(z + k, peers - 1) * held]
        valid = [(z >= k).astype(jnp.int32), (z + k < peers).astype(jnp.int32)]
        acc, *more_keeps = lesser_part(
            hi, lo, rightward, leftward, jnp.stack(firsts + valid + [inner]), acc, after
        )
        keeps += more_keeps
        counts.append(2)
        listed += [firsts[0], valid[0], firsts[1], valid[1]]
    if other is None:
        other = jnp.zeros_like(near_left)
    listed += [x.astype(jnp.int32) for x in (active, from_left, from_right, limit)]
    to_left, to_right, own = edge_part(
        jnp.stack(listed), other, near_right, near_left, keeps, tuple(counts)
    )
    back_right = send(to_left, down)
    back_left = send(to_right, up)
    lesser = band(acc, own, back_left, back_right, energies)

    mine = lax.dynamic_slice_in_dim(neighbours, e * group, group, axis=0)
    first = z * atoms + e * group
    offset = mine - (first + jnp.arange(group, dtype=jnp.int32))[:, None]
    column = jnp.where(offset < 0, offset + REACH, offset + REACH - 1)
    where = column + 2 * REACH * jnp.arange(group, dtype=jnp.int32)[:, None]
    where = jnp.pad(where.reshape(1, pairs), ((0, 0), (0, padded - pairs)), constant_values=-1)
    pick = picks(where, group * LANES)
    mix = build_mix(phonon_shift, phonon_weight, energies)
    factors = lax.dynamic_slice_in_dim(
        dham.transpose(1, 2, 3, 0).reshape(3 * W * W, -1), e * pairs, pairs, axis=1
    )
    factors = jnp.pad(factors, ((0, 0), (0, padded - pairs)))

    recv = lax.all_to_all(lesser, "energy", split_axis=0, concat_axis=0, tiled=True)
    spread = scatter(recv, pick, mix, factors, pairs)
    result = lax.all_to_all(spread, "energy", split_axis=0, concat_axis=0, tiled=True)
    return result.reshape(1, atoms * degree, 2 * W * W)


def solution(mesh):
    return jax.shard_map(
        per_device,
        mesh=mesh,
        in_specs=(
            P("energy", None, "orb", None),
            P("energy", "orb", None, None, None),
            P("orb", None),
            P(),
            P(),
            P("orb", None, None, None),
        ),
        out_specs=P("energy", "orb", None),
        check_vma=False,
    )
```

```python
import functools

import jax
import jax.numpy as jnp
from jax import lax
from jax.experimental import pallas as pl
from jax.experimental.pallas import tpu as pltpu
from jax.sharding import PartitionSpec as P

W = 8
BS = 128
REACH = 8
MARGIN = REACH * W
HALF = MARGIN // 2
TILE = 128
LANES = 128
F32, BF16 = jnp.float32, jnp.bfloat16

NT = (((1,), (1,)), ((), ()))
NN = (((1,), (0,)), ((), ()))


def halves(x):
    hi = x.astype(BF16)
    return hi, (x - hi.astype(F32)).astype(BF16)


def dot(a, b, dims):
    return lax.dot_general(a, b, dims, preferred_element_type=F32)


def dot3(a, b, dims):
    left = jnp.concatenate([a[0], a[0], a[1]], axis=1)
    right = jnp.concatenate([b[0], b[1], b[0]], axis=dims[0][1][0])
    return dot(left, right, dims)


def blocks_at_once(held):
    return 2 if held % 2 == 0 else 1


def some_blocks(lane, weights, hi_ref, lo_ref, acc_ref, edges, active):
    rows = hi_ref.shape[0] - 2 * MARGIN
    wide = 2 * BS
    split, products = [], []
    for n, (real, imag) in enumerate(weights):
        top = jnp.concatenate([real, imag], axis=1)
        weight = halves(jnp.concatenate([top, jnp.concatenate([-imag, real], axis=1)], axis=0))
        cols = pl.ds(lane + n * wide, wide)
        own = [ref[MARGIN : MARGIN + rows, cols] for ref in (hi_ref, lo_ref)]
        product = halves(dot3(own, weight, NN))
        for ref, part in zip(edges, product):
            ref[n, :MARGIN, :] = part[:MARGIN]
            ref[n, 3 * MARGIN :, :] = part[rows - MARGIN :]
        split.append(weight)
        products.append(product)
    cols = pl.ds(lane, len(weights) * wide)
    for t in range(rows // TILE):
        both = []
        for part in zip(*products):
            lanes = []
            for x in part:
                x = x[t * TILE : (t + 1) * TILE]
                turned = jnp.concatenate([x[:, BS:], -x[:, :BS]], axis=1)
                lanes.append(jnp.concatenate([x, turned], axis=0))
            both.append(jnp.concatenate(lanes, axis=1))
        near = pl.ds(t * TILE, TILE + 2 * MARGIN)
        acc_ref[t] = acc_ref[t] + dot3(both, (hi_ref[near, cols], lo_ref[near, cols]), NT)

    @pl.when(active)
    def _():
        for n, weight in enumerate(split):
            one = pl.ds(lane + n * wide, wide)
            outer = [
                jnp.concatenate(
                    [ref[MARGIN : 2 * MARGIN, one], ref[rows : rows + MARGIN, one]], axis=0
                )
                for ref in (hi_ref, lo_ref)
            ]
            for ref, part in zip(edges, halves(dot3(outer, weight, NT))):
                ref[n, MARGIN : 3 * MARGIN, :] = part


def shard_loop(first_block, self_ref, hi_ref, lo_ref, acc_ref, keeps, slot, active):
    held = self_ref.shape[1]
    once = blocks_at_once(held)

    def step(g, carry):
        lane = pl.multiple_of((first_block + g * once) * 2 * BS, 2 * BS)
        weights = [
            (self_ref[0, g * once + n, 0], self_ref[0, g * once + n, 1]) for n in range(once)
        ]
        slots = pl.ds(slot + g * once, once)
        kept = tuple(ref.at[slots] for ref in keeps)
        some_blocks(lane, weights, hi_ref, lo_ref, acc_ref, kept, active)
        return carry

    lax.fori_loop(0, held // once, step, 0)


def is_far(peers):
    return peers >= 4


def is_inner():
    z, peers = lax.axis_index("orb"), lax.axis_size("orb")
    if is_far(peers):
        return jnp.logical_and(z > 0, z < peers - 1)
    return z >= 0


def neighbour(distance):
    z, peers = lax.axis_index("orb"), lax.axis_size("orb")
    number = z + distance
    return jnp.clip(number, 0, peers - 1), jnp.logical_and(number >= 0, number < peers)


def own_kernel(
    green_ref, sigma_ref, *rest
):
    acc_ref, keep_hi_ref, keep_lo_ref, hi_ref, lo_ref, buf, self_ref, sem = rest[-8:]
    rows, held = green_ref.shape[2], sigma_ref.shape[1]
    blocks = green_ref.shape[3] // BS
    begin, active = lax.axis_index("orb") * held, is_inner()

    def block_of(s):
        return lax.rem(begin + s, blocks)

    def fetch(s):
        col = pl.multiple_of(block_of(s) * BS, BS)
        return pltpu.make_async_copy(
            green_ref.at[0, :, :, pl.ds(col, BS)], buf.at[s], sem.at[s]
        )

    def store(s, carry):
        fetch(s).wait()
        lanes = pl.ds(pl.multiple_of(block_of(s) * 2 * BS, 2 * BS), 2 * BS)
        parts = halves(jnp.concatenate([buf[s, 0], buf[s, 1]], axis=1))
        for ref, part in zip((hi_ref, lo_ref), parts):
            ref[MARGIN : MARGIN + rows, lanes] = part
        return carry

    load = pltpu.make_async_copy(sigma_ref, self_ref, sem.at[blocks])
    load.start()
    for s in range(blocks):
        fetch(s).start()
    acc_ref[...] = jnp.zeros_like(acc_ref)
    for ref in (hi_ref, lo_ref):
        ref[:MARGIN, :] = jnp.zeros((MARGIN, ref.shape[1]), BF16)
        ref[MARGIN + rows :, :] = jnp.zeros((MARGIN, ref.shape[1]), BF16)
    lax.fori_loop(0, held, store, 0)
    load.wait()
    shard_loop(begin, self_ref, hi_ref, lo_ref, acc_ref, (keep_hi_ref, keep_lo_ref), 0, active)
    lax.fori_loop(held, blocks, store, 0)


def own_part(green, sigma, after):
    rows, held = green.shape[2], sigma.shape[1]
    tiles, blocks = rows // TILE, green.shape[3] // BS
    vmem = pl.BlockSpec(memory_space=pltpu.VMEM)
    hbm = pl.BlockSpec(memory_space=pl.ANY)
    keep = jax.ShapeDtypeStruct((held, 4 * MARGIN, 2 * BS), BF16)
    whole = jax.ShapeDtypeStruct((rows + 2 * MARGIN, blocks * 2 * BS), BF16)
    return pl.pallas_call(
        own_kernel,
        out_shape=(
            jax.ShapeDtypeStruct((tiles, 2 * TILE, TILE + 2 * MARGIN), F32),
            keep,
            keep,
            whole,
            whole,
        ),
        in_specs=[hbm] * (2 + len(after)),
        out_specs=(vmem,) * 5,
        scratch_shapes=[
            pltpu.VMEM((blocks, 2, rows, BS), F32),
            pltpu.VMEM(sigma.shape, F32),
            pltpu.SemaphoreType.DMA((blocks + 1,)),
        ],
        compiler_params=pltpu.CompilerParams(vmem_limit_bytes=40 << 20),
        cost_estimate=pl.CostEstimate(
            flops=held * 6 * rows * 2 * BS * (2 * BS + 4 * TILE),
            bytes_accessed=blocks * rows * BS * 8,
            transcendentals=0,
        ),
        name="lesser_own",
    )(green, sigma, *after)


def lesser_kernel(places, held, hi_ref, lo_ref, before_ref, *rest):
    sigmas, rest = rest[: len(places)], rest[len(places) :]
    acc_ref, *keeps = rest[-3:]
    acc_ref[...] = before_ref[...]
    slot = 0
    for (distance, first), self_ref in zip(places, sigmas):
        number, valid = neighbour(distance)

        @pl.when(valid)
        def _():
            shard_loop(
                number * held + first, self_ref, hi_ref, lo_ref, acc_ref, keeps, slot, is_inner()
            )

        slot += self_ref.shape[1]


def lesser_part(hi, lo, before, shards, places, held, after=()):
    vmem = pl.BlockSpec(memory_space=pltpu.VMEM)
    count = sum(x.shape[1] for x in shards)
    kept = jax.ShapeDtypeStruct((count, 4 * MARGIN, 2 * BS), BF16)
    outs = [jax.ShapeDtypeStruct(before.shape, F32), kept, kept]
    return pl.pallas_call(
        functools.partial(lesser_kernel, places, held),
        out_shape=outs,
        in_specs=[vmem] * (3 + len(shards)) + [pl.BlockSpec(memory_space=pl.ANY)] * len(after),
        out_specs=[vmem] * len(outs),
        input_output_aliases={2: 0},
        compiler_params=pltpu.CompilerParams(vmem_limit_bytes=26 << 20),
        cost_estimate=pl.CostEstimate(
            flops=count * 3 * hi.shape[0] * 2 * BS * (2 * BS + 4 * TILE),
            bytes_accessed=8 * before.size,
            transcendentals=0,
        ),
        name="lesser_more",
    )(hi, lo, before, *shards, *after)


def rows_kernel(count, green_ref, *rest):
    outs, sem = rest[-1 - count : -1], rest[-1]
    z, rows = lax.axis_index("orb"), green_ref.shape[2]
    starts = [rows - HALF, 0, jnp.where(z == 0, rows - MARGIN, HALF)]
    copies = [
        pltpu.make_async_copy(
            green_ref.at[0, :, pl.ds(pl.multiple_of(starts[n], HALF), HALF), :],
            out,
            sem.at[n],
        )
        for n, out in enumerate(outs)
    ]
    for copy in copies:
        copy.start()
    for copy in copies:
        copy.wait()


def rows_at(green, count):
    out = jax.ShapeDtypeStruct((2, HALF, green.shape[3]), F32)
    return pl.pallas_call(
        functools.partial(rows_kernel, count),
        out_shape=[out] * count,
        in_specs=[pl.BlockSpec(memory_space=pl.ANY)],
        out_specs=[pl.BlockSpec(memory_space=pltpu.VMEM)] * count,
        scratch_shapes=[pltpu.SemaphoreType.DMA((count,))],
        compiler_params=pltpu.CompilerParams(vmem_limit_bytes=8 << 20),
        name="rows",
    )(green)


def load_kernel(cases, first, piece, green_ref, right_ref, left_ref, *rest):
    outs, sem = rest[-1 - 2 * len(first) : -1], rest[-1]
    per = BS // HALF
    for side, ((rows, begin), source) in enumerate(zip(cases, (right_ref, left_ref))):
        row = pl.multiple_of(begin, HALF)
        taken, passed = [], []
        for n, block in enumerate(first):
            out = outs[side * len(first) + n]
            passed.append(
                pltpu.make_async_copy(
                    source.at[:, pl.ds(block - first[0], piece)], out, sem.at[side, n]
                )
            )
            for m in range(piece):
                for part in range(2):
                    for q in range(per):
                        col = ((block + m) * per + q) * BS
                        taken.append(
                            pltpu.make_async_copy(
                                green_ref.at[0, part, pl.ds(row, HALF), pl.ds(col, BS)],
                                out.at[0, m, part, pl.ds(q * HALF, HALF), :],
                                sem.at[side, len(taken)],
                            )
                        )
        for want, copies in ((True, taken), (False, passed)):

            @pl.when(rows == want)
            def _():
                for copy in copies:
                    copy.start()

    for side, ((rows, begin), source) in enumerate(zip(cases, (right_ref, left_ref))):
        row = pl.multiple_of(begin, HALF)
        for want in (True, False):

            @pl.when(rows == want)
            def _():
                count = 0
                for n, block in enumerate(first):
                    out = outs[side * len(first) + n]
                    if not want:
                        pltpu.make_async_copy(
                            source.at[:, pl.ds(block - first[0], piece)], out, sem.at[side, n]
                        ).wait()
                        continue
                    for m in range(piece):
                        for part in range(2):
                            for q in range(per):
                                col = ((block + m) * per + q) * BS
                                pltpu.make_async_copy(
                                    green_ref.at[0, part, pl.ds(row, HALF), pl.ds(col, BS)],
                                    out.at[0, m, part, pl.ds(q * HALF, HALF), :],
                                    sem.at[side, count],
                                ).wait()
                                count += 1


def load(stage, green, right, left, first, piece, after):
    rows = green.shape[2]

    def kernel(*refs):
        z, peers = lax.axis_index("orb"), lax.axis_size("orb")
        if stage == 0:
            cases = ((z == 0, rows - MARGIN), (z == peers - 1, HALF))
        else:
            cases = ((z < peers - 2, rows - HALF), (z > 1, 0))
        load_kernel(cases, first, piece, *refs)

    hbm = pl.BlockSpec(memory_space=pl.ANY)
    out = jax.ShapeDtypeStruct((1, piece) + right.shape[2:], F32)
    outs = pl.pallas_call(
        kernel,
        out_shape=[out] * (2 * len(first)),
        in_specs=[hbm] * (3 + len(after)),
        out_specs=[hbm] * (2 * len(first)),
        scratch_shapes=[
            pltpu.SemaphoreType.DMA((2, len(first) * piece * 2 * (BS // HALF)))
        ],
        compiler_params=pltpu.CompilerParams(vmem_limit_bytes=2 << 20),
        cost_estimate=pl.CostEstimate(
            flops=0, bytes_accessed=8 * out.size * len(first), transcendentals=0
        ),
        name="load",
    )(green, right, left, *after)
    return outs[: len(first)], outs[len(first) :]


def edge_kernel(places, held, part_of, riding, last, *refs):
    halos, refs = refs[: 4 if riding else 3], refs[4 if riding else 3 :]
    keeps, refs = refs[: 2 * len(places)], refs[2 * len(places) :]
    z, peers = lax.axis_index("orb"), lax.axis_size("orb")
    if is_far(peers):
        from_left, from_right = z == 1, z == peers - 2
    else:
        from_left = from_right = z < 0
    limit = jnp.where(from_right, MARGIN, HALF)
    if part_of[0] > 0:
        before_ref, refs = refs[0], refs[1:]
    acc_ref = refs[-1]
    acc_ref[...] = before_ref[...] if part_of[0] > 0 else jnp.zeros_like(acc_ref)
    group = peers // part_of[1]
    begin = part_of[0] * group

    def halo_rows(ref, part, number, s):
        if riding:
            return ref[0, number - begin, part, s * HALF : (s + 1) * HALF, :]
        col = pl.multiple_of((number * held + s) * BS, BS)
        return ref[part, :, pl.ds(col, BS)]

    def add(number, first, hi, lo, at, count):
        for side in range(2):
            fields = []
            for part in range(2):
                inner, outer = [], []
                for s in range(first, first + count):
                    if riding:
                        near, beyond = halos[2 + side], halos[side]
                    else:
                        near, beyond = halos[1 + side], halos[0]
                    inner.append(halo_rows(near, part, number, s))
                    outer.append(halo_rows(beyond, part, number, s))
                inner, outer = jnp.concatenate(inner, axis=1), jnp.concatenate(outer, axis=1)
                outer = jnp.where(from_left if side == 0 else from_right, outer, 0.0)
                rows = [outer, inner] if side == 0 else [inner, outer]
                fields.append(halves(jnp.concatenate(rows, axis=0)))
            halo = []
            for real, imag in zip(*fields):
                lanes = []
                for s in range(count):
                    one = slice(s * BS, (s + 1) * BS)
                    lanes += [
                        jnp.concatenate([real[:, one], -imag[:, one]], axis=0),
                        jnp.concatenate([imag[:, one], real[:, one]], axis=0),
                    ]
                halo.append(jnp.concatenate(lanes, axis=1))
            rows = slice(side * TILE, (side + 1) * TILE)
            kept = [
                jnp.concatenate([ref[at + s, rows, :] for s in range(count)], axis=1)
                for ref in (hi, lo)
            ]
            acc_ref[side] = acc_ref[side] + dot3(halo, kept, NT)

    @pl.when(is_inner())
    def _():
        for k, shards in enumerate(places):
            at = 0
            for distance, first, count in shards:
                number, valid = neighbour(distance)
                valid = valid & (number >= begin) & (number < begin + group)

                @pl.when(valid)
                def _():
                    add(number, first, keeps[2 * k], keeps[2 * k + 1], at, count)

                at += count

    if not last:
        return
    left_ref, right_ref, own_ref = refs[-4:-1]
    lane = lax.broadcasted_iota(jnp.int32, (MARGIN, LANES), 1)
    row = lax.broadcasted_iota(jnp.int32, (MARGIN, LANES), 0)
    low = lane < MARGIN
    left, right = acc_ref[0], acc_ref[1]
    turned_left, turned_right = left.T[:MARGIN], right.T[MARGIN:]
    left_ref[0] = jnp.where(low, 0.0, left[:MARGIN])
    left_ref[1] = jnp.where(low, 0.0, -left[MARGIN:])
    right_ref[0] = jnp.where(lane < limit, right[:MARGIN], 0.0)
    right_ref[1] = jnp.where(lane < limit, -right[MARGIN:], 0.0)
    own_ref[0, 0] = jnp.where(low, turned_left, 0.0)
    own_ref[0, 1] = jnp.where(low, pltpu.roll(turned_left, MARGIN, 1), 0.0)
    mine = jnp.logical_and(row < limit, lane >= MARGIN)
    own_ref[1, 0] = jnp.where(mine, pltpu.roll(turned_right, MARGIN, 1), 0.0)
    own_ref[1, 1] = jnp.where(mine, turned_right, 0.0)


def edge_part(halos, keeps, places, held, part_of, riding, before, after):
    vmem = pl.BlockSpec(memory_space=pltpu.VMEM)
    last = part_of[0] == part_of[1] - 1
    side = jax.ShapeDtypeStruct((2, MARGIN, LANES), F32)
    acc = (2, TILE, TILE)
    ends = [side, side, jax.ShapeDtypeStruct((2, 2, MARGIN, LANES), F32)]
    args = [*halos, *keeps] + ([] if before is None else [before])
    return pl.pallas_call(
        functools.partial(edge_kernel, places, held, part_of, riding, last),
        out_shape=ends if last else [jax.ShapeDtypeStruct(acc, F32)],
        in_specs=[vmem] * len(args) + [pl.BlockSpec(memory_space=pl.ANY)] * len(after),
        out_specs=[vmem] * (3 if last else 1),
        scratch_shapes=[pltpu.VMEM(acc, F32)] if last else [],
        compiler_params=pltpu.CompilerParams(vmem_limit_bytes=20 << 20),
        cost_estimate=pl.CostEstimate(
            flops=(1 << 31) // part_of[1],
            bytes_accessed=(8 << 20) // part_of[1],
            transcendentals=0,
        ),
        name="edges",
    )(*args, *after)


def band_kernel(acc_ref, own_ref, from_left_ref, from_right_ref, out_ref, rows_ref):
    tiles = acc_ref.shape[0]
    group = out_ref.shape[2]
    per_tile = TILE // W
    for t in range(tiles):
        for part in range(2):
            base = part * TILE
            x = acc_ref[t, base : base + TILE, :]
            rows_ref[t, part] = x
            if t == 0:
                extra = own_ref[0, part] + from_left_ref[part]
                rows_ref[t, part, :MARGIN, :LANES] = x[:MARGIN, :LANES] + extra
            if t == tiles - 1:
                extra = own_ref[1, part] + from_right_ref[part]
                rows_ref[t, part, MARGIN:, LANES:] = x[MARGIN:, LANES:] + extra
    low = lax.broadcasted_iota(jnp.int32, (W, LANES), 1) < MARGIN
    width = TILE + 2 * MARGIN
    for a in range(per_tile):
        for t in range(tiles):
            atom = t * per_tile + a
            for part in range(2):
                x = rows_ref[t, part, a * W : (a + 1) * W, :]
                before = pltpu.roll(x, (width - a * W) % width, 1)[:, :LANES]
                after = pltpu.roll(x, (width - (a + 1) * W) % width, 1)[:, :LANES]
                out_ref[atom // group, part, atom % group] = jnp.where(low, before, after)


def band(acc, own, from_left, from_right, energies):
    tiles = acc.shape[0]
    atoms = tiles * TILE // W
    vmem = pl.BlockSpec(memory_space=pltpu.VMEM)
    return pl.pallas_call(
        band_kernel,
        out_shape=jax.ShapeDtypeStruct((energies, 2, atoms // energies, W, LANES), F32),
        in_specs=[vmem] * 4,
        out_specs=vmem,
        scratch_shapes=[pltpu.VMEM((tiles, 2, TILE, TILE + 2 * MARGIN), F32)],
        compiler_params=pltpu.CompilerParams(vmem_limit_bytes=16 << 20),
        name="band",
    )(acc, own, from_left, from_right)


def scatter_kernel(recv_ref, where_ref, mix_ref, dham_ref, out_ref, smeared_ref, result_ref):
    energies, _, group, _, _ = recv_ref.shape
    padded = dham_ref.shape[1]
    pairs = out_ref.shape[1]
    columns = [
        recv_ref[:, :, a, :, :].reshape(energies * 2 * W, LANES) for a in range(group)
    ]
    received = halves(jnp.concatenate(columns, axis=1))
    mixed = halves(dot3(halves(mix_ref[...]), received, NN))
    entry = lax.broadcasted_iota(jnp.int32, (group * LANES, padded), 0)
    first = where_ref[...] * W
    for j in range(W):
        pick = jnp.where(entry == first + j, 1.0, 0.0).astype(BF16)
        smeared_ref[:, j * padded : (j + 1) * padded] = dot(mixed[0], pick, NN) + dot(
            mixed[1], pick, NN
        )

    def block(part, j, k):
        row = (part * W + j) * energies
        return smeared_ref[row : row + energies, k * padded : (k + 1) * padded]

    def factor(c, i, j):
        row = (c * W + i) * W + j
        return dham_ref[row : row + 1, :]

    for part in range(2):
        for i in range(W):
            total = [None] * W
            for c in range(3):
                for k in range(W):
                    t = None
                    for j in range(W):
                        term = factor(c, i, j) * block(part, j, k)
                        t = term if t is None else t + term
                    for l in range(W):
                        term = t * factor(c, l, k)
                        total[l] = term if total[l] is None else total[l] + term
            for l in range(W):
                row = ((part * W + i) * W + l) * energies
                result_ref[row : row + energies, :] = total[l]
    for e in range(energies):
        one = result_ref[pl.ds(e, 2 * W * W, stride=energies), :]
        out_ref[e] = one.T[:pairs, :]


def scatter(recv, where, mix, dham, pairs):
    energies, _, group, _, _ = recv.shape
    padded = dham.shape[1]
    vmem = pl.BlockSpec(memory_space=pltpu.VMEM)
    return pl.pallas_call(
        scatter_kernel,
        out_shape=jax.ShapeDtypeStruct((energies, pairs, 2 * W * W), F32),
        in_specs=[vmem] * 4,
        out_specs=vmem,
        scratch_shapes=[
            pltpu.VMEM((2 * W * energies, W * padded), F32),
            pltpu.VMEM((2 * W * W * energies, padded), F32),
        ],
        compiler_params=pltpu.CompilerParams(vmem_limit_bytes=24 << 20),
        name="scatter",
    )(recv, where, mix, dham)


def build_kernel(phonon_shift, phonon_weight, energies):
    rows_e = jnp.arange(energies, dtype=jnp.int32)[None, :, None]
    cols_f = jnp.arange(energies, dtype=jnp.int32)[None, None, :]
    shifts = phonon_shift[:, None, None]
    emission = (cols_f == rows_e + shifts).astype(F32)
    absorption = (cols_f == rows_e - shifts).astype(F32)
    terms = (
        phonon_weight[0][:, None, None] * emission + phonon_weight[1][:, None, None] * absorption
    )
    return jnp.sum(terms, axis=0)


def build_mix(phonon_shift, phonon_weight, energies):
    kernel = build_kernel(phonon_shift, phonon_weight, energies)
    same = jnp.eye(2 * W, dtype=F32)
    mix = same[:, None, None, :] * kernel[None, :, :, None]
    return mix.reshape(2 * W * energies, energies * 2 * W)


def send(x, pairs):
    return lax.ppermute(x, "orb", pairs)


def per_device(green, sigma, neighbours, phonon_shift, phonon_weight, dham):
    energies = lax.axis_size("energy")
    peers = lax.axis_size("orb")
    e, z = lax.axis_index("energy"), lax.axis_index("orb")
    rows = green.shape[2]
    atoms = rows // W
    degree = neighbours.shape[1]
    group = atoms // energies
    pairs = group * degree
    padded = -(-pairs // LANES) * LANES
    held = sigma.shape[1]

    far = is_far(peers)
    riding = peers == 4 and held == BS // HALF
    up = [(i, i + 1) for i in range(peers - 1)]
    down = [(i + 1, i) for i in range(peers - 1)]
    fixed = pltpu.with_memory_space_constraint(green, pltpu.HBM)
    right, left = send(sigma, up), send(sigma, down)

    mine = lax.dynamic_slice_in_dim(neighbours, e * group, group, axis=0)
    first = z * atoms + e * group
    offset = mine - (first + jnp.arange(group, dtype=jnp.int32))[:, None]
    column = jnp.where(offset < 0, offset + REACH, offset + REACH - 1)
    where = column + 2 * REACH * jnp.arange(group, dtype=jnp.int32)[:, None]
    where = jnp.pad(where.reshape(1, pairs), ((0, 0), (0, padded - pairs)), constant_values=-1)
    mix = build_mix(phonon_shift, phonon_weight, energies)
    factors = lax.dynamic_slice_in_dim(
        dham.transpose(1, 2, 3, 0).reshape(3 * W * W, -1), e * pairs, pairs, axis=1
    )
    factors = jnp.pad(factors, ((0, 0), (0, padded - pairs)))


    acc, *keeps, hi, lo = own_part(
        fixed, pltpu.with_memory_space_constraint(sigma, pltpu.HBM), [where, mix, factors]
    )
    more = functools.partial(lesser_part, hi, lo, held=held)
    places = [[(0, 0, held)], [(-1, 0, held), (1, 0, held)]]
    if riding:
        piece = held // 2
        cuts = [0, piece]
        rights, lefts = load(0, fixed, right, left, cuts, piece, [keeps[-1]])
        rights, lefts = [send(x, up) for x in rights], [send(x, down) for x in lefts]
        acc, *kept = more(acc, [right, left], [(-1, 0), (1, 0)])
        keeps += kept
        ends = []
        for h, first in enumerate(cuts):
            (over,), (under,) = load(
                1, fixed, rights[h], lefts[h], [first], piece, [kept[-1]]
            )
            ends.append((send(over, up), send(under, down)))
        acc, *kept = more(
            acc, [*rights, *lefts], [(d, first) for d in (-2, 2) for first in cuts]
        )
        keeps += kept
        places.append([(d, first, piece) for d in (-2, 2) for first in cuts])
        edge = None
        for h, first in enumerate(cuts):
            acc, *kept = more(
                acc, list(ends[h]), [(-3, first), (3, first)], after=[] if edge is None else [edge]
            )
            halos = [rights[h], lefts[h], *ends[h]]
            edge = edge_part(halos, keeps, places, held, (h, 2), True, edge, kept[:1])
            edge = edge[0] if h == 0 else edge
        to_left, to_right, own = edge
    else:
        last, leading, *outer = rows_at(fixed, 3 if far else 2)
        near_right = send(last, up[:-1] if far else up)
        near_left = send(leading, down[1:] if far else down)
        if far:
            other = send(outer[0], [(0, 1), (peers - 1, peers - 2)])
        else:
            other = jnp.zeros_like(near_left)
        for k in range(1, peers):
            acc, *kept = more(acc, [right, left], [(-k, 0), (k, 0)])
            keeps += kept
            if k > 1:
                places.append([(-k, 0, held), (k, 0, held)])
            right, left = send(right, up[k:]), send(left, down[: peers - 1 - k])
        to_left, to_right, own = edge_part(
            [other, near_right, near_left], keeps, places, held, (0, 1), False, None, []
        )
    back_right = send(to_left, down)
    back_left = send(to_right, up)
    lesser = band(acc, own, back_left, back_right, energies)

    recv = lax.all_to_all(lesser, "energy", split_axis=0, concat_axis=0, tiled=True)
    spread = scatter(recv, where, mix, factors, pairs)
    result = lax.all_to_all(spread, "energy", split_axis=0, concat_axis=0, tiled=True)
    return result.reshape(1, atoms * degree, 2 * W * W)


def solution(mesh):
    return jax.shard_map(
        per_device,
        mesh=mesh,
        in_specs=(
            P("energy", None, "orb", None),
            P("energy", "orb", None, None, None),
            P("orb", None),
            P(),
            P(),
            P("orb", None, None, None),
        ),
        out_specs=P("energy", "orb", None),
        check_vma=False,
    )
```

```python
import functools

import jax
import jax.numpy as jnp
from jax import lax
from jax.experimental import pallas as pl
from jax.experimental.pallas import tpu as pltpu
from jax.sharding import PartitionSpec as P

W = 8
BS = 128
REACH = 8
MARGIN = REACH * W
HALF = MARGIN // 2
TILE = 128
LANES = 128
F32, BF16 = jnp.float32, jnp.bfloat16

NT = (((1,), (1,)), ((), ()))
NN = (((1,), (0,)), ((), ()))


def halves(x):
    hi = x.astype(BF16)
    return hi, (x - hi.astype(F32)).astype(BF16)


def dot(a, b, dims):
    return lax.dot_general(a, b, dims, preferred_element_type=F32)


def dot3(a, b, dims):
    left = jnp.concatenate([a[0], a[0], a[1]], axis=1)
    right = jnp.concatenate([b[0], b[1], b[0]], axis=dims[0][1][0])
    return dot(left, right, dims)


def blocks_at_once(held):
    return 2 if held % 2 == 0 else 1


def some_blocks(lane, weights, hi_ref, lo_ref, acc_ref, edges, active):
    rows = hi_ref.shape[0] - 2 * MARGIN
    wide = 2 * BS
    split, products = [], []
    for n, (real, imag) in enumerate(weights):
        top = jnp.concatenate([real, imag], axis=1)
        weight = halves(jnp.concatenate([top, jnp.concatenate([-imag, real], axis=1)], axis=0))
        cols = pl.ds(lane + n * wide, wide)
        own = [ref[MARGIN : MARGIN + rows, cols] for ref in (hi_ref, lo_ref)]
        product = halves(dot3(own, weight, NN))
        for ref, part in zip(edges, product):
            ref[n, :MARGIN, :] = part[:MARGIN]
            ref[n, 3 * MARGIN :, :] = part[rows - MARGIN :]
        split.append(weight)
        products.append(product)
    cols = pl.ds(lane, len(weights) * wide)
    for t in range(rows // TILE):
        both = []
        for part in zip(*products):
            lanes = []
            for x in part:
                x = x[t * TILE : (t + 1) * TILE]
                turned = jnp.concatenate([x[:, BS:], -x[:, :BS]], axis=1)
                lanes.append(jnp.concatenate([x, turned], axis=0))
            both.append(jnp.concatenate(lanes, axis=1))
        near = pl.ds(t * TILE, TILE + 2 * MARGIN)
        acc_ref[t] = acc_ref[t] + dot3(both, (hi_ref[near, cols], lo_ref[near, cols]), NT)

    @pl.when(active)
    def _():
        for n, weight in enumerate(split):
            one = pl.ds(lane + n * wide, wide)
            outer = [
                jnp.concatenate(
                    [ref[MARGIN : 2 * MARGIN, one], ref[rows : rows + MARGIN, one]], axis=0
                )
                for ref in (hi_ref, lo_ref)
            ]
            for ref, part in zip(edges, halves(dot3(outer, weight, NT))):
                ref[n, MARGIN : 3 * MARGIN, :] = part


def shard_loop(first_block, self_ref, hi_ref, lo_ref, acc_ref, keeps, slot, active):
    held = self_ref.shape[1]
    once = blocks_at_once(held)

    def step(g, carry):
        lane = pl.multiple_of((first_block + g * once) * 2 * BS, 2 * BS)
        weights = [
            (self_ref[0, g * once + n, 0], self_ref[0, g * once + n, 1]) for n in range(once)
        ]
        slots = pl.ds(slot + g * once, once)
        kept = tuple(ref.at[slots] for ref in keeps)
        some_blocks(lane, weights, hi_ref, lo_ref, acc_ref, kept, active)
        return carry

    lax.fori_loop(0, held // once, step, 0)


def is_far(peers):
    return peers >= 4


def is_inner():
    z, peers = lax.axis_index("orb"), lax.axis_size("orb")
    if is_far(peers):
        return jnp.logical_and(z > 0, z < peers - 1)
    return z >= 0


def neighbour(distance):
    z, peers = lax.axis_index("orb"), lax.axis_size("orb")
    number = z + distance
    return jnp.clip(number, 0, peers - 1), jnp.logical_and(number >= 0, number < peers)


def own_kernel(
    green_ref, sigma_ref, *rest
):
    acc_ref, keep_hi_ref, keep_lo_ref, hi_ref, lo_ref, buf, self_ref, sem = rest[-8:]
    rows, held = green_ref.shape[2], sigma_ref.shape[1]
    blocks = green_ref.shape[3] // BS
    begin, active = lax.axis_index("orb") * held, is_inner()

    def block_of(s):
        return lax.rem(begin + s, blocks)

    def fetch(s):
        col = pl.multiple_of(block_of(s) * BS, BS)
        return pltpu.make_async_copy(
            green_ref.at[0, :, :, pl.ds(col, BS)], buf.at[s], sem.at[s]
        )

    def store(s, carry):
        fetch(s).wait()
        lanes = pl.ds(pl.multiple_of(block_of(s) * 2 * BS, 2 * BS), 2 * BS)
        parts = halves(jnp.concatenate([buf[s, 0], buf[s, 1]], axis=1))
        for ref, part in zip((hi_ref, lo_ref), parts):
            ref[MARGIN : MARGIN + rows, lanes] = part
        return carry

    load = pltpu.make_async_copy(sigma_ref, self_ref, sem.at[blocks])
    load.start()
    for s in range(blocks):
        fetch(s).start()
    acc_ref[...] = jnp.zeros_like(acc_ref)
    for ref in (hi_ref, lo_ref):
        ref[:MARGIN, :] = jnp.zeros((MARGIN, ref.shape[1]), BF16)
        ref[MARGIN + rows :, :] = jnp.zeros((MARGIN, ref.shape[1]), BF16)
    lax.fori_loop(0, held, store, 0)
    load.wait()
    shard_loop(begin, self_ref, hi_ref, lo_ref, acc_ref, (keep_hi_ref, keep_lo_ref), 0, active)
    lax.fori_loop(held, blocks, store, 0)


def own_part(green, sigma, after):
    rows, held = green.shape[2], sigma.shape[1]
    tiles, blocks = rows // TILE, green.shape[3] // BS
    vmem = pl.BlockSpec(memory_space=pltpu.VMEM)
    hbm = pl.BlockSpec(memory_space=pl.ANY)
    keep = jax.ShapeDtypeStruct((held, 4 * MARGIN, 2 * BS), BF16)
    whole = jax.ShapeDtypeStruct((rows + 2 * MARGIN, blocks * 2 * BS), BF16)
    return pl.pallas_call(
        own_kernel,
        out_shape=(
            jax.ShapeDtypeStruct((tiles, 2 * TILE, TILE + 2 * MARGIN), F32),
            keep,
            keep,
            whole,
            whole,
        ),
        in_specs=[hbm] * (2 + len(after)),
        out_specs=(vmem,) * 5,
        scratch_shapes=[
            pltpu.VMEM((blocks, 2, rows, BS), F32),
            pltpu.VMEM(sigma.shape, F32),
            pltpu.SemaphoreType.DMA((blocks + 1,)),
        ],
        compiler_params=pltpu.CompilerParams(vmem_limit_bytes=40 << 20),
        cost_estimate=pl.CostEstimate(
            flops=held * 6 * rows * 2 * BS * (2 * BS + 4 * TILE),
            bytes_accessed=blocks * rows * BS * 8,
            transcendentals=0,
        ),
        name="lesser_own",
    )(green, sigma, *after)


def lesser_kernel(places, held, hi_ref, lo_ref, before_ref, *rest):
    sigmas, rest = rest[: len(places)], rest[len(places) :]
    acc_ref, *keeps = rest[-3:]
    acc_ref[...] = before_ref[...]
    slot = 0
    for distance, self_ref in zip(places, sigmas):
        number, valid = neighbour(distance)

        @pl.when(valid)
        def _():
            shard_loop(
                number * held, self_ref, hi_ref, lo_ref, acc_ref, keeps, slot, is_inner()
            )

        slot += self_ref.shape[1]


def lesser_part(hi, lo, before, shards, places, held, after=()):
    vmem = pl.BlockSpec(memory_space=pltpu.VMEM)
    count = sum(x.shape[1] for x in shards)
    kept = jax.ShapeDtypeStruct((count, 4 * MARGIN, 2 * BS), BF16)
    outs = [jax.ShapeDtypeStruct(before.shape, F32), kept, kept]
    return pl.pallas_call(
        functools.partial(lesser_kernel, places, held),
        out_shape=outs,
        in_specs=[vmem] * (3 + len(shards)) + [pl.BlockSpec(memory_space=pl.ANY)] * len(after),
        out_specs=[vmem] * len(outs),
        input_output_aliases={2: 0},
        compiler_params=pltpu.CompilerParams(vmem_limit_bytes=26 << 20),
        cost_estimate=pl.CostEstimate(
            flops=count * 3 * hi.shape[0] * 2 * BS * (2 * BS + 4 * TILE),
            bytes_accessed=8 * before.size,
            transcendentals=0,
        ),
        name="lesser_more",
    )(hi, lo, before, *shards, *after)


def rows_kernel(count, green_ref, *rest):
    outs, sem = rest[-1 - count : -1], rest[-1]
    z, rows = lax.axis_index("orb"), green_ref.shape[2]
    starts = [rows - HALF, 0, jnp.where(z == 0, rows - MARGIN, HALF)]
    copies = [
        pltpu.make_async_copy(
            green_ref.at[0, :, pl.ds(pl.multiple_of(starts[n], HALF), HALF), :],
            out,
            sem.at[n],
        )
        for n, out in enumerate(outs)
    ]
    for copy in copies:
        copy.start()
    for copy in copies:
        copy.wait()


def rows_at(green, count):
    out = jax.ShapeDtypeStruct((2, HALF, green.shape[3]), F32)
    return pl.pallas_call(
        functools.partial(rows_kernel, count),
        out_shape=[out] * count,
        in_specs=[pl.BlockSpec(memory_space=pl.ANY)],
        out_specs=[pl.BlockSpec(memory_space=pltpu.VMEM)] * count,
        scratch_shapes=[pltpu.SemaphoreType.DMA((count,))],
        compiler_params=pltpu.CompilerParams(vmem_limit_bytes=8 << 20),
        name="rows",
    )(green)


def gate_kernel(*refs):
    del refs


def gate(right, left, after):
    hbm = pl.BlockSpec(memory_space=pl.ANY)
    return pl.pallas_call(
        gate_kernel,
        out_shape=[jax.ShapeDtypeStruct(x.shape, x.dtype) for x in (right, left)],
        in_specs=[hbm] * 3,
        out_specs=[hbm] * 2,
        input_output_aliases={0: 0, 1: 1},
        compiler_params=pltpu.CompilerParams(vmem_limit_bytes=1 << 20),
        cost_estimate=pl.CostEstimate(flops=0, bytes_accessed=0, transcendentals=0),
        name="gate",
    )(right, left, after)


def edge_kernel(places, held, a_ref, b_ref, c_ref, *refs):
    keeps = refs[: 2 * len(places)]
    left_ref, right_ref, own_ref, acc_ref = refs[2 * len(places) :]
    z, peers = lax.axis_index("orb"), lax.axis_size("orb")
    if is_far(peers):
        from_left, from_right = z == 1, z == peers - 2
    else:
        from_left = from_right = z < 0
    limit = jnp.where(from_right, MARGIN, HALF)
    acc_ref[...] = jnp.zeros_like(acc_ref)

    def add(number, hi, lo, at):
        cols = pl.ds(pl.multiple_of(number * held * BS, BS), held * BS)
        for side in range(2):
            fields = []
            for part in range(2):
                outer = jnp.where(
                    from_left if side == 0 else from_right, a_ref[part, :, cols], 0.0
                )
                inner = (b_ref if side == 0 else c_ref)[part, :, cols]
                rows = [outer, inner] if side == 0 else [inner, outer]
                fields.append(halves(jnp.concatenate(rows, axis=0)))
            halo = []
            for real, imag in zip(*fields):
                lanes = []
                for s in range(held):
                    one = slice(s * BS, (s + 1) * BS)
                    lanes += [
                        jnp.concatenate([real[:, one], -imag[:, one]], axis=0),
                        jnp.concatenate([imag[:, one], real[:, one]], axis=0),
                    ]
                halo.append(jnp.concatenate(lanes, axis=1))
            rows = slice(side * TILE, (side + 1) * TILE)
            kept = [
                jnp.concatenate([ref[at + s, rows, :] for s in range(held)], axis=1)
                for ref in (hi, lo)
            ]
            acc_ref[side] = acc_ref[side] + dot3(halo, kept, NT)

    @pl.when(is_inner())
    def _():
        for k, shards in enumerate(places):
            for n, distance in enumerate(shards):
                number, valid = neighbour(distance)

                @pl.when(valid)
                def _():
                    add(number, keeps[2 * k], keeps[2 * k + 1], n * held)

    lane = lax.broadcasted_iota(jnp.int32, (MARGIN, LANES), 1)
    row = lax.broadcasted_iota(jnp.int32, (MARGIN, LANES), 0)
    low = lane < MARGIN
    left, right = acc_ref[0], acc_ref[1]
    turned_left, turned_right = left.T[:MARGIN], right.T[MARGIN:]
    left_ref[0] = jnp.where(low, 0.0, left[:MARGIN])
    left_ref[1] = jnp.where(low, 0.0, -left[MARGIN:])
    right_ref[0] = jnp.where(lane < limit, right[:MARGIN], 0.0)
    right_ref[1] = jnp.where(lane < limit, -right[MARGIN:], 0.0)
    own_ref[0, 0] = jnp.where(low, turned_left, 0.0)
    own_ref[0, 1] = jnp.where(low, pltpu.roll(turned_left, MARGIN, 1), 0.0)
    mine = jnp.logical_and(row < limit, lane >= MARGIN)
    own_ref[1, 0] = jnp.where(mine, pltpu.roll(turned_right, MARGIN, 1), 0.0)
    own_ref[1, 1] = jnp.where(mine, turned_right, 0.0)


def edge_part(halos, keeps, places, held):
    vmem = pl.BlockSpec(memory_space=pltpu.VMEM)
    side = jax.ShapeDtypeStruct((2, MARGIN, LANES), F32)
    return pl.pallas_call(
        functools.partial(edge_kernel, places, held),
        out_shape=(side, side, jax.ShapeDtypeStruct((2, 2, MARGIN, LANES), F32)),
        in_specs=[vmem] * (len(halos) + len(keeps)),
        out_specs=(vmem, vmem, vmem),
        scratch_shapes=[pltpu.VMEM((2, TILE, TILE), F32)],
        compiler_params=pltpu.CompilerParams(vmem_limit_bytes=20 << 20),
        cost_estimate=pl.CostEstimate(
            flops=1 << 31, bytes_accessed=8 << 20, transcendentals=0
        ),
        name="edges",
    )(*halos, *keeps)


def band_kernel(acc_ref, own_ref, from_left_ref, from_right_ref, out_ref, rows_ref):
    tiles = acc_ref.shape[0]
    group = out_ref.shape[2]
    per_tile = TILE // W
    for t in range(tiles):
        for part in range(2):
            base = part * TILE
            x = acc_ref[t, base : base + TILE, :]
            rows_ref[t, part] = x
            if t == 0:
                extra = own_ref[0, part] + from_left_ref[part]
                rows_ref[t, part, :MARGIN, :LANES] = x[:MARGIN, :LANES] + extra
            if t == tiles - 1:
                extra = own_ref[1, part] + from_right_ref[part]
                rows_ref[t, part, MARGIN:, LANES:] = x[MARGIN:, LANES:] + extra
    low = lax.broadcasted_iota(jnp.int32, (W, LANES), 1) < MARGIN
    width = TILE + 2 * MARGIN
    for a in range(per_tile):
        for t in range(tiles):
            atom = t * per_tile + a
            for part in range(2):
                x = rows_ref[t, part, a * W : (a + 1) * W, :]
                before = pltpu.roll(x, (width - a * W) % width, 1)[:, :LANES]
                after = pltpu.roll(x, (width - (a + 1) * W) % width, 1)[:, :LANES]
                out_ref[atom // group, part, atom % group] = jnp.where(low, before, after)


def band(acc, own, from_left, from_right, energies):
    tiles = acc.shape[0]
    atoms = tiles * TILE // W
    vmem = pl.BlockSpec(memory_space=pltpu.VMEM)
    return pl.pallas_call(
        band_kernel,
        out_shape=jax.ShapeDtypeStruct((energies, 2, atoms // energies, W, LANES), F32),
        in_specs=[vmem] * 4,
        out_specs=vmem,
        scratch_shapes=[pltpu.VMEM((tiles, 2, TILE, TILE + 2 * MARGIN), F32)],
        compiler_params=pltpu.CompilerParams(vmem_limit_bytes=16 << 20),
        name="band",
    )(acc, own, from_left, from_right)


def scatter_kernel(recv_ref, where_ref, mix_ref, dham_ref, out_ref, smeared_ref, result_ref):
    energies, _, group, _, _ = recv_ref.shape
    padded = dham_ref.shape[1]
    pairs = out_ref.shape[1]
    columns = [
        recv_ref[:, :, a, :, :].reshape(energies * 2 * W, LANES) for a in range(group)
    ]
    received = halves(jnp.concatenate(columns, axis=1))
    mixed = halves(dot3(halves(mix_ref[...]), received, NN))
    entry = lax.broadcasted_iota(jnp.int32, (group * LANES, padded), 0)
    first = where_ref[...] * W
    for j in range(W):
        pick = jnp.where(entry == first + j, 1.0, 0.0).astype(BF16)
        smeared_ref[:, j * padded : (j + 1) * padded] = dot(mixed[0], pick, NN) + dot(
            mixed[1], pick, NN
        )

    def block(part, j, k):
        row = (part * W + j) * energies
        return smeared_ref[row : row + energies, k * padded : (k + 1) * padded]

    def factor(c, i, j):
        row = (c * W + i) * W + j
        return dham_ref[row : row + 1, :]

    for part in range(2):
        for i in range(W):
            total = [None] * W
            for c in range(3):
                for k in range(W):
                    t = None
                    for j in range(W):
                        term = factor(c, i, j) * block(part, j, k)
                        t = term if t is None else t + term
                    for l in range(W):
                        term = t * factor(c, l, k)
                        total[l] = term if total[l] is None else total[l] + term
            for l in range(W):
                row = ((part * W + i) * W + l) * energies
                result_ref[row : row + energies, :] = total[l]
    for e in range(energies):
        one = result_ref[pl.ds(e, 2 * W * W, stride=energies), :]
        out_ref[e] = one.T[:pairs, :]


def scatter(recv, where, mix, dham, pairs):
    energies, _, group, _, _ = recv.shape
    padded = dham.shape[1]
    vmem = pl.BlockSpec(memory_space=pltpu.VMEM)
    return pl.pallas_call(
        scatter_kernel,
        out_shape=jax.ShapeDtypeStruct((energies, pairs, 2 * W * W), F32),
        in_specs=[vmem] * 4,
        out_specs=vmem,
        scratch_shapes=[
            pltpu.VMEM((2 * W * energies, W * padded), F32),
            pltpu.VMEM((2 * W * W * energies, padded), F32),
        ],
        compiler_params=pltpu.CompilerParams(vmem_limit_bytes=24 << 20),
        name="scatter",
    )(recv, where, mix, dham)


def build_kernel(phonon_shift, phonon_weight, energies):
    rows_e = jnp.arange(energies, dtype=jnp.int32)[None, :, None]
    cols_f = jnp.arange(energies, dtype=jnp.int32)[None, None, :]
    shifts = phonon_shift[:, None, None]
    emission = (cols_f == rows_e + shifts).astype(F32)
    absorption = (cols_f == rows_e - shifts).astype(F32)
    terms = (
        phonon_weight[0][:, None, None] * emission + phonon_weight[1][:, None, None] * absorption
    )
    return jnp.sum(terms, axis=0)


def build_mix(phonon_shift, phonon_weight, energies):
    kernel = build_kernel(phonon_shift, phonon_weight, energies)
    same = jnp.eye(2 * W, dtype=F32)
    mix = same[:, None, None, :] * kernel[None, :, :, None]
    return mix.reshape(2 * W * energies, energies * 2 * W)


def send(x, pairs):
    return lax.ppermute(x, "orb", pairs)


def per_device(green, sigma, neighbours, phonon_shift, phonon_weight, dham):
    energies = lax.axis_size("energy")
    peers = lax.axis_size("orb")
    e, z = lax.axis_index("energy"), lax.axis_index("orb")
    rows = green.shape[2]
    atoms = rows // W
    degree = neighbours.shape[1]
    group = atoms // energies
    pairs = group * degree
    padded = -(-pairs // LANES) * LANES
    held = sigma.shape[1]

    far = is_far(peers)
    up = [(i, i + 1) for i in range(peers - 1)]
    down = [(i + 1, i) for i in range(peers - 1)]
    fixed = pltpu.with_memory_space_constraint(green, pltpu.HBM)
    right, left = send(sigma, up), send(sigma, down)
    last, leading, *outer = rows_at(fixed, 3 if far else 2)
    near_right = send(last, up[:-1] if far else up)
    near_left = send(leading, down[1:] if far else down)
    if far:
        other = send(outer[0], [(0, 1), (peers - 1, peers - 2)])
    else:
        other = jnp.zeros_like(near_left)

    mine = lax.dynamic_slice_in_dim(neighbours, e * group, group, axis=0)
    first = z * atoms + e * group
    offset = mine - (first + jnp.arange(group, dtype=jnp.int32))[:, None]
    column = jnp.where(offset < 0, offset + REACH, offset + REACH - 1)
    where = column + 2 * REACH * jnp.arange(group, dtype=jnp.int32)[:, None]
    where = jnp.pad(where.reshape(1, pairs), ((0, 0), (0, padded - pairs)), constant_values=-1)
    mix = build_mix(phonon_shift, phonon_weight, energies)
    factors = lax.dynamic_slice_in_dim(
        dham.transpose(1, 2, 3, 0).reshape(3 * W * W, -1), e * pairs, pairs, axis=1
    )
    factors = jnp.pad(factors, ((0, 0), (0, padded - pairs)))


    acc, *keeps, hi, lo = own_part(
        fixed, pltpu.with_memory_space_constraint(sigma, pltpu.HBM), [where, mix, factors, last]
    )
    places = [[0]]
    for k in range(1, peers):
        if k < peers - 1:
            right, left = gate(right, left, keeps[-1])
            following = send(right, up[k:]), send(left, down[: peers - 1 - k])
            after = []
        else:
            if not far:
                acc, *kept = lesser_part(hi, lo, acc, [right, left], [-k, k], held)
                keeps += kept
                places.append([-k, k])
            to_left, to_right, own = edge_part(
                [other, near_right, near_left], keeps, places, held
            )
            back_right, back_left = send(to_left, down), send(to_right, up)
            after = [to_left]
            if not far:
                break
        acc, *kept = lesser_part(hi, lo, acc, [right, left], [-k, k], held, after)
        keeps += kept
        places.append([-k, k])
        if k < peers - 1:
            right, left = following
    lesser = band(acc, own, back_left, back_right, energies)

    recv = lax.all_to_all(lesser, "energy", split_axis=0, concat_axis=0, tiled=True)
    spread = scatter(recv, where, mix, factors, pairs)
    result = lax.all_to_all(spread, "energy", split_axis=0, concat_axis=0, tiled=True)
    return result.reshape(1, atoms * degree, 2 * W * W)


def solution(mesh):
    return jax.shard_map(
        per_device,
        mesh=mesh,
        in_specs=(
            P("energy", None, "orb", None),
            P("energy", "orb", None, None, None),
            P("orb", None),
            P(),
            P(),
            P("orb", None, None, None),
        ),
        out_specs=P("energy", "orb", None),
        check_vma=False,
    )
```

```python
import functools

import jax
import jax.numpy as jnp
from jax import lax
from jax.experimental import pallas as pl
from jax.experimental.pallas import tpu as pltpu
from jax.sharding import PartitionSpec as P

W = 8
BS = 128
REACH = 8
MARGIN = REACH * W
HALF = MARGIN // 2
TILE = 128
LANES = 128
F32, BF16 = jnp.float32, jnp.bfloat16

NT = (((1,), (1,)), ((), ()))
NN = (((1,), (0,)), ((), ()))


def halves(x):
    hi = x.astype(BF16)
    return hi, (x - hi.astype(F32)).astype(BF16)


def dot(a, b, dims):
    return lax.dot_general(a, b, dims, preferred_element_type=F32)


def dot3(a, b, dims):
    left = jnp.concatenate([a[0], a[0], a[1]], axis=1)
    right = jnp.concatenate([b[0], b[1], b[0]], axis=dims[0][1][0])
    return dot(left, right, dims)


def blocks_at_once(held):
    return 2 if held % 2 == 0 else 1


def some_blocks(lane, weights, hi_ref, lo_ref, acc_ref, edges, active):
    rows = hi_ref.shape[0] - 2 * MARGIN
    wide = 2 * BS
    split, products = [], []
    for n, (real, imag) in enumerate(weights):
        top = jnp.concatenate([real, imag], axis=1)
        weight = halves(jnp.concatenate([top, jnp.concatenate([-imag, real], axis=1)], axis=0))
        cols = pl.ds(lane + n * wide, wide)
        own = [ref[MARGIN : MARGIN + rows, cols] for ref in (hi_ref, lo_ref)]
        product = halves(dot3(own, weight, NN))
        for ref, part in zip(edges, product):
            ref[n, :MARGIN, :] = part[:MARGIN]
            ref[n, 3 * MARGIN :, :] = part[rows - MARGIN :]
        split.append(weight)
        products.append(product)
    cols = pl.ds(lane, len(weights) * wide)
    for t in range(rows // TILE):
        both = []
        for part in zip(*products):
            lanes = []
            for x in part:
                x = x[t * TILE : (t + 1) * TILE]
                turned = jnp.concatenate([x[:, BS:], -x[:, :BS]], axis=1)
                lanes.append(jnp.concatenate([x, turned], axis=0))
            both.append(jnp.concatenate(lanes, axis=1))
        near = pl.ds(t * TILE, TILE + 2 * MARGIN)
        acc_ref[t] = acc_ref[t] + dot3(both, (hi_ref[near, cols], lo_ref[near, cols]), NT)

    if not edges:
        return

    @pl.when(active)
    def _():
        for n, weight in enumerate(split):
            one = pl.ds(lane + n * wide, wide)
            outer = [
                jnp.concatenate(
                    [ref[MARGIN : 2 * MARGIN, one], ref[rows : rows + MARGIN, one]], axis=0
                )
                for ref in (hi_ref, lo_ref)
            ]
            for ref, part in zip(edges, halves(dot3(outer, weight, NT))):
                ref[n, MARGIN : 3 * MARGIN, :] = part


def shard_loop(first_block, self_ref, hi_ref, lo_ref, acc_ref, keeps, slot, active):
    held = self_ref.shape[1]
    once = blocks_at_once(held)

    def step(g, carry):
        lane = pl.multiple_of((first_block + g * once) * 2 * BS, 2 * BS)
        weights = [
            (self_ref[0, g * once + n, 0], self_ref[0, g * once + n, 1]) for n in range(once)
        ]
        slots = pl.ds(slot + g * once, once)
        kept = tuple(ref.at[slots] for ref in keeps)
        some_blocks(lane, weights, hi_ref, lo_ref, acc_ref, kept, active)
        return carry

    lax.fori_loop(0, held // once, step, 0)


def is_far(peers):
    return peers >= 4


def is_inner():
    z, peers = lax.axis_index("orb"), lax.axis_size("orb")
    if is_far(peers):
        return jnp.logical_and(z > 0, z < peers - 1)
    return z >= 0


def neighbour(distance):
    z, peers = lax.axis_index("orb"), lax.axis_size("orb")
    number = z + distance
    return jnp.clip(number, 0, peers - 1), jnp.logical_and(number >= 0, number < peers)


def own_kernel(
    green_ref, sigma_ref, *rest
):
    acc_ref, keep_hi_ref, keep_lo_ref, hi_ref, lo_ref, buf, self_ref, sem = rest[-8:]
    rows, held = green_ref.shape[2], sigma_ref.shape[1]
    blocks = green_ref.shape[3] // BS
    begin, active = lax.axis_index("orb") * held, is_inner()

    def block_of(s):
        return lax.rem(begin + s, blocks)

    def fetch(s):
        col = pl.multiple_of(block_of(s) * BS, BS)
        return pltpu.make_async_copy(
            green_ref.at[0, :, :, pl.ds(col, BS)], buf.at[s], sem.at[s]
        )

    def store(s, carry):
        fetch(s).wait()
        lanes = pl.ds(pl.multiple_of(block_of(s) * 2 * BS, 2 * BS), 2 * BS)
        parts = halves(jnp.concatenate([buf[s, 0], buf[s, 1]], axis=1))
        for ref, part in zip((hi_ref, lo_ref), parts):
            ref[MARGIN : MARGIN + rows, lanes] = part
        return carry

    load = pltpu.make_async_copy(sigma_ref, self_ref, sem.at[blocks])
    load.start()
    for s in range(blocks):
        fetch(s).start()
    acc_ref[...] = jnp.zeros_like(acc_ref)
    for ref in (hi_ref, lo_ref):
        ref[:MARGIN, :] = jnp.zeros((MARGIN, ref.shape[1]), BF16)
        ref[MARGIN + rows :, :] = jnp.zeros((MARGIN, ref.shape[1]), BF16)
    lax.fori_loop(0, held, store, 0)
    load.wait()
    shard_loop(begin, self_ref, hi_ref, lo_ref, acc_ref, (keep_hi_ref, keep_lo_ref), 0, active)
    lax.fori_loop(held, blocks, store, 0)


def own_part(green, sigma, after):
    rows, held = green.shape[2], sigma.shape[1]
    tiles, blocks = rows // TILE, green.shape[3] // BS
    vmem = pl.BlockSpec(memory_space=pltpu.VMEM)
    hbm = pl.BlockSpec(memory_space=pl.ANY)
    keep = jax.ShapeDtypeStruct((held, 4 * MARGIN, 2 * BS), BF16)
    whole = jax.ShapeDtypeStruct((rows + 2 * MARGIN, blocks * 2 * BS), BF16)
    return pl.pallas_call(
        own_kernel,
        out_shape=(
            jax.ShapeDtypeStruct((tiles, 2 * TILE, TILE + 2 * MARGIN), F32),
            keep,
            keep,
            whole,
            whole,
        ),
        in_specs=[hbm] * (2 + len(after)),
        out_specs=(vmem,) * 5,
        scratch_shapes=[
            pltpu.VMEM((blocks, 2, rows, BS), F32),
            pltpu.VMEM(sigma.shape, F32),
            pltpu.SemaphoreType.DMA((blocks + 1,)),
        ],
        compiler_params=pltpu.CompilerParams(vmem_limit_bytes=40 << 20),
        cost_estimate=pl.CostEstimate(
            flops=held * rows * BS * BS,
            bytes_accessed=blocks * rows * BS,
            transcendentals=0,
        ),
        name="lesser_own",
    )(green, sigma, *after)


def lesser_kernel(places, held, extra, hi_ref, lo_ref, before_ref, *rest):
    sigmas, rest = rest[: len(places)], rest[len(places) :]
    rest = rest[extra:]
    acc_ref, keeps = rest[0], rest[1:]
    acc_ref[...] = before_ref[...]
    slot = 0
    for distance, self_ref in zip(places, sigmas):
        number, valid = neighbour(distance)

        @pl.when(valid)
        def _():
            shard_loop(
                number * held, self_ref, hi_ref, lo_ref, acc_ref, keeps, slot, is_inner()
            )

        slot += self_ref.shape[1]


def lesser_part(hi, lo, before, shards, places, held, after=(), keep=True):
    vmem = pl.BlockSpec(memory_space=pltpu.VMEM)
    count = sum(x.shape[1] for x in shards)
    kept = jax.ShapeDtypeStruct((count, 4 * MARGIN, 2 * BS), BF16)
    outs = [jax.ShapeDtypeStruct(before.shape, F32)] + ([kept, kept] if keep else [])
    return pl.pallas_call(
        functools.partial(lesser_kernel, places, held, len(after)),
        out_shape=outs,
        in_specs=[vmem] * (3 + len(shards)) + [pl.BlockSpec(memory_space=pl.ANY)] * len(after),
        out_specs=[vmem] * len(outs),
        input_output_aliases={2: 0},
        compiler_params=pltpu.CompilerParams(vmem_limit_bytes=26 << 20),
        cost_estimate=pl.CostEstimate(
            flops=count * hi.shape[0] * BS * BS,
            bytes_accessed=before.size,
            transcendentals=0,
        ),
        name="lesser_more",
    )(hi, lo, before, *shards, *after)


def rows_kernel(near, green_ref, *rest):
    count = 2 if near else 1
    outs, sem = rest[-1 - count : -1], rest[-1]
    z, rows = lax.axis_index("orb"), green_ref.shape[2]
    starts = [rows - HALF, 0] if near else [jnp.where(z == 0, rows - MARGIN, HALF)]
    copies = [
        pltpu.make_async_copy(
            green_ref.at[0, :, pl.ds(pl.multiple_of(starts[n], HALF), HALF), :],
            out,
            sem.at[n],
        )
        for n, out in enumerate(outs)
    ]
    for copy in copies:
        copy.start()
    for copy in copies:
        copy.wait()


def rows_at(green, near, after=()):
    count = 2 if near else 1
    out = jax.ShapeDtypeStruct((2, HALF, green.shape[3]), F32)
    return pl.pallas_call(
        functools.partial(rows_kernel, near),
        out_shape=[out] * count,
        in_specs=[pl.BlockSpec(memory_space=pl.ANY)] * (1 + len(after)),
        out_specs=[pl.BlockSpec(memory_space=pltpu.VMEM)] * count,
        scratch_shapes=[pltpu.SemaphoreType.DMA((count,))],
        compiler_params=pltpu.CompilerParams(vmem_limit_bytes=8 << 20),
        name="rows",
    )(green, *after)


def gate_kernel(*refs):
    del refs


def gate(right, left, *after):
    hbm = pl.BlockSpec(memory_space=pl.ANY)
    return pl.pallas_call(
        gate_kernel,
        out_shape=[jax.ShapeDtypeStruct(x.shape, x.dtype) for x in (right, left)],
        in_specs=[hbm] * (2 + len(after)),
        out_specs=[hbm] * 2,
        input_output_aliases={0: 0, 1: 1},
        compiler_params=pltpu.CompilerParams(vmem_limit_bytes=1 << 20),
        cost_estimate=pl.CostEstimate(flops=0, bytes_accessed=0, transcendentals=0),
        name="gate",
    )(right, left, *after)


def edge_kernel(places, held, a_ref, b_ref, c_ref, *refs):
    keeps = refs[: 2 * len(places)]
    left_ref, right_ref, own_ref, acc_ref = refs[2 * len(places) :]
    z, peers = lax.axis_index("orb"), lax.axis_size("orb")
    if is_far(peers):
        from_left, from_right = z == 1, z == peers - 2
    else:
        from_left = from_right = z < 0
    limit = jnp.where(from_right, MARGIN, HALF)
    acc_ref[...] = jnp.zeros_like(acc_ref)

    def add(number, hi, lo, at):
        cols = pl.ds(pl.multiple_of(number * held * BS, BS), held * BS)
        for side in range(2):
            fields = []
            for part in range(2):
                outer = jnp.where(
                    from_left if side == 0 else from_right, a_ref[part, :, cols], 0.0
                )
                inner = (b_ref if side == 0 else c_ref)[part, :, cols]
                rows = [outer, inner] if side == 0 else [inner, outer]
                fields.append(halves(jnp.concatenate(rows, axis=0)))
            halo = []
            for real, imag in zip(*fields):
                lanes = []
                for s in range(held):
                    one = slice(s * BS, (s + 1) * BS)
                    lanes += [
                        jnp.concatenate([real[:, one], -imag[:, one]], axis=0),
                        jnp.concatenate([imag[:, one], real[:, one]], axis=0),
                    ]
                halo.append(jnp.concatenate(lanes, axis=1))
            rows = slice(side * TILE, (side + 1) * TILE)
            kept = [
                jnp.concatenate([ref[at + s, rows, :] for s in range(held)], axis=1)
                for ref in (hi, lo)
            ]
            acc_ref[side] = acc_ref[side] + dot3(halo, kept, NT)

    @pl.when(is_inner())
    def _():
        for k, shards in enumerate(places):
            for n, distance in enumerate(shards):
                number, valid = neighbour(distance)

                @pl.when(valid)
                def _():
                    add(number, keeps[2 * k], keeps[2 * k + 1], n * held)

    lane = lax.broadcasted_iota(jnp.int32, (MARGIN, LANES), 1)
    row = lax.broadcasted_iota(jnp.int32, (MARGIN, LANES), 0)
    low = lane < MARGIN
    left, right = acc_ref[0], acc_ref[1]
    turned_left, turned_right = left.T[:MARGIN], right.T[MARGIN:]
    left_ref[0] = jnp.where(low, 0.0, left[:MARGIN])
    left_ref[1] = jnp.where(low, 0.0, -left[MARGIN:])
    right_ref[0] = jnp.where(lane < limit, right[:MARGIN], 0.0)
    right_ref[1] = jnp.where(lane < limit, -right[MARGIN:], 0.0)
    own_ref[0, 0] = jnp.where(low, turned_left, 0.0)
    own_ref[0, 1] = jnp.where(low, pltpu.roll(turned_left, MARGIN, 1), 0.0)
    mine = jnp.logical_and(row < limit, lane >= MARGIN)
    own_ref[1, 0] = jnp.where(mine, pltpu.roll(turned_right, MARGIN, 1), 0.0)
    own_ref[1, 1] = jnp.where(mine, turned_right, 0.0)


def edge_part(halos, keeps, places, held):
    vmem = pl.BlockSpec(memory_space=pltpu.VMEM)
    side = jax.ShapeDtypeStruct((2, MARGIN, LANES), F32)
    return pl.pallas_call(
        functools.partial(edge_kernel, places, held),
        out_shape=(side, side, jax.ShapeDtypeStruct((2, 2, MARGIN, LANES), F32)),
        in_specs=[vmem] * (len(halos) + len(keeps)),
        out_specs=(vmem, vmem, vmem),
        scratch_shapes=[pltpu.VMEM((2, TILE, TILE), F32)],
        compiler_params=pltpu.CompilerParams(vmem_limit_bytes=20 << 20),
        cost_estimate=pl.CostEstimate(
            flops=1 << 31, bytes_accessed=8 << 20, transcendentals=0
        ),
        name="edges",
    )(*halos, *keeps)


def band_kernel(acc_ref, own_ref, from_left_ref, from_right_ref, out_ref, rows_ref):
    tiles = acc_ref.shape[0]
    group = out_ref.shape[2]
    per_tile = TILE // W
    for t in range(tiles):
        for part in range(2):
            base = part * TILE
            x = acc_ref[t, base : base + TILE, :]
            rows_ref[t, part] = x
            if t == 0:
                extra = own_ref[0, part] + from_left_ref[part]
                rows_ref[t, part, :MARGIN, :LANES] = x[:MARGIN, :LANES] + extra
            if t == tiles - 1:
                extra = own_ref[1, part] + from_right_ref[part]
                rows_ref[t, part, MARGIN:, LANES:] = x[MARGIN:, LANES:] + extra
    low = lax.broadcasted_iota(jnp.int32, (W, LANES), 1) < MARGIN
    width = TILE + 2 * MARGIN
    for a in range(per_tile):
        for t in range(tiles):
            atom = t * per_tile + a
            for part in range(2):
                x = rows_ref[t, part, a * W : (a + 1) * W, :]
                before = pltpu.roll(x, (width - a * W) % width, 1)[:, :LANES]
                after = pltpu.roll(x, (width - (a + 1) * W) % width, 1)[:, :LANES]
                out_ref[atom // group, part, atom % group] = jnp.where(low, before, after)


def band(acc, own, from_left, from_right, energies):
    tiles = acc.shape[0]
    atoms = tiles * TILE // W
    vmem = pl.BlockSpec(memory_space=pltpu.VMEM)
    return pl.pallas_call(
        band_kernel,
        out_shape=jax.ShapeDtypeStruct((energies, 2, atoms // energies, W, LANES), F32),
        in_specs=[vmem] * 4,
        out_specs=vmem,
        scratch_shapes=[pltpu.VMEM((tiles, 2, TILE, TILE + 2 * MARGIN), F32)],
        compiler_params=pltpu.CompilerParams(vmem_limit_bytes=16 << 20),
        name="band",
    )(acc, own, from_left, from_right)


def scatter_kernel(recv_ref, where_ref, mix_ref, dham_ref, out_ref, smeared_ref, result_ref):
    energies, _, group, _, _ = recv_ref.shape
    padded = dham_ref.shape[1]
    pairs = out_ref.shape[1]
    columns = [
        recv_ref[:, :, a, :, :].reshape(energies * 2 * W, LANES) for a in range(group)
    ]
    received = halves(jnp.concatenate(columns, axis=1))
    mixed = halves(dot3(halves(mix_ref[...]), received, NN))
    entry = lax.broadcasted_iota(jnp.int32, (group * LANES, padded), 0)
    first = where_ref[...] * W
    for j in range(W):
        pick = jnp.where(entry == first + j, 1.0, 0.0).astype(BF16)
        smeared_ref[:, j * padded : (j + 1) * padded] = dot(mixed[0], pick, NN) + dot(
            mixed[1], pick, NN
        )

    def block(part, j, k):
        row = (part * W + j) * energies
        return smeared_ref[row : row + energies, k * padded : (k + 1) * padded]

    def factor(c, i, j):
        row = (c * W + i) * W + j
        return dham_ref[row : row + 1, :]

    for part in range(2):
        for i in range(W):
            total = [None] * W
            for c in range(3):
                for k in range(W):
                    t = None
                    for j in range(W):
                        term = factor(c, i, j) * block(part, j, k)
                        t = term if t is None else t + term
                    for l in range(W):
                        term = t * factor(c, l, k)
                        total[l] = term if total[l] is None else total[l] + term
            for l in range(W):
                row = ((part * W + i) * W + l) * energies
                result_ref[row : row + energies, :] = total[l]
    for e in range(energies):
        one = result_ref[pl.ds(e, 2 * W * W, stride=energies), :]
        out_ref[e] = one.T[:pairs, :]


def scatter(recv, where, mix, dham, pairs):
    energies, _, group, _, _ = recv.shape
    padded = dham.shape[1]
    vmem = pl.BlockSpec(memory_space=pltpu.VMEM)
    return pl.pallas_call(
        scatter_kernel,
        out_shape=jax.ShapeDtypeStruct((energies, pairs, 2 * W * W), F32),
        in_specs=[vmem] * 4,
        out_specs=vmem,
        scratch_shapes=[
            pltpu.VMEM((2 * W * energies, W * padded), F32),
            pltpu.VMEM((2 * W * W * energies, padded), F32),
        ],
        compiler_params=pltpu.CompilerParams(vmem_limit_bytes=24 << 20),
        name="scatter",
    )(recv, where, mix, dham)


def build_kernel(phonon_shift, phonon_weight, energies):
    rows_e = jnp.arange(energies, dtype=jnp.int32)[None, :, None]
    cols_f = jnp.arange(energies, dtype=jnp.int32)[None, None, :]
    shifts = phonon_shift[:, None, None]
    emission = (cols_f == rows_e + shifts).astype(F32)
    absorption = (cols_f == rows_e - shifts).astype(F32)
    terms = (
        phonon_weight[0][:, None, None] * emission + phonon_weight[1][:, None, None] * absorption
    )
    return jnp.sum(terms, axis=0)


def build_mix(phonon_shift, phonon_weight, energies):
    kernel = build_kernel(phonon_shift, phonon_weight, energies)
    same = jnp.eye(2 * W, dtype=F32)
    mix = same[:, None, None, :] * kernel[None, :, :, None]
    return mix.reshape(2 * W * energies, energies * 2 * W)


def send(x, pairs):
    return lax.ppermute(x, "orb", pairs)


def per_device(green, sigma, neighbours, phonon_shift, phonon_weight, dham):
    energies = lax.axis_size("energy")
    peers = lax.axis_size("orb")
    e, z = lax.axis_index("energy"), lax.axis_index("orb")
    rows = green.shape[2]
    atoms = rows // W
    degree = neighbours.shape[1]
    group = atoms // energies
    pairs = group * degree
    padded = -(-pairs // LANES) * LANES
    held = sigma.shape[1]

    far = is_far(peers)
    up = [(i, i + 1) for i in range(peers - 1)]
    down = [(i + 1, i) for i in range(peers - 1)]
    fixed = pltpu.with_memory_space_constraint(green, pltpu.HBM)
    right, left = send(sigma, up), send(sigma, down)
    last, leading = rows_at(fixed, True)
    near_right = send(last, up[:-1] if far else up)
    near_left = send(leading, down[1:] if far else down)
    mine = lax.dynamic_slice_in_dim(neighbours, e * group, group, axis=0)
    first = z * atoms + e * group
    offset = mine - (first + jnp.arange(group, dtype=jnp.int32))[:, None]
    column = jnp.where(offset < 0, offset + REACH, offset + REACH - 1)
    where = column + 2 * REACH * jnp.arange(group, dtype=jnp.int32)[:, None]
    where = jnp.pad(where.reshape(1, pairs), ((0, 0), (0, padded - pairs)), constant_values=-1)
    mix = build_mix(phonon_shift, phonon_weight, energies)
    factors = lax.dynamic_slice_in_dim(
        dham.transpose(1, 2, 3, 0).reshape(3 * W * W, -1), e * pairs, pairs, axis=1
    )
    factors = jnp.pad(factors, ((0, 0), (0, padded - pairs)))


    acc, *keeps, hi, lo = own_part(
        fixed, pltpu.with_memory_space_constraint(sigma, pltpu.HBM), [where, mix, factors, last]
    )
    places = [[0]]
    if far:
        (outer,) = rows_at(fixed, False, [keeps[-1]])
        other = send(outer, [(0, 1), (peers - 1, peers - 2)])
    else:
        outer = other = jnp.zeros_like(near_left)
    for k in range(1, peers):
        if k < peers - 1:
            right, left = gate(right, left, keeps[-1], outer if k == 1 else other)
            following = send(right, up[k:]), send(left, down[: peers - 1 - k])
            after = []
        else:
            if not far:
                acc, *kept = lesser_part(hi, lo, acc, [right, left], [-k, k], held)
                keeps += kept
                places.append([-k, k])
            to_left, to_right, own = edge_part(
                [other, near_right, near_left], keeps, places, held
            )
            back_right = send(to_left, down[:-1] if far else down)
            back_left = send(to_right, up[1:] if far else up)
            after = [to_left]
            if not far:
                break
        acc, *kept = lesser_part(hi, lo, acc, [right, left], [-k, k], held, after, k < peers - 1)
        keeps += kept
        places.append([-k, k])
        if k < peers - 1:
            right, left = following
    lesser = band(acc, own, back_left, back_right, energies)

    recv = lax.all_to_all(lesser, "energy", split_axis=0, concat_axis=0, tiled=True)
    spread = scatter(recv, where, mix, factors, pairs)
    result = lax.all_to_all(spread, "energy", split_axis=0, concat_axis=0, tiled=True)
    return result.reshape(1, atoms * degree, 2 * W * W)


def solution(mesh):
    return jax.shard_map(
        per_device,
        mesh=mesh,
        in_specs=(
            P("energy", None, "orb", None),
            P("energy", "orb", None, None, None),
            P("orb", None),
            P(),
            P(),
            P("orb", None, None, None),
        ),
        out_specs=P("energy", "orb", None),
        check_vma=False,
    )
```

```python
import functools

import jax
import jax.numpy as jnp
from jax import lax
from jax.experimental import pallas as pl
from jax.experimental.pallas import tpu as pltpu
from jax.sharding import PartitionSpec as P

W = 8
BS = 128
REACH = 8
MARGIN = REACH * W
HALF = MARGIN // 2
TILE = 128
LANES = 128
F32, BF16 = jnp.float32, jnp.bfloat16

NT = (((1,), (1,)), ((), ()))
NN = (((1,), (0,)), ((), ()))


def halves(x):
    hi = x.astype(BF16)
    return hi, (x - hi.astype(F32)).astype(BF16)


def dot(a, b, dims):
    return lax.dot_general(a, b, dims, preferred_element_type=F32)


def dot3(a, b, dims):
    left = jnp.concatenate([a[0], a[0], a[1]], axis=1)
    right = jnp.concatenate([b[0], b[1], b[0]], axis=dims[0][1][0])
    return dot(left, right, dims)


def blocks_at_once(held):
    return 2 if held % 2 == 0 else 1


def some_blocks(lane, weights, hi_ref, lo_ref, acc_ref, edges, active):
    rows = hi_ref.shape[0] - 2 * MARGIN
    wide = 2 * BS
    split, products = [], []
    for n, (real, imag) in enumerate(weights):
        top = jnp.concatenate([real, imag], axis=1)
        weight = halves(jnp.concatenate([top, jnp.concatenate([-imag, real], axis=1)], axis=0))
        cols = pl.ds(lane + n * wide, wide)
        own = [ref[MARGIN : MARGIN + rows, cols] for ref in (hi_ref, lo_ref)]
        product = halves(dot3(own, weight, NN))
        for ref, part in zip(edges, product):
            ref[n, :MARGIN, :] = part[:MARGIN]
            ref[n, 3 * MARGIN :, :] = part[rows - MARGIN :]
        split.append(weight)
        products.append(product)
    cols = pl.ds(lane, len(weights) * wide)
    for t in range(rows // TILE):
        both = []
        for part in zip(*products):
            lanes = []
            for x in part:
                x = x[t * TILE : (t + 1) * TILE]
                turned = jnp.concatenate([x[:, BS:], -x[:, :BS]], axis=1)
                lanes.append(jnp.concatenate([x, turned], axis=0))
            both.append(jnp.concatenate(lanes, axis=1))
        near = pl.ds(t * TILE, TILE + 2 * MARGIN)
        acc_ref[t] = acc_ref[t] + dot3(both, (hi_ref[near, cols], lo_ref[near, cols]), NT)

    if not edges:
        return

    @pl.when(active)
    def _():
        for n, weight in enumerate(split):
            one = pl.ds(lane + n * wide, wide)
            outer = [
                jnp.concatenate(
                    [ref[MARGIN : 2 * MARGIN, one], ref[rows : rows + MARGIN, one]], axis=0
                )
                for ref in (hi_ref, lo_ref)
            ]
            for ref, part in zip(edges, halves(dot3(outer, weight, NT))):
                ref[n, MARGIN : 3 * MARGIN, :] = part


def shard_loop(first_block, self_ref, hi_ref, lo_ref, acc_ref, keeps, slot, active):
    held = self_ref.shape[1]
    once = blocks_at_once(held)

    def step(g, carry):
        lane = pl.multiple_of((first_block + g * once) * 2 * BS, 2 * BS)
        weights = [
            (self_ref[0, g * once + n, 0], self_ref[0, g * once + n, 1]) for n in range(once)
        ]
        slots = pl.ds(slot + g * once, once)
        kept = tuple(ref.at[slots] for ref in keeps)
        some_blocks(lane, weights, hi_ref, lo_ref, acc_ref, kept, active)
        return carry

    lax.fori_loop(0, held // once, step, 0)


def is_far(peers):
    return peers >= 4


def is_inner():
    z, peers = lax.axis_index("orb"), lax.axis_size("orb")
    if is_far(peers):
        return jnp.logical_and(z > 0, z < peers - 1)
    return z >= 0


def neighbour(distance):
    def place():
        z, peers = lax.axis_index("orb"), lax.axis_size("orb")
        number = z + distance
        return jnp.clip(number, 0, peers - 1), jnp.logical_and(number >= 0, number < peers)

    return place


def reflected(offset, inner):
    def place():
        z = lax.axis_index("orb")
        is_inner_one = jnp.logical_or(z == 1, z == 2)
        valid = z >= 0 if inner is None else is_inner_one == inner
        return lax.rem(offset + 4 - z, 4), valid

    return place


def beside():
    z = lax.axis_index("orb")
    return jnp.where(lax.rem(z, 2) == 0, z + 1, z - 1), z >= 0


def two_off(inner):
    def place():
        z = lax.axis_index("orb")
        return lax.rem(z + 2, 4), jnp.logical_or(z == 1, z == 2) == inner

    return place


def own_kernel(
    green_ref, sigma_ref, *rest
):
    acc_ref, keep_hi_ref, keep_lo_ref, hi_ref, lo_ref, buf, self_ref, sem = rest[-8:]
    rows, held = green_ref.shape[2], sigma_ref.shape[1]
    blocks = green_ref.shape[3] // BS
    begin, active = lax.axis_index("orb") * held, is_inner()

    def block_of(s):
        return lax.rem(begin + s, blocks)

    def fetch(s):
        col = pl.multiple_of(block_of(s) * BS, BS)
        return pltpu.make_async_copy(
            green_ref.at[0, :, :, pl.ds(col, BS)], buf.at[s], sem.at[s]
        )

    def store(s, carry):
        fetch(s).wait()
        lanes = pl.ds(pl.multiple_of(block_of(s) * 2 * BS, 2 * BS), 2 * BS)
        parts = halves(jnp.concatenate([buf[s, 0], buf[s, 1]], axis=1))
        for ref, part in zip((hi_ref, lo_ref), parts):
            ref[MARGIN : MARGIN + rows, lanes] = part
        return carry

    load = pltpu.make_async_copy(sigma_ref, self_ref, sem.at[blocks])
    load.start()
    for s in range(blocks):
        fetch(s).start()
    acc_ref[...] = jnp.zeros_like(acc_ref)
    for ref in (hi_ref, lo_ref):
        ref[:MARGIN, :] = jnp.zeros((MARGIN, ref.shape[1]), BF16)
        ref[MARGIN + rows :, :] = jnp.zeros((MARGIN, ref.shape[1]), BF16)
    lax.fori_loop(0, held, store, 0)
    load.wait()
    shard_loop(begin, self_ref, hi_ref, lo_ref, acc_ref, (keep_hi_ref, keep_lo_ref), 0, active)
    lax.fori_loop(held, blocks, store, 0)


def own_part(green, sigma, after):
    rows, held = green.shape[2], sigma.shape[1]
    tiles, blocks = rows // TILE, green.shape[3] // BS
    vmem = pl.BlockSpec(memory_space=pltpu.VMEM)
    hbm = pl.BlockSpec(memory_space=pl.ANY)
    keep = jax.ShapeDtypeStruct((held, 4 * MARGIN, 2 * BS), BF16)
    whole = jax.ShapeDtypeStruct((rows + 2 * MARGIN, blocks * 2 * BS), BF16)
    return pl.pallas_call(
        own_kernel,
        out_shape=(
            jax.ShapeDtypeStruct((tiles, 2 * TILE, TILE + 2 * MARGIN), F32),
            keep,
            keep,
            whole,
            whole,
        ),
        in_specs=[hbm] * (2 + len(after)),
        out_specs=(vmem,) * 5,
        scratch_shapes=[
            pltpu.VMEM((blocks, 2, rows, BS), F32),
            pltpu.VMEM(sigma.shape, F32),
            pltpu.SemaphoreType.DMA((blocks + 1,)),
        ],
        compiler_params=pltpu.CompilerParams(vmem_limit_bytes=40 << 20),
        cost_estimate=pl.CostEstimate(
            flops=held * rows * BS * BS,
            bytes_accessed=blocks * rows * BS,
            transcendentals=0,
        ),
        name="lesser_own",
    )(green, sigma, *after)


def lesser_kernel(places, held, extra, hi_ref, lo_ref, before_ref, *rest):
    sigmas, rest = rest[: len(places)], rest[len(places) :]
    rest = rest[extra:]
    acc_ref, keeps = rest[0], rest[1:]
    acc_ref[...] = before_ref[...]
    slot = 0
    for place, self_ref in zip(places, sigmas):
        number, valid = place()

        @pl.when(valid)
        def _():
            shard_loop(
                number * held, self_ref, hi_ref, lo_ref, acc_ref, keeps, slot, is_inner()
            )

        slot += self_ref.shape[1]


def lesser_part(hi, lo, before, shards, places, held, after=(), keep=True):
    vmem = pl.BlockSpec(memory_space=pltpu.VMEM)
    count = sum(x.shape[1] for x in shards)
    kept = jax.ShapeDtypeStruct((count, 4 * MARGIN, 2 * BS), BF16)
    outs = [jax.ShapeDtypeStruct(before.shape, F32)] + ([kept, kept] if keep else [])
    return pl.pallas_call(
        functools.partial(lesser_kernel, places, held, len(after)),
        out_shape=outs,
        in_specs=[vmem] * (3 + len(shards)) + [pl.BlockSpec(memory_space=pl.ANY)] * len(after),
        out_specs=[vmem] * len(outs),
        input_output_aliases={2: 0},
        compiler_params=pltpu.CompilerParams(vmem_limit_bytes=26 << 20),
        cost_estimate=pl.CostEstimate(
            flops=count * hi.shape[0] * BS * BS,
            bytes_accessed=before.size,
            transcendentals=0,
        ),
        name="lesser_more",
    )(hi, lo, before, *shards, *after)


def rows_kernel(wanted, green_ref, *rest):
    outs, sem = rest[-1 - len(wanted) : -1], rest[-1]
    copies = []
    for n, ((size, start), out) in enumerate(zip(wanted, outs)):
        row = pl.multiple_of(start(lax.axis_index("orb"), green_ref.shape[2]), HALF)
        copies.append(
            pltpu.make_async_copy(green_ref.at[0, :, pl.ds(row, size), :], out, sem.at[n])
        )
    for copy in copies:
        copy.start()
    for copy in copies:
        copy.wait()


def rows_at(green, wanted, after=()):
    count = len(wanted)
    outs = [jax.ShapeDtypeStruct((2, size, green.shape[3]), F32) for size, _ in wanted]
    return pl.pallas_call(
        functools.partial(rows_kernel, wanted),
        out_shape=outs,
        in_specs=[pl.BlockSpec(memory_space=pl.ANY)] * (1 + len(after)),
        out_specs=[pl.BlockSpec(memory_space=pltpu.VMEM)] * count,
        scratch_shapes=[pltpu.SemaphoreType.DMA((count,))],
        compiler_params=pltpu.CompilerParams(vmem_limit_bytes=8 << 20),
        cost_estimate=pl.CostEstimate(
            flops=0, bytes_accessed=4 * sum(x.size for x in outs), transcendentals=0
        ),
        name="rows",
    )(green, *after)


def gate_kernel(*refs):
    del refs


def gate(arrays, after):
    hbm = pl.BlockSpec(memory_space=pl.ANY)
    return pl.pallas_call(
        gate_kernel,
        out_shape=[jax.ShapeDtypeStruct(x.shape, x.dtype) for x in arrays],
        in_specs=[hbm] * (len(arrays) + len(after)),
        out_specs=[hbm] * len(arrays),
        input_output_aliases={n: n for n in range(len(arrays))},
        compiler_params=pltpu.CompilerParams(vmem_limit_bytes=1 << 20),
        cost_estimate=pl.CostEstimate(flops=0, bytes_accessed=0, transcendentals=0),
        name="gate",
    )(*arrays, *after)


def edge_kernel(places, held, paired, *refs):
    halos, refs = refs[: 2 if paired else 3], refs[2 if paired else 3 :]
    keeps = refs[: 2 * len(places)]
    left_ref, right_ref, own_ref, acc_ref = refs[2 * len(places) :]
    z, peers = lax.axis_index("orb"), lax.axis_size("orb")
    if is_far(peers):
        from_left, from_right = z == 1, z == peers - 2
    else:
        from_left = from_right = z < 0
    limit = jnp.where(from_right, MARGIN, HALF)
    acc_ref[...] = jnp.zeros_like(acc_ref)

    def rows_of(part, cols):
        if not paired:
            return [ref[part, :, cols] for ref in halos]
        first, second = halos[0][part, :HALF, cols], halos[0][part, HALF:, cols]
        middle = halos[1][part, :, cols]
        return (
            jnp.where(from_left, first, second),
            jnp.where(from_left, second, middle),
            jnp.where(from_left, middle, first),
        )

    def add(number, hi, lo, at):
        cols = pl.ds(pl.multiple_of(number * held * BS, BS), held * BS)
        wide = [rows_of(part, cols) for part in range(2)]
        for side in range(2):
            fields = []
            for part in range(2):
                outer = jnp.where(from_left if side == 0 else from_right, wide[part][0], 0.0)
                inner = wide[part][1 + side]
                rows = [outer, inner] if side == 0 else [inner, outer]
                fields.append(halves(jnp.concatenate(rows, axis=0)))
            halo = []
            for real, imag in zip(*fields):
                lanes = []
                for s in range(held):
                    one = slice(s * BS, (s + 1) * BS)
                    lanes += [
                        jnp.concatenate([real[:, one], -imag[:, one]], axis=0),
                        jnp.concatenate([imag[:, one], real[:, one]], axis=0),
                    ]
                halo.append(jnp.concatenate(lanes, axis=1))
            rows = slice(side * TILE, (side + 1) * TILE)
            kept = [
                jnp.concatenate([ref[at + s, rows, :] for s in range(held)], axis=1)
                for ref in (hi, lo)
            ]
            acc_ref[side] = acc_ref[side] + dot3(halo, kept, NT)

    @pl.when(is_inner())
    def _():
        for k, shards in enumerate(places):
            for n, place in enumerate(shards):
                number, valid = place()

                @pl.when(valid)
                def _():
                    add(number, keeps[2 * k], keeps[2 * k + 1], n * held)

    lane = lax.broadcasted_iota(jnp.int32, (MARGIN, LANES), 1)
    row = lax.broadcasted_iota(jnp.int32, (MARGIN, LANES), 0)
    low = lane < MARGIN
    left, right = acc_ref[0], acc_ref[1]
    turned_left, turned_right = left.T[:MARGIN], right.T[MARGIN:]
    for part in range(2):
        rows = slice(part * MARGIN, (part + 1) * MARGIN)
        sign = 1.0 - 2.0 * part
        to_left = jnp.where(low, 0.0, sign * left[rows])
        to_right = jnp.where(lane < limit, sign * right[rows], 0.0)
        if paired:
            to_left, to_right = (
                jnp.where(from_left, to_left, to_right),
                jnp.where(from_left, to_right, to_left),
            )
        left_ref[part] = to_left
        right_ref[part] = to_right
    own_ref[0, 0] = jnp.where(low, turned_left, 0.0)
    own_ref[0, 1] = jnp.where(low, pltpu.roll(turned_left, MARGIN, 1), 0.0)
    mine = jnp.logical_and(row < limit, lane >= MARGIN)
    own_ref[1, 0] = jnp.where(mine, pltpu.roll(turned_right, MARGIN, 1), 0.0)
    own_ref[1, 1] = jnp.where(mine, turned_right, 0.0)


def edge_part(halos, keeps, places, held, paired=False):
    vmem = pl.BlockSpec(memory_space=pltpu.VMEM)
    side = jax.ShapeDtypeStruct((2, MARGIN, LANES), F32)
    return pl.pallas_call(
        functools.partial(edge_kernel, places, held, paired),
        out_shape=(side, side, jax.ShapeDtypeStruct((2, 2, MARGIN, LANES), F32)),
        in_specs=[vmem] * (len(halos) + len(keeps)),
        out_specs=(vmem, vmem, vmem),
        scratch_shapes=[pltpu.VMEM((2, TILE, TILE), F32)],
        compiler_params=pltpu.CompilerParams(vmem_limit_bytes=20 << 20),
        cost_estimate=pl.CostEstimate(
            flops=1 << 31, bytes_accessed=8 << 20, transcendentals=0
        ),
        name="edges",
    )(*halos, *keeps)


def band_kernel(paired, acc_ref, own_ref, from_left_ref, from_right_ref, out_ref, rows_ref):
    tiles = acc_ref.shape[0]
    returned = [[ref[part] for part in range(2)] for ref in (from_left_ref, from_right_ref)]
    if paired:
        either = [x + y for x, y in zip(*returned)]
        high = lax.axis_index("orb") >= 2
        returned = [
            [jnp.where(high, x, 0.0) for x in either],
            [jnp.where(high, 0.0, x) for x in either],
        ]
    group = out_ref.shape[2]
    per_tile = TILE // W
    for t in range(tiles):
        for part in range(2):
            base = part * TILE
            x = acc_ref[t, base : base + TILE, :]
            rows_ref[t, part] = x
            if t == 0:
                extra = own_ref[0, part] + returned[0][part]
                rows_ref[t, part, :MARGIN, :LANES] = x[:MARGIN, :LANES] + extra
            if t == tiles - 1:
                extra = own_ref[1, part] + returned[1][part]
                rows_ref[t, part, MARGIN:, LANES:] = x[MARGIN:, LANES:] + extra
    low = lax.broadcasted_iota(jnp.int32, (W, LANES), 1) < MARGIN
    width = TILE + 2 * MARGIN
    for a in range(per_tile):
        for t in range(tiles):
            atom = t * per_tile + a
            for part in range(2):
                x = rows_ref[t, part, a * W : (a + 1) * W, :]
                before = pltpu.roll(x, (width - a * W) % width, 1)[:, :LANES]
                after = pltpu.roll(x, (width - (a + 1) * W) % width, 1)[:, :LANES]
                out_ref[atom // group, part, atom % group] = jnp.where(low, before, after)


def band(acc, own, from_left, from_right, energies, paired):
    tiles = acc.shape[0]
    atoms = tiles * TILE // W
    vmem = pl.BlockSpec(memory_space=pltpu.VMEM)
    return pl.pallas_call(
        functools.partial(band_kernel, paired),
        out_shape=jax.ShapeDtypeStruct((energies, 2, atoms // energies, W, LANES), F32),
        in_specs=[vmem] * 4,
        out_specs=vmem,
        scratch_shapes=[pltpu.VMEM((tiles, 2, TILE, TILE + 2 * MARGIN), F32)],
        compiler_params=pltpu.CompilerParams(vmem_limit_bytes=16 << 20),
        name="band",
    )(acc, own, from_left, from_right)


def scatter_kernel(recv_ref, where_ref, mix_ref, dham_ref, out_ref, smeared_ref, result_ref):
    energies, _, group, _, _ = recv_ref.shape
    padded = dham_ref.shape[1]
    pairs = out_ref.shape[1]
    columns = [
        recv_ref[:, :, a, :, :].reshape(energies * 2 * W, LANES) for a in range(group)
    ]
    received = halves(jnp.concatenate(columns, axis=1))
    mixed = halves(dot3(halves(mix_ref[...]), received, NN))
    entry = lax.broadcasted_iota(jnp.int32, (group * LANES, padded), 0)
    first = where_ref[...] * W
    for j in range(W):
        pick = jnp.where(entry == first + j, 1.0, 0.0).astype(BF16)
        smeared_ref[:, j * padded : (j + 1) * padded] = dot(mixed[0], pick, NN) + dot(
            mixed[1], pick, NN
        )

    def block(part, j, k):
        row = (part * W + j) * energies
        return smeared_ref[row : row + energies, k * padded : (k + 1) * padded]

    def factor(c, i, j):
        row = (c * W + i) * W + j
        return dham_ref[row : row + 1, :]

    for part in range(2):
        for i in range(W):
            total = [None] * W
            for c in range(3):
                for k in range(W):
                    t = None
                    for j in range(W):
                        term = factor(c, i, j) * block(part, j, k)
                        t = term if t is None else t + term
                    for l in range(W):
                        term = t * factor(c, l, k)
                        total[l] = term if total[l] is None else total[l] + term
            for l in range(W):
                row = ((part * W + i) * W + l) * energies
                result_ref[row : row + energies, :] = total[l]
    for e in range(energies):
        one = result_ref[pl.ds(e, 2 * W * W, stride=energies), :]
        out_ref[e] = one.T[:pairs, :]


def scatter(recv, where, mix, dham, pairs):
    energies, _, group, _, _ = recv.shape
    padded = dham.shape[1]
    vmem = pl.BlockSpec(memory_space=pltpu.VMEM)
    return pl.pallas_call(
        scatter_kernel,
        out_shape=jax.ShapeDtypeStruct((energies, pairs, 2 * W * W), F32),
        in_specs=[vmem] * 4,
        out_specs=vmem,
        scratch_shapes=[
            pltpu.VMEM((2 * W * energies, W * padded), F32),
            pltpu.VMEM((2 * W * W * energies, padded), F32),
        ],
        compiler_params=pltpu.CompilerParams(vmem_limit_bytes=24 << 20),
        name="scatter",
    )(recv, where, mix, dham)


def build_kernel(phonon_shift, phonon_weight, energies):
    rows_e = jnp.arange(energies, dtype=jnp.int32)[None, :, None]
    cols_f = jnp.arange(energies, dtype=jnp.int32)[None, None, :]
    shifts = phonon_shift[:, None, None]
    emission = (cols_f == rows_e + shifts).astype(F32)
    absorption = (cols_f == rows_e - shifts).astype(F32)
    terms = (
        phonon_weight[0][:, None, None] * emission + phonon_weight[1][:, None, None] * absorption
    )
    return jnp.sum(terms, axis=0)


def build_mix(phonon_shift, phonon_weight, energies):
    kernel = build_kernel(phonon_shift, phonon_weight, energies)
    same = jnp.eye(2 * W, dtype=F32)
    mix = same[:, None, None, :] * kernel[None, :, :, None]
    return mix.reshape(2 * W * energies, energies * 2 * W)


def send(x, pairs):
    return lax.ppermute(x, "orb", pairs)


def per_device(green, sigma, neighbours, phonon_shift, phonon_weight, dham):
    energies = lax.axis_size("energy")
    peers = lax.axis_size("orb")
    e, z = lax.axis_index("energy"), lax.axis_index("orb")
    rows = green.shape[2]
    atoms = rows // W
    degree = neighbours.shape[1]
    group = atoms // energies
    pairs = group * degree
    padded = -(-pairs // LANES) * LANES
    held = sigma.shape[1]

    far, paired = is_far(peers), peers == 4
    up = [(i, i + 1) for i in range(peers - 1)]
    down = [(i + 1, i) for i in range(peers - 1)]
    fixed = pltpu.with_memory_space_constraint(green, pltpu.HBM)
    if paired:
        ends, middle, outward = [(0, 1), (3, 2)], [(1, 2), (2, 1)], [(1, 0), (2, 3)]
        aside, across = send(sigma, ends + outward), send(sigma, middle)
        near = rows_at(fixed, [(HALF, lambda z, rows: jnp.where(z == 1, rows - HALF, 0))])
    else:
        right, left = send(sigma, up), send(sigma, down)
        near = rows_at(fixed, [(HALF, lambda z, rows: rows - HALF), (HALF, lambda z, rows: 0 * z)])

    mine = lax.dynamic_slice_in_dim(neighbours, e * group, group, axis=0)
    first = z * atoms + e * group
    offset = mine - (first + jnp.arange(group, dtype=jnp.int32))[:, None]
    column = jnp.where(offset < 0, offset + REACH, offset + REACH - 1)
    where = column + 2 * REACH * jnp.arange(group, dtype=jnp.int32)[:, None]
    where = jnp.pad(where.reshape(1, pairs), ((0, 0), (0, padded - pairs)), constant_values=-1)
    mix = build_mix(phonon_shift, phonon_weight, energies)
    factors = lax.dynamic_slice_in_dim(
        dham.transpose(1, 2, 3, 0).reshape(3 * W * W, -1), e * pairs, pairs, axis=1
    )
    factors = jnp.pad(factors, ((0, 0), (0, padded - pairs)))


    acc, *keeps, hi, lo = own_part(
        fixed,
        pltpu.with_memory_space_constraint(sigma, pltpu.HBM),
        [where, mix, factors, near[0]],
    )
    more = functools.partial(lesser_part, hi, lo, held=held)
    places = [[neighbour(0)]]
    if paired:
        (outer,) = rows_at(
            fixed, [(MARGIN, lambda z, rows: jnp.where(z == 0, rows - MARGIN, 0))], [keeps[-1]]
        )
        aside, across = gate([aside, across], [keeps[-1], outer])
        second_across, second_aside = send(aside, middle), send(across, outward)
        halos = [send(outer, ends), send(near[0], middle)]
        places.append([beside, reflected(3, True)])
        acc, *kept = more(acc, [aside, across], places[-1])
        keeps += kept
        (second_across,) = gate([second_across], [kept[-1]])
        third_aside = send(second_across, outward)
        places.append([two_off(True), two_off(False)])
        acc, *kept = more(acc, [second_across, second_aside], places[-1])
        keeps += kept
        to_end, to_middle, own = edge_part(halos, keeps, places, held, True)
        back_left, back_right = send(to_end, outward), send(to_middle, middle)
        (acc,) = more(acc, [third_aside], [reflected(3, False)], after=[to_end], keep=False)
    else:
        near_right = send(near[0], up[:-1] if far else up)
        near_left = send(near[1], down[1:] if far else down)
        if far:
            (outer,) = rows_at(
                fixed,
                [(HALF, lambda z, rows: jnp.where(z == 0, rows - MARGIN, HALF))],
                [keeps[-1]],
            )
            other = send(outer, [(0, 1), (peers - 1, peers - 2)])
        else:
            outer = other = jnp.zeros_like(near_left)
        for k in range(1, peers):
            around = [neighbour(-k), neighbour(k)]
            if k < peers - 1:
                right, left = gate([right, left], [keeps[-1], outer if k == 1 else other])
                following = send(right, up[k:]), send(left, down[: peers - 1 - k])
                after = []
            else:
                if not far:
                    acc, *kept = more(acc, [right, left], around)
                    keeps += kept
                    places.append(around)
                to_left, to_right, own = edge_part(
                    [other, near_right, near_left], keeps, places, held
                )
                back_right = send(to_left, down[:-1] if far else down)
                back_left = send(to_right, up[1:] if far else up)
                after = [to_left]
                if not far:
                    break
            acc, *kept = more(acc, [right, left], around, after=after, keep=k < peers - 1)
            keeps += kept
            places.append(around)
            if k < peers - 1:
                right, left = following
    lesser = band(acc, own, back_left, back_right, energies, paired)

    recv = lax.all_to_all(lesser, "energy", split_axis=0, concat_axis=0, tiled=True)
    spread = scatter(recv, where, mix, factors, pairs)
    result = lax.all_to_all(spread, "energy", split_axis=0, concat_axis=0, tiled=True)
    return result.reshape(1, atoms * degree, 2 * W * W)


def solution(mesh):
    return jax.shard_map(
        per_device,
        mesh=mesh,
        in_specs=(
            P("energy", None, "orb", None),
            P("energy", "orb", None, None, None),
            P("orb", None),
            P(),
            P(),
            P("orb", None, None, None),
        ),
        out_specs=P("energy", "orb", None),
        check_vma=False,
    )
```

```python
import functools

import jax
import jax.numpy as jnp
from jax import lax
from jax.experimental import pallas as pl
from jax.experimental.pallas import tpu as pltpu
from jax.sharding import PartitionSpec as P

W = 8
BS = 128
REACH = 8
MARGIN = REACH * W
HALF = MARGIN // 2
TILE = 128
LANES = 128
F32, BF16 = jnp.float32, jnp.bfloat16

NT = (((1,), (1,)), ((), ()))
NN = (((1,), (0,)), ((), ()))


def halves(x):
    hi = x.astype(BF16)
    return hi, (x - hi.astype(F32)).astype(BF16)


def dot(a, b, dims):
    return lax.dot_general(a, b, dims, preferred_element_type=F32)


def dot3(a, b, dims):
    left = jnp.concatenate([a[0], a[0], a[1]], axis=1)
    right = jnp.concatenate([b[0], b[1], b[0]], axis=dims[0][1][0])
    return dot(left, right, dims)


def blocks_at_once(held):
    return 2 if held % 2 == 0 else 1


def some_blocks(lane, weights, hi_ref, lo_ref, acc_ref, edges, active):
    rows = hi_ref.shape[0] - 2 * MARGIN
    wide = 2 * BS
    split, products = [], []
    for n, (real, imag) in enumerate(weights):
        top = jnp.concatenate([real, imag], axis=1)
        weight = halves(jnp.concatenate([top, jnp.concatenate([-imag, real], axis=1)], axis=0))
        cols = pl.ds(lane + n * wide, wide)
        own = [ref[MARGIN : MARGIN + rows, cols] for ref in (hi_ref, lo_ref)]
        product = halves(dot3(own, weight, NN))
        for ref, part in zip(edges, product):
            ref[n, :MARGIN, :] = part[:MARGIN]
            ref[n, 3 * MARGIN :, :] = part[rows - MARGIN :]
        split.append(weight)
        products.append(product)
    cols = pl.ds(lane, len(weights) * wide)
    for t in range(rows // TILE):
        both = []
        for part in zip(*products):
            lanes = []
            for x in part:
                x = x[t * TILE : (t + 1) * TILE]
                turned = jnp.concatenate([x[:, BS:], -x[:, :BS]], axis=1)
                lanes.append(jnp.concatenate([x, turned], axis=0))
            both.append(jnp.concatenate(lanes, axis=1))
        near = pl.ds(t * TILE, TILE + 2 * MARGIN)
        acc_ref[t] = acc_ref[t] + dot3(both, (hi_ref[near, cols], lo_ref[near, cols]), NT)

    if not edges:
        return

    @pl.when(active)
    def _():
        for n, weight in enumerate(split):
            one = pl.ds(lane + n * wide, wide)
            outer = [
                jnp.concatenate(
                    [ref[MARGIN : 2 * MARGIN, one], ref[rows : rows + MARGIN, one]], axis=0
                )
                for ref in (hi_ref, lo_ref)
            ]
            for ref, part in zip(edges, halves(dot3(outer, weight, NT))):
                ref[n, MARGIN : 3 * MARGIN, :] = part


def shard_loop(first_block, self_ref, hi_ref, lo_ref, acc_ref, keeps, slot, active):
    held = self_ref.shape[1]
    once = blocks_at_once(held)

    def step(g, carry):
        lane = pl.multiple_of((first_block + g * once) * 2 * BS, 2 * BS)
        weights = [
            (self_ref[0, g * once + n, 0], self_ref[0, g * once + n, 1]) for n in range(once)
        ]
        slots = pl.ds(slot + g * once, once)
        kept = tuple(ref.at[slots] for ref in keeps)
        some_blocks(lane, weights, hi_ref, lo_ref, acc_ref, kept, active)
        return carry

    lax.fori_loop(0, held // once, step, 0)


def is_far(peers):
    return peers >= 4


def is_inner():
    z, peers = lax.axis_index("orb"), lax.axis_size("orb")
    if is_far(peers):
        return jnp.logical_and(z > 0, z < peers - 1)
    return z >= 0


def neighbour(distance):
    def place():
        z, peers = lax.axis_index("orb"), lax.axis_size("orb")
        number = z + distance
        return jnp.clip(number, 0, peers - 1), jnp.logical_and(number >= 0, number < peers)

    return place


def reflected(offset, inner):
    def place():
        z = lax.axis_index("orb")
        is_inner_one = jnp.logical_or(z == 1, z == 2)
        valid = z >= 0 if inner is None else is_inner_one == inner
        return lax.rem(offset + 4 - z, 4), valid

    return place


def beside():
    z = lax.axis_index("orb")
    return jnp.where(lax.rem(z, 2) == 0, z + 1, z - 1), z >= 0


def two_off(inner):
    def place():
        z = lax.axis_index("orb")
        return lax.rem(z + 2, 4), jnp.logical_or(z == 1, z == 2) == inner

    return place


def own_kernel(wanted, extra, green_ref, sigma_ref, *rest):
    acc_ref, keep_hi_ref, keep_lo_ref, hi_ref, lo_ref, *rest = rest[extra:]
    *sent, buf, self_ref, sem, sent_sem = rest
    rows, held = green_ref.shape[2], sigma_ref.shape[1]
    blocks = green_ref.shape[3] // BS
    begin, active = lax.axis_index("orb") * held, is_inner()

    def block_of(s):
        return lax.rem(begin + s, blocks)

    def fetch(s):
        col = pl.multiple_of(block_of(s) * BS, BS)
        return pltpu.make_async_copy(
            green_ref.at[0, :, :, pl.ds(col, BS)], buf.at[s], sem.at[s]
        )

    def store(s, carry):
        fetch(s).wait()
        lanes = pl.ds(pl.multiple_of(block_of(s) * 2 * BS, 2 * BS), 2 * BS)
        parts = halves(jnp.concatenate([buf[s, 0], buf[s, 1]], axis=1))
        for ref, part in zip((hi_ref, lo_ref), parts):
            ref[MARGIN : MARGIN + rows, lanes] = part
        return carry

    load = pltpu.make_async_copy(sigma_ref, self_ref, sem.at[blocks])
    load.start()
    for s in range(blocks):
        fetch(s).start()
    copies = []
    for n, ((size, start), out) in enumerate(zip(wanted, sent)):
        row = pl.multiple_of(start(lax.axis_index("orb"), rows), HALF)
        copies.append(
            pltpu.make_async_copy(green_ref.at[0, :, pl.ds(row, size), :], out, sent_sem.at[n])
        )
    for copy in copies:
        copy.start()
    acc_ref[...] = jnp.zeros_like(acc_ref)
    for ref in (hi_ref, lo_ref):
        ref[:MARGIN, :] = jnp.zeros((MARGIN, ref.shape[1]), BF16)
        ref[MARGIN + rows :, :] = jnp.zeros((MARGIN, ref.shape[1]), BF16)
    lax.fori_loop(0, held, store, 0)
    load.wait()
    shard_loop(begin, self_ref, hi_ref, lo_ref, acc_ref, (keep_hi_ref, keep_lo_ref), 0, active)
    lax.fori_loop(held, blocks, store, 0)
    for copy in copies:
        copy.wait()


def own_part(green, sigma, wanted, after):
    rows, held = green.shape[2], sigma.shape[1]
    tiles, blocks = rows // TILE, green.shape[3] // BS
    vmem = pl.BlockSpec(memory_space=pltpu.VMEM)
    hbm = pl.BlockSpec(memory_space=pl.ANY)
    keep = jax.ShapeDtypeStruct((held, 4 * MARGIN, 2 * BS), BF16)
    whole = jax.ShapeDtypeStruct((rows + 2 * MARGIN, blocks * 2 * BS), BF16)
    return pl.pallas_call(
        functools.partial(own_kernel, wanted, len(after)),
        out_shape=(
            jax.ShapeDtypeStruct((tiles, 2 * TILE, TILE + 2 * MARGIN), F32),
            keep,
            keep,
            whole,
            whole,
            *[jax.ShapeDtypeStruct((2, size, green.shape[3]), F32) for size, _ in wanted],
        ),
        in_specs=[hbm] * (2 + len(after)),
        out_specs=(vmem,) * (5 + len(wanted)),
        scratch_shapes=[
            pltpu.VMEM((blocks, 2, rows, BS), F32),
            pltpu.VMEM(sigma.shape, F32),
            pltpu.SemaphoreType.DMA((blocks + 1,)),
            pltpu.SemaphoreType.DMA((len(wanted),)),
        ],
        compiler_params=pltpu.CompilerParams(vmem_limit_bytes=40 << 20),
        cost_estimate=pl.CostEstimate(
            flops=held * rows * BS * BS,
            bytes_accessed=blocks * rows * BS,
            transcendentals=0,
        ),
        name="lesser_own",
    )(green, sigma, *after)


def lesser_kernel(places, held, extra, hi_ref, lo_ref, before_ref, *rest):
    sigmas, rest = rest[: len(places)], rest[len(places) :]
    rest = rest[extra:]
    acc_ref, keeps = rest[0], rest[1:]
    acc_ref[...] = before_ref[...]
    slot = 0
    for place, self_ref in zip(places, sigmas):
        number, valid = place()

        @pl.when(valid)
        def _():
            shard_loop(
                number * held, self_ref, hi_ref, lo_ref, acc_ref, keeps, slot, is_inner()
            )

        slot += self_ref.shape[1]


def lesser_part(hi, lo, before, shards, places, held, after=(), keep=True):
    vmem = pl.BlockSpec(memory_space=pltpu.VMEM)
    count = sum(x.shape[1] for x in shards)
    kept = jax.ShapeDtypeStruct((count, 4 * MARGIN, 2 * BS), BF16)
    outs = [jax.ShapeDtypeStruct(before.shape, F32)] + ([kept, kept] if keep else [])
    return pl.pallas_call(
        functools.partial(lesser_kernel, places, held, len(after)),
        out_shape=outs,
        in_specs=[vmem] * (3 + len(shards)) + [pl.BlockSpec(memory_space=pl.ANY)] * len(after),
        out_specs=[vmem] * len(outs),
        input_output_aliases={2: 0},
        compiler_params=pltpu.CompilerParams(vmem_limit_bytes=26 << 20),
        cost_estimate=pl.CostEstimate(
            flops=count * hi.shape[0] * BS * BS,
            bytes_accessed=before.size,
            transcendentals=0,
        ),
        name="lesser_more",
    )(hi, lo, before, *shards, *after)


def gate_kernel(*refs):
    del refs


def gate(arrays, after):
    hbm = pl.BlockSpec(memory_space=pl.ANY)
    return pl.pallas_call(
        gate_kernel,
        out_shape=[jax.ShapeDtypeStruct(x.shape, x.dtype) for x in arrays],
        in_specs=[hbm] * (len(arrays) + len(after)),
        out_specs=[hbm] * len(arrays),
        input_output_aliases={n: n for n in range(len(arrays))},
        compiler_params=pltpu.CompilerParams(vmem_limit_bytes=1 << 20),
        cost_estimate=pl.CostEstimate(flops=0, bytes_accessed=0, transcendentals=0),
        name="gate",
    )(*arrays, *after)


def edge_kernel(places, held, paired, *refs):
    halos, refs = refs[: 2 if paired else 3], refs[2 if paired else 3 :]
    keeps = refs[: 2 * len(places)]
    left_ref, right_ref, own_ref, acc_ref = refs[2 * len(places) :]
    z, peers = lax.axis_index("orb"), lax.axis_size("orb")
    if is_far(peers):
        from_left, from_right = z == 1, z == peers - 2
    else:
        from_left = from_right = z < 0
    limit = jnp.where(from_right, MARGIN, HALF)
    acc_ref[...] = jnp.zeros_like(acc_ref)

    def rows_of(part, cols):
        if not paired:
            return [ref[part, :, cols] for ref in halos]
        first, second = halos[0][part, :HALF, cols], halos[0][part, HALF:, cols]
        middle = halos[1][part, :, cols]
        return (
            jnp.where(from_left, first, second),
            jnp.where(from_left, second, middle),
            jnp.where(from_left, middle, first),
        )

    def add(number, hi, lo, at):
        cols = pl.ds(pl.multiple_of(number * held * BS, BS), held * BS)
        wide = [rows_of(part, cols) for part in range(2)]
        for side in range(2):
            fields = []
            for part in range(2):
                outer = jnp.where(from_left if side == 0 else from_right, wide[part][0], 0.0)
                inner = wide[part][1 + side]
                rows = [outer, inner] if side == 0 else [inner, outer]
                fields.append(halves(jnp.concatenate(rows, axis=0)))
            halo = []
            for real, imag in zip(*fields):
                lanes = []
                for s in range(held):
                    one = slice(s * BS, (s + 1) * BS)
                    lanes += [
                        jnp.concatenate([real[:, one], -imag[:, one]], axis=0),
                        jnp.concatenate([imag[:, one], real[:, one]], axis=0),
                    ]
                halo.append(jnp.concatenate(lanes, axis=1))
            rows = slice(side * TILE, (side + 1) * TILE)
            kept = [
                jnp.concatenate([ref[at + s, rows, :] for s in range(held)], axis=1)
                for ref in (hi, lo)
            ]
            acc_ref[side] = acc_ref[side] + dot3(halo, kept, NT)

    @pl.when(is_inner())
    def _():
        for k, shards in enumerate(places):
            for n, place in enumerate(shards):
                number, valid = place()

                @pl.when(valid)
                def _():
                    add(number, keeps[2 * k], keeps[2 * k + 1], n * held)

    lane = lax.broadcasted_iota(jnp.int32, (MARGIN, LANES), 1)
    row = lax.broadcasted_iota(jnp.int32, (MARGIN, LANES), 0)
    low = lane < MARGIN
    left, right = acc_ref[0], acc_ref[1]
    turned_left, turned_right = left.T[:MARGIN], right.T[MARGIN:]
    for part in range(2):
        rows = slice(part * MARGIN, (part + 1) * MARGIN)
        sign = 1.0 - 2.0 * part
        to_left = jnp.where(low, 0.0, sign * left[rows])
        to_right = jnp.where(lane < limit, sign * right[rows], 0.0)
        if paired:
            to_left, to_right = (
                jnp.where(from_left, to_left, to_right),
                jnp.where(from_left, to_right, to_left),
            )
        left_ref[part] = to_left
        right_ref[part] = to_right
    own_ref[0, 0] = jnp.where(low, turned_left, 0.0)
    own_ref[0, 1] = jnp.where(low, pltpu.roll(turned_left, MARGIN, 1), 0.0)
    mine = jnp.logical_and(row < limit, lane >= MARGIN)
    own_ref[1, 0] = jnp.where(mine, pltpu.roll(turned_right, MARGIN, 1), 0.0)
    own_ref[1, 1] = jnp.where(mine, turned_right, 0.0)


def edge_part(halos, keeps, places, held, paired=False):
    vmem = pl.BlockSpec(memory_space=pltpu.VMEM)
    side = jax.ShapeDtypeStruct((2, MARGIN, LANES), F32)
    return pl.pallas_call(
        functools.partial(edge_kernel, places, held, paired),
        out_shape=(side, side, jax.ShapeDtypeStruct((2, 2, MARGIN, LANES), F32)),
        in_specs=[vmem] * (len(halos) + len(keeps)),
        out_specs=(vmem, vmem, vmem),
        scratch_shapes=[pltpu.VMEM((2, TILE, TILE), F32)],
        compiler_params=pltpu.CompilerParams(vmem_limit_bytes=20 << 20),
        cost_estimate=pl.CostEstimate(
            flops=1 << 31, bytes_accessed=8 << 20, transcendentals=0
        ),
        name="edges",
    )(*halos, *keeps)


def band_kernel(paired, acc_ref, own_ref, from_left_ref, from_right_ref, out_ref, rows_ref):
    tiles = acc_ref.shape[0]
    returned = [[ref[part] for part in range(2)] for ref in (from_left_ref, from_right_ref)]
    if paired:
        either = [x + y for x, y in zip(*returned)]
        high = lax.axis_index("orb") >= 2
        returned = [
            [jnp.where(high, x, 0.0) for x in either],
            [jnp.where(high, 0.0, x) for x in either],
        ]
    group = out_ref.shape[2]
    per_tile = TILE // W
    for t in range(tiles):
        for part in range(2):
            base = part * TILE
            x = acc_ref[t, base : base + TILE, :]
            rows_ref[t, part] = x
            if t == 0:
                extra = own_ref[0, part] + returned[0][part]
                rows_ref[t, part, :MARGIN, :LANES] = x[:MARGIN, :LANES] + extra
            if t == tiles - 1:
                extra = own_ref[1, part] + returned[1][part]
                rows_ref[t, part, MARGIN:, LANES:] = x[MARGIN:, LANES:] + extra
    low = lax.broadcasted_iota(jnp.int32, (W, LANES), 1) < MARGIN
    width = TILE + 2 * MARGIN
    for a in range(per_tile):
        for t in range(tiles):
            atom = t * per_tile + a
            for part in range(2):
                x = rows_ref[t, part, a * W : (a + 1) * W, :]
                before = pltpu.roll(x, (width - a * W) % width, 1)[:, :LANES]
                after = pltpu.roll(x, (width - (a + 1) * W) % width, 1)[:, :LANES]
                out_ref[atom // group, part, atom % group] = jnp.where(low, before, after)


def band(acc, own, from_left, from_right, energies, paired):
    tiles = acc.shape[0]
    atoms = tiles * TILE // W
    vmem = pl.BlockSpec(memory_space=pltpu.VMEM)
    return pl.pallas_call(
        functools.partial(band_kernel, paired),
        out_shape=jax.ShapeDtypeStruct((energies, 2, atoms // energies, W, LANES), F32),
        in_specs=[vmem] * 4,
        out_specs=vmem,
        scratch_shapes=[pltpu.VMEM((tiles, 2, TILE, TILE + 2 * MARGIN), F32)],
        compiler_params=pltpu.CompilerParams(vmem_limit_bytes=16 << 20),
        name="band",
    )(acc, own, from_left, from_right)


def scatter_kernel(recv_ref, where_ref, mix_ref, dham_ref, out_ref, smeared_ref, result_ref):
    energies, _, group, _, _ = recv_ref.shape
    padded = dham_ref.shape[1]
    pairs = out_ref.shape[1]
    columns = [
        recv_ref[:, :, a, :, :].reshape(energies * 2 * W, LANES) for a in range(group)
    ]
    received = halves(jnp.concatenate(columns, axis=1))
    mixed = halves(dot3(halves(mix_ref[...]), received, NN))
    entry = lax.broadcasted_iota(jnp.int32, (group * LANES, padded), 0)
    first = where_ref[...] * W
    for j in range(W):
        pick = jnp.where(entry == first + j, 1.0, 0.0).astype(BF16)
        smeared_ref[:, j * padded : (j + 1) * padded] = dot(mixed[0], pick, NN) + dot(
            mixed[1], pick, NN
        )

    def block(part, j, k):
        row = (part * W + j) * energies
        return smeared_ref[row : row + energies, k * padded : (k + 1) * padded]

    def factor(c, i, j):
        row = (c * W + i) * W + j
        return dham_ref[row : row + 1, :]

    for part in range(2):
        for i in range(W):
            total = [None] * W
            for c in range(3):
                for k in range(W):
                    t = None
                    for j in range(W):
                        term = factor(c, i, j) * block(part, j, k)
                        t = term if t is None else t + term
                    for l in range(W):
                        term = t * factor(c, l, k)
                        total[l] = term if total[l] is None else total[l] + term
            for l in range(W):
                row = ((part * W + i) * W + l) * energies
                result_ref[row : row + energies, :] = total[l]
    for e in range(energies):
        one = result_ref[pl.ds(e, 2 * W * W, stride=energies), :]
        out_ref[e] = one.T[:pairs, :]


def scatter(recv, where, mix, dham, pairs):
    energies, _, group, _, _ = recv.shape
    padded = dham.shape[1]
    vmem = pl.BlockSpec(memory_space=pltpu.VMEM)
    return pl.pallas_call(
        scatter_kernel,
        out_shape=jax.ShapeDtypeStruct((energies, pairs, 2 * W * W), F32),
        in_specs=[vmem] * 4,
        out_specs=vmem,
        scratch_shapes=[
            pltpu.VMEM((2 * W * energies, W * padded), F32),
            pltpu.VMEM((2 * W * W * energies, padded), F32),
        ],
        compiler_params=pltpu.CompilerParams(vmem_limit_bytes=24 << 20),
        name="scatter",
    )(recv, where, mix, dham)


def build_kernel(phonon_shift, phonon_weight, energies):
    rows_e = jnp.arange(energies, dtype=jnp.int32)[None, :, None]
    cols_f = jnp.arange(energies, dtype=jnp.int32)[None, None, :]
    shifts = phonon_shift[:, None, None]
    emission = (cols_f == rows_e + shifts).astype(F32)
    absorption = (cols_f == rows_e - shifts).astype(F32)
    terms = (
        phonon_weight[0][:, None, None] * emission + phonon_weight[1][:, None, None] * absorption
    )
    return jnp.sum(terms, axis=0)


def build_mix(phonon_shift, phonon_weight, energies):
    kernel = build_kernel(phonon_shift, phonon_weight, energies)
    same = jnp.eye(2 * W, dtype=F32)
    mix = same[:, None, None, :] * kernel[None, :, :, None]
    return mix.reshape(2 * W * energies, energies * 2 * W)


def send(x, pairs):
    return lax.ppermute(x, "orb", pairs)


def per_device(green, sigma, neighbours, phonon_shift, phonon_weight, dham):
    energies = lax.axis_size("energy")
    peers = lax.axis_size("orb")
    e, z = lax.axis_index("energy"), lax.axis_index("orb")
    rows = green.shape[2]
    atoms = rows // W
    degree = neighbours.shape[1]
    group = atoms // energies
    pairs = group * degree
    padded = -(-pairs // LANES) * LANES
    held = sigma.shape[1]

    far, paired = is_far(peers), peers == 4
    up = [(i, i + 1) for i in range(peers - 1)]
    down = [(i + 1, i) for i in range(peers - 1)]
    fixed = pltpu.with_memory_space_constraint(green, pltpu.HBM)
    if paired:
        ends, middle, outward = [(0, 1), (3, 2)], [(1, 2), (2, 1)], [(1, 0), (2, 3)]
        aside, across = send(sigma, ends + outward), send(sigma, middle)
        wanted = [
            (MARGIN, lambda z, rows: jnp.where(z == 0, rows - MARGIN, 0)),
            (HALF, lambda z, rows: jnp.where(z == 1, rows - HALF, 0)),
        ]
    else:
        right, left = send(sigma, up), send(sigma, down)
        wanted = [
            (HALF, lambda z, rows: jnp.where(z == 0, rows - MARGIN, HALF)),
            (HALF, lambda z, rows: rows - HALF),
            (HALF, lambda z, rows: 0 * z),
        ]

    mine = lax.dynamic_slice_in_dim(neighbours, e * group, group, axis=0)
    first = z * atoms + e * group
    offset = mine - (first + jnp.arange(group, dtype=jnp.int32))[:, None]
    column = jnp.where(offset < 0, offset + REACH, offset + REACH - 1)
    where = column + 2 * REACH * jnp.arange(group, dtype=jnp.int32)[:, None]
    where = jnp.pad(where.reshape(1, pairs), ((0, 0), (0, padded - pairs)), constant_values=-1)
    mix = build_mix(phonon_shift, phonon_weight, energies)
    factors = lax.dynamic_slice_in_dim(
        dham.transpose(1, 2, 3, 0).reshape(3 * W * W, -1), e * pairs, pairs, axis=1
    )
    factors = jnp.pad(factors, ((0, 0), (0, padded - pairs)))


    acc, keep_hi, keep_lo, hi, lo, outer, near, *nearer = own_part(
        fixed,
        pltpu.with_memory_space_constraint(sigma, pltpu.HBM),
        wanted,
        [where, mix, factors],
    )
    keeps = [keep_hi, keep_lo]
    more = functools.partial(lesser_part, hi, lo, held=held)
    places = [[neighbour(0)]]
    if paired:
        aside, across = gate([aside, across], [keeps[-1]])
        second_across, second_aside = send(aside, middle), send(across, outward)
        halos = [send(outer, ends), send(near, middle)]
        places.append([beside, reflected(3, True)])
        acc, *kept = more(acc, [aside, across], places[-1])
        keeps += kept
        (second_across,) = gate([second_across], [kept[-1]])
        third_aside = send(second_across, outward)
        places.append([two_off(True), two_off(False)])
        acc, *kept = more(acc, [second_across, second_aside], places[-1])
        keeps += kept
        to_end, to_middle, own = edge_part(halos, keeps, places, held, True)
        back_left, back_right = send(to_end, outward), send(to_middle, middle)
        (acc,) = more(acc, [third_aside], [reflected(3, False)], after=[to_end], keep=False)
    else:
        near_right = send(near, up[:-1] if far else up)
        near_left = send(nearer[0], down[1:] if far else down)
        if far:
            other = send(outer, [(0, 1), (peers - 1, peers - 2)])
        else:
            other = jnp.zeros_like(near_left)
        for k in range(1, peers):
            around = [neighbour(-k), neighbour(k)]
            if k < peers - 1:
                right, left = gate([right, left], [keeps[-1], outer if k == 1 else other])
                following = send(right, up[k:]), send(left, down[: peers - 1 - k])
                after = []
            else:
                if not far:
                    acc, *kept = more(acc, [right, left], around)
                    keeps += kept
                    places.append(around)
                to_left, to_right, own = edge_part(
                    [other, near_right, near_left], keeps, places, held
                )
                back_right = send(to_left, down[:-1] if far else down)
                back_left = send(to_right, up[1:] if far else up)
                after = [to_left]
                if not far:
                    break
            acc, *kept = more(acc, [right, left], around, after=after, keep=k < peers - 1)
            keeps += kept
            places.append(around)
            if k < peers - 1:
                right, left = following
    lesser = band(acc, own, back_left, back_right, energies, paired)

    recv = lax.all_to_all(lesser, "energy", split_axis=0, concat_axis=0, tiled=True)
    spread = scatter(recv, where, mix, factors, pairs)
    result = lax.all_to_all(spread, "energy", split_axis=0, concat_axis=0, tiled=True)
    return result.reshape(1, atoms * degree, 2 * W * W)


def solution(mesh):
    return jax.shard_map(
        per_device,
        mesh=mesh,
        in_specs=(
            P("energy", None, "orb", None),
            P("energy", "orb", None, None, None),
            P("orb", None),
            P(),
            P(),
            P("orb", None, None, None),
        ),
        out_specs=P("energy", "orb", None),
        check_vma=False,
    )
```

```python
import functools

import jax
import jax.numpy as jnp
from jax import lax
from jax.experimental import pallas as pl
from jax.experimental.pallas import tpu as pltpu
from jax.sharding import PartitionSpec as P

W = 8
BS = 128
REACH = 8
MARGIN = REACH * W
HALF = MARGIN // 2
TILE = 128
LANES = 128
F32, BF16 = jnp.float32, jnp.bfloat16

NT = (((1,), (1,)), ((), ()))
NN = (((1,), (0,)), ((), ()))


def halves(x):
    hi = x.astype(BF16)
    return hi, (x - hi.astype(F32)).astype(BF16)


def dot(a, b, dims):
    return lax.dot_general(a, b, dims, preferred_element_type=F32)


def dot3(a, b, dims):
    left = jnp.concatenate([a[0], a[0], a[1]], axis=1)
    right = jnp.concatenate([b[0], b[1], b[0]], axis=dims[0][1][0])
    return dot(left, right, dims)


def blocks_at_once(held):
    return 2 if held % 2 == 0 else 1


def some_blocks(lane, weights, hi_ref, lo_ref, acc_ref, edges, active):
    rows = hi_ref.shape[0] - 2 * MARGIN
    wide = 2 * BS
    split, products = [], []
    for n, (real, imag) in enumerate(weights):
        top = jnp.concatenate([real, imag], axis=1)
        weight = halves(jnp.concatenate([top, jnp.concatenate([-imag, real], axis=1)], axis=0))
        cols = pl.ds(lane + n * wide, wide)
        own = [ref[MARGIN : MARGIN + rows, cols] for ref in (hi_ref, lo_ref)]
        product = halves(dot3(own, weight, NN))
        for ref, part in zip(edges, product):
            ref[n, :MARGIN, :] = part[:MARGIN]
            ref[n, 3 * MARGIN :, :] = part[rows - MARGIN :]
        split.append(weight)
        products.append(product)
    cols = pl.ds(lane, len(weights) * wide)
    for t in range(rows // TILE):
        both = []
        for part in zip(*products):
            lanes = []
            for x in part:
                x = x[t * TILE : (t + 1) * TILE]
                turned = jnp.concatenate([x[:, BS:], -x[:, :BS]], axis=1)
                lanes.append(jnp.concatenate([x, turned], axis=0))
            both.append(jnp.concatenate(lanes, axis=1))
        near = pl.ds(t * TILE, TILE + 2 * MARGIN)
        acc_ref[t] = acc_ref[t] + dot3(both, (hi_ref[near, cols], lo_ref[near, cols]), NT)

    if not edges:
        return

    @pl.when(active)
    def _():
        for n, weight in enumerate(split):
            one = pl.ds(lane + n * wide, wide)
            outer = [
                jnp.concatenate(
                    [ref[MARGIN : 2 * MARGIN, one], ref[rows : rows + MARGIN, one]], axis=0
                )
                for ref in (hi_ref, lo_ref)
            ]
            for ref, part in zip(edges, halves(dot3(outer, weight, NT))):
                ref[n, MARGIN : 3 * MARGIN, :] = part


def shard_loop(first_block, self_ref, hi_ref, lo_ref, acc_ref, keeps, slot, active):
    held = self_ref.shape[1]
    once = blocks_at_once(held)

    def step(g, carry):
        lane = pl.multiple_of((first_block + g * once) * 2 * BS, 2 * BS)
        weights = [
            (self_ref[0, g * once + n, 0], self_ref[0, g * once + n, 1]) for n in range(once)
        ]
        slots = pl.ds(slot + g * once, once)
        kept = tuple(ref.at[slots] for ref in keeps)
        some_blocks(lane, weights, hi_ref, lo_ref, acc_ref, kept, active)
        return carry

    lax.fori_loop(0, held // once, step, 0)


def is_far(peers):
    return peers >= 4


def is_inner():
    z, peers = lax.axis_index("orb"), lax.axis_size("orb")
    if is_far(peers):
        return jnp.logical_and(z > 0, z < peers - 1)
    return z >= 0


def neighbour(distance):
    def place():
        z, peers = lax.axis_index("orb"), lax.axis_size("orb")
        number = z + distance
        return jnp.clip(number, 0, peers - 1), jnp.logical_and(number >= 0, number < peers)

    return place


def reflected(offset, inner):
    def place():
        z = lax.axis_index("orb")
        is_inner_one = jnp.logical_or(z == 1, z == 2)
        valid = z >= 0 if inner is None else is_inner_one == inner
        return lax.rem(offset + 4 - z, 4), valid

    return place


def beside():
    z = lax.axis_index("orb")
    return jnp.where(lax.rem(z, 2) == 0, z + 1, z - 1), z >= 0


def two_off(inner):
    def place():
        z = lax.axis_index("orb")
        return lax.rem(z + 2, 4), jnp.logical_or(z == 1, z == 2) == inner

    return place


def own_kernel(wanted, extra, green_ref, sigma_ref, *rest):
    acc_ref, keep_hi_ref, keep_lo_ref, hi_ref, lo_ref, *rest = rest[extra:]
    *sent, buf, self_ref, sem, sent_sem = rest
    rows, held = green_ref.shape[2], sigma_ref.shape[1]
    blocks = green_ref.shape[3] // BS
    begin, active = lax.axis_index("orb") * held, is_inner()

    def block_of(s):
        return lax.rem(begin + s, blocks)

    def fetch(s):
        col = pl.multiple_of(block_of(s) * BS, BS)
        return pltpu.make_async_copy(
            green_ref.at[0, :, :, pl.ds(col, BS)], buf.at[s], sem.at[s]
        )

    def store(s, carry):
        fetch(s).wait()
        lanes = pl.ds(pl.multiple_of(block_of(s) * 2 * BS, 2 * BS), 2 * BS)
        parts = halves(jnp.concatenate([buf[s, 0], buf[s, 1]], axis=1))
        for ref, part in zip((hi_ref, lo_ref), parts):
            ref[MARGIN : MARGIN + rows, lanes] = part
        return carry

    load = pltpu.make_async_copy(sigma_ref, self_ref, sem.at[blocks])
    load.start()
    for s in range(blocks):
        fetch(s).start()
    copies = []
    for n, ((size, start), out) in enumerate(zip(wanted, sent)):
        row = pl.multiple_of(start(lax.axis_index("orb"), rows), HALF)
        copies.append(
            pltpu.make_async_copy(green_ref.at[0, :, pl.ds(row, size), :], out, sent_sem.at[n])
        )
    for copy in copies:
        copy.start()
    acc_ref[...] = jnp.zeros_like(acc_ref)
    for ref in (hi_ref, lo_ref):
        ref[:MARGIN, :] = jnp.zeros((MARGIN, ref.shape[1]), BF16)
        ref[MARGIN + rows :, :] = jnp.zeros((MARGIN, ref.shape[1]), BF16)
    lax.fori_loop(0, held, store, 0)
    load.wait()
    shard_loop(begin, self_ref, hi_ref, lo_ref, acc_ref, (keep_hi_ref, keep_lo_ref), 0, active)
    lax.fori_loop(held, blocks, store, 0)
    for copy in copies:
        copy.wait()


def own_part(green, sigma, wanted, after):
    rows, held = green.shape[2], sigma.shape[1]
    tiles, blocks = rows // TILE, green.shape[3] // BS
    vmem = pl.BlockSpec(memory_space=pltpu.VMEM)
    hbm = pl.BlockSpec(memory_space=pl.ANY)
    keep = jax.ShapeDtypeStruct((held, 4 * MARGIN, 2 * BS), BF16)
    whole = jax.ShapeDtypeStruct((rows + 2 * MARGIN, blocks * 2 * BS), BF16)
    return pl.pallas_call(
        functools.partial(own_kernel, wanted, len(after)),
        out_shape=(
            jax.ShapeDtypeStruct((tiles, 2 * TILE, TILE + 2 * MARGIN), F32),
            keep,
            keep,
            whole,
            whole,
            *[jax.ShapeDtypeStruct((2, size, green.shape[3]), F32) for size, _ in wanted],
        ),
        in_specs=[hbm] * (2 + len(after)),
        out_specs=(vmem,) * (5 + len(wanted)),
        scratch_shapes=[
            pltpu.VMEM((blocks, 2, rows, BS), F32),
            pltpu.VMEM(sigma.shape, F32),
            pltpu.SemaphoreType.DMA((blocks + 1,)),
            pltpu.SemaphoreType.DMA((len(wanted),)),
        ],
        compiler_params=pltpu.CompilerParams(vmem_limit_bytes=40 << 20),
        cost_estimate=pl.CostEstimate(
            flops=held * rows * BS * BS,
            bytes_accessed=blocks * rows * BS,
            transcendentals=0,
        ),
        name="lesser_own",
    )(green, sigma, *after)


def lesser_kernel(places, held, extra, hi_ref, lo_ref, before_ref, *rest):
    sigmas, rest = rest[: len(places)], rest[len(places) :]
    rest = rest[extra:]
    acc_ref, keeps = rest[0], rest[1:]
    acc_ref[...] = before_ref[...]
    slot = 0
    for place, self_ref in zip(places, sigmas):
        number, valid = place()

        @pl.when(valid)
        def _():
            shard_loop(
                number * held, self_ref, hi_ref, lo_ref, acc_ref, keeps, slot, is_inner()
            )

        slot += self_ref.shape[1]


def lesser_part(hi, lo, before, shards, places, held, after=(), keep=True):
    vmem = pl.BlockSpec(memory_space=pltpu.VMEM)
    count = sum(x.shape[1] for x in shards)
    kept = jax.ShapeDtypeStruct((count, 4 * MARGIN, 2 * BS), BF16)
    outs = [jax.ShapeDtypeStruct(before.shape, F32)] + ([kept, kept] if keep else [])
    return pl.pallas_call(
        functools.partial(lesser_kernel, places, held, len(after)),
        out_shape=outs,
        in_specs=[vmem] * (3 + len(shards)) + [pl.BlockSpec(memory_space=pl.ANY)] * len(after),
        out_specs=[vmem] * len(outs),
        input_output_aliases={2: 0},
        compiler_params=pltpu.CompilerParams(vmem_limit_bytes=26 << 20),
        cost_estimate=pl.CostEstimate(
            flops=count * hi.shape[0] * BS * BS,
            bytes_accessed=before.size,
            transcendentals=0,
        ),
        name="lesser_more",
    )(hi, lo, before, *shards, *after)


def gate_kernel(*refs):
    del refs


def gate(arrays, after):
    hbm = pl.BlockSpec(memory_space=pl.ANY)
    return pl.pallas_call(
        gate_kernel,
        out_shape=[jax.ShapeDtypeStruct(x.shape, x.dtype) for x in arrays],
        in_specs=[hbm] * (len(arrays) + len(after)),
        out_specs=[hbm] * len(arrays),
        input_output_aliases={n: n for n in range(len(arrays))},
        compiler_params=pltpu.CompilerParams(vmem_limit_bytes=1 << 20),
        cost_estimate=pl.CostEstimate(flops=0, bytes_accessed=0, transcendentals=0),
        name="gate",
    )(*arrays, *after)


def edge_kernel(places, held, paired, *refs):
    halos, refs = refs[: 2 if paired else 3], refs[2 if paired else 3 :]
    keeps = refs[: 2 * len(places)]
    left_ref, right_ref, own_ref, acc_ref = refs[2 * len(places) :]
    z, peers = lax.axis_index("orb"), lax.axis_size("orb")
    if is_far(peers):
        from_left, from_right = z == 1, z == peers - 2
    else:
        from_left = from_right = z < 0
    limit = jnp.where(from_right, MARGIN, HALF)
    acc_ref[...] = jnp.zeros_like(acc_ref)

    def rows_of(part, cols):
        if not paired:
            return [ref[part, :, cols] for ref in halos]
        first, second = halos[0][part, :HALF, cols], halos[0][part, HALF:, cols]
        middle = halos[1][part, :, cols]
        return (
            jnp.where(from_left, first, second),
            jnp.where(from_left, second, middle),
            jnp.where(from_left, middle, first),
        )

    def add(number, hi, lo, at):
        cols = pl.ds(pl.multiple_of(number * held * BS, BS), held * BS)
        wide = [rows_of(part, cols) for part in range(2)]
        for side in range(2):
            fields = []
            for part in range(2):
                outer = jnp.where(from_left if side == 0 else from_right, wide[part][0], 0.0)
                inner = wide[part][1 + side]
                rows = [outer, inner] if side == 0 else [inner, outer]
                fields.append(halves(jnp.concatenate(rows, axis=0)))
            halo = []
            for real, imag in zip(*fields):
                lanes = []
                for s in range(held):
                    one = slice(s * BS, (s + 1) * BS)
                    lanes += [
                        jnp.concatenate([real[:, one], -imag[:, one]], axis=0),
                        jnp.concatenate([imag[:, one], real[:, one]], axis=0),
                    ]
                halo.append(jnp.concatenate(lanes, axis=1))
            rows = slice(side * TILE, (side + 1) * TILE)
            kept = [
                jnp.concatenate([ref[at + s, rows, :] for s in range(held)], axis=1)
                for ref in (hi, lo)
            ]
            acc_ref[side] = acc_ref[side] + dot3(halo, kept, NT)

    @pl.when(is_inner())
    def _():
        for k, shards in enumerate(places):
            for n, place in enumerate(shards):
                number, valid = place()
                if paired:
                    add(number, keeps[2 * k], keeps[2 * k + 1], n * held)
                    continue

                @pl.when(valid)
                def _():
                    add(number, keeps[2 * k], keeps[2 * k + 1], n * held)

    lane = lax.broadcasted_iota(jnp.int32, (MARGIN, LANES), 1)
    row = lax.broadcasted_iota(jnp.int32, (MARGIN, LANES), 0)
    low = lane < MARGIN
    left, right = acc_ref[0], acc_ref[1]
    turned_left, turned_right = left.T[:MARGIN], right.T[MARGIN:]
    for part in range(2):
        rows = slice(part * MARGIN, (part + 1) * MARGIN)
        sign = 1.0 - 2.0 * part
        to_left = jnp.where(low, 0.0, sign * left[rows])
        to_right = jnp.where(lane < limit, sign * right[rows], 0.0)
        if paired:
            to_left, to_right = (
                jnp.where(from_left, to_left, to_right),
                jnp.where(from_left, to_right, to_left),
            )
        left_ref[part] = to_left
        right_ref[part] = to_right
    own_ref[0, 0] = jnp.where(low, turned_left, 0.0)
    own_ref[0, 1] = jnp.where(low, pltpu.roll(turned_left, MARGIN, 1), 0.0)
    mine = jnp.logical_and(row < limit, lane >= MARGIN)
    own_ref[1, 0] = jnp.where(mine, pltpu.roll(turned_right, MARGIN, 1), 0.0)
    own_ref[1, 1] = jnp.where(mine, turned_right, 0.0)


def edge_part(halos, keeps, places, held, paired=False):
    vmem = pl.BlockSpec(memory_space=pltpu.VMEM)
    side = jax.ShapeDtypeStruct((2, MARGIN, LANES), F32)
    return pl.pallas_call(
        functools.partial(edge_kernel, places, held, paired),
        out_shape=(side, side, jax.ShapeDtypeStruct((2, 2, MARGIN, LANES), F32)),
        in_specs=[vmem] * (len(halos) + len(keeps)),
        out_specs=(vmem, vmem, vmem),
        scratch_shapes=[pltpu.VMEM((2, TILE, TILE), F32)],
        compiler_params=pltpu.CompilerParams(vmem_limit_bytes=20 << 20),
        cost_estimate=pl.CostEstimate(
            flops=1 << 31, bytes_accessed=8 << 20, transcendentals=0
        ),
        name="edges",
    )(*halos, *keeps)


def band_kernel(paired, acc_ref, own_ref, from_left_ref, from_right_ref, out_ref, rows_ref):
    tiles = acc_ref.shape[0]
    returned = [[ref[part] for part in range(2)] for ref in (from_left_ref, from_right_ref)]
    if paired:
        either = [x + y for x, y in zip(*returned)]
        high = lax.axis_index("orb") >= 2
        returned = [
            [jnp.where(high, x, 0.0) for x in either],
            [jnp.where(high, 0.0, x) for x in either],
        ]
    group = out_ref.shape[2]
    per_tile = TILE // W
    for t in range(tiles):
        for part in range(2):
            base = part * TILE
            x = acc_ref[t, base : base + TILE, :]
            rows_ref[t, part] = x
            if t == 0:
                extra = own_ref[0, part] + returned[0][part]
                rows_ref[t, part, :MARGIN, :LANES] = x[:MARGIN, :LANES] + extra
            if t == tiles - 1:
                extra = own_ref[1, part] + returned[1][part]
                rows_ref[t, part, MARGIN:, LANES:] = x[MARGIN:, LANES:] + extra
    low = lax.broadcasted_iota(jnp.int32, (W, LANES), 1) < MARGIN
    width = TILE + 2 * MARGIN
    for a in range(per_tile):
        for t in range(tiles):
            atom = t * per_tile + a
            for part in range(2):
                x = rows_ref[t, part, a * W : (a + 1) * W, :]
                before = pltpu.roll(x, (width - a * W) % width, 1)[:, :LANES]
                after = pltpu.roll(x, (width - (a + 1) * W) % width, 1)[:, :LANES]
                out_ref[atom // group, part, atom % group] = jnp.where(low, before, after)


def band(acc, own, from_left, from_right, energies, paired):
    tiles = acc.shape[0]
    atoms = tiles * TILE // W
    vmem = pl.BlockSpec(memory_space=pltpu.VMEM)
    return pl.pallas_call(
        functools.partial(band_kernel, paired),
        out_shape=jax.ShapeDtypeStruct((energies, 2, atoms // energies, W, LANES), F32),
        in_specs=[vmem] * 4,
        out_specs=vmem,
        scratch_shapes=[pltpu.VMEM((tiles, 2, TILE, TILE + 2 * MARGIN), F32)],
        compiler_params=pltpu.CompilerParams(vmem_limit_bytes=16 << 20),
        name="band",
    )(acc, own, from_left, from_right)


def scatter_kernel(
    recv_ref, where_ref, mix_ref, dham_ref, out_ref, smeared_ref, result_ref, factor_ref
):
    energies, _, group, _, _ = recv_ref.shape
    padded = dham_ref.shape[1]
    pairs = out_ref.shape[1]
    columns = [
        recv_ref[:, :, a, :, :].reshape(energies * 2 * W, LANES) for a in range(group)
    ]
    received = halves(jnp.concatenate(columns, axis=1))
    mixed = jnp.concatenate(halves(dot3(halves(mix_ref[...]), received, NN)), axis=0)
    rows = smeared_ref.shape[0]
    entry = lax.broadcasted_iota(jnp.int32, (group * LANES, padded), 0)
    offset = entry - where_ref[...] * W
    for j in range(0, W, 2):
        pick = jnp.concatenate(
            [jnp.where(offset == j + n, 1.0, 0.0).astype(BF16) for n in range(2)], axis=1
        )
        both = dot(mixed, pick, NN)
        smeared_ref[:, j * padded : (j + 2) * padded] = both[:rows] + both[rows:]
    for row in range(dham_ref.shape[0]):
        factor_ref[row] = jnp.broadcast_to(dham_ref[row : row + 1, :], (energies, padded))

    def block(part, j, k):
        row = (part * W + j) * energies
        return smeared_ref[row : row + energies, k * padded : (k + 1) * padded]

    for part in range(2):
        for i in range(W):
            total = [None] * W
            for c in range(3):
                factors = [factor_ref[(c * W + i) * W + j] for j in range(W)]
                for k in range(W):
                    t = None
                    for j in range(W):
                        term = factors[j] * block(part, j, k)
                        t = term if t is None else t + term
                    for l in range(W):
                        term = t * factor_ref[(c * W + l) * W + k]
                        total[l] = term if total[l] is None else total[l] + term
            for l in range(W):
                row = ((part * W + i) * W + l) * energies
                result_ref[row : row + energies, :] = total[l]
    for e in range(energies):
        one = result_ref[pl.ds(e, 2 * W * W, stride=energies), :]
        out_ref[e] = one.T[:pairs, :]


def scatter(recv, where, mix, dham, pairs):
    energies, _, group, _, _ = recv.shape
    padded = dham.shape[1]
    vmem = pl.BlockSpec(memory_space=pltpu.VMEM)
    return pl.pallas_call(
        scatter_kernel,
        out_shape=jax.ShapeDtypeStruct((energies, pairs, 2 * W * W), F32),
        in_specs=[vmem] * 4,
        out_specs=vmem,
        scratch_shapes=[
            pltpu.VMEM((2 * W * energies, W * padded), F32),
            pltpu.VMEM((2 * W * W * energies, padded), F32),
            pltpu.VMEM((dham.shape[0], energies, padded), F32),
        ],
        compiler_params=pltpu.CompilerParams(vmem_limit_bytes=24 << 20),
        name="scatter",
    )(recv, where, mix, dham)


def build_kernel(phonon_shift, phonon_weight, energies):
    rows_e = jnp.arange(energies, dtype=jnp.int32)[None, :, None]
    cols_f = jnp.arange(energies, dtype=jnp.int32)[None, None, :]
    shifts = phonon_shift[:, None, None]
    emission = (cols_f == rows_e + shifts).astype(F32)
    absorption = (cols_f == rows_e - shifts).astype(F32)
    terms = (
        phonon_weight[0][:, None, None] * emission + phonon_weight[1][:, None, None] * absorption
    )
    return jnp.sum(terms, axis=0)


def build_mix(phonon_shift, phonon_weight, energies):
    kernel = build_kernel(phonon_shift, phonon_weight, energies)
    same = jnp.eye(2 * W, dtype=F32)
    mix = same[:, None, None, :] * kernel[None, :, :, None]
    return mix.reshape(2 * W * energies, energies * 2 * W)


def send(x, pairs):
    return lax.ppermute(x, "orb", pairs)


def per_device(green, sigma, neighbours, phonon_shift, phonon_weight, dham):
    energies = lax.axis_size("energy")
    peers = lax.axis_size("orb")
    e, z = lax.axis_index("energy"), lax.axis_index("orb")
    rows = green.shape[2]
    atoms = rows // W
    degree = neighbours.shape[1]
    group = atoms // energies
    pairs = group * degree
    padded = -(-pairs // LANES) * LANES
    held = sigma.shape[1]

    far, paired = is_far(peers), peers == 4
    up = [(i, i + 1) for i in range(peers - 1)]
    down = [(i + 1, i) for i in range(peers - 1)]
    fixed = pltpu.with_memory_space_constraint(green, pltpu.HBM)
    if paired:
        ends, middle, outward = [(0, 1), (3, 2)], [(1, 2), (2, 1)], [(1, 0), (2, 3)]
        aside, across = send(sigma, ends + outward), send(sigma, middle)
        wanted = [
            (MARGIN, lambda z, rows: jnp.where(z == 0, rows - MARGIN, 0)),
            (HALF, lambda z, rows: jnp.where(z == 1, rows - HALF, 0)),
        ]
    else:
        right, left = send(sigma, up), send(sigma, down)
        wanted = [
            (HALF, lambda z, rows: jnp.where(z == 0, rows - MARGIN, HALF)),
            (HALF, lambda z, rows: rows - HALF),
            (HALF, lambda z, rows: 0 * z),
        ]

    mine = lax.dynamic_slice_in_dim(neighbours, e * group, group, axis=0)
    first = z * atoms + e * group
    offset = mine - (first + jnp.arange(group, dtype=jnp.int32))[:, None]
    column = jnp.where(offset < 0, offset + REACH, offset + REACH - 1)
    where = column + 2 * REACH * jnp.arange(group, dtype=jnp.int32)[:, None]
    where = jnp.pad(where.reshape(1, pairs), ((0, 0), (0, padded - pairs)), constant_values=-1)
    mix = build_mix(phonon_shift, phonon_weight, energies)
    factors = lax.dynamic_slice_in_dim(
        dham.transpose(1, 2, 3, 0).reshape(3 * W * W, -1), e * pairs, pairs, axis=1
    )
    factors = jnp.pad(factors, ((0, 0), (0, padded - pairs)))


    acc, keep_hi, keep_lo, hi, lo, outer, near, *nearer = own_part(
        fixed,
        pltpu.with_memory_space_constraint(sigma, pltpu.HBM),
        wanted,
        [where, mix, factors],
    )
    keeps = [keep_hi, keep_lo]
    more = functools.partial(lesser_part, hi, lo, held=held)
    places = [[neighbour(0)]]
    if paired:
        aside, across = gate([aside, across], [keeps[-1]])
        second_across, second_aside = send(aside, middle), send(across, outward)
        halos = [send(outer, ends), send(near, middle)]
        places.append([beside, reflected(3, True)])
        acc, *kept = more(acc, [aside, across], places[-1])
        keeps += kept
        (second_across,) = gate([second_across], [kept[-1]])
        third_aside = send(second_across, outward)
        places.append([two_off(True), two_off(False)])
        acc, *kept = more(acc, [second_across, second_aside], places[-1])
        keeps += kept
        to_end, to_middle, own = edge_part(
            halos, keeps, [*places[:-1], places[-1][:1]], held, True
        )
        back_left, back_right = send(to_end, outward), send(to_middle, middle)
        (acc,) = more(acc, [third_aside], [reflected(3, False)], after=[to_end], keep=False)
    else:
        near_right = send(near, up[:-1] if far else up)
        near_left = send(nearer[0], down[1:] if far else down)
        if far:
            other = send(outer, [(0, 1), (peers - 1, peers - 2)])
        else:
            other = jnp.zeros_like(near_left)
        for k in range(1, peers):
            around = [neighbour(-k), neighbour(k)]
            if k < peers - 1:
                right, left = gate([right, left], [keeps[-1], outer if k == 1 else other])
                following = send(right, up[k:]), send(left, down[: peers - 1 - k])
                after = []
            else:
                if not far:
                    acc, *kept = more(acc, [right, left], around)
                    keeps += kept
                    places.append(around)
                to_left, to_right, own = edge_part(
                    [other, near_right, near_left], keeps, places, held
                )
                back_right = send(to_left, down[:-1] if far else down)
                back_left = send(to_right, up[1:] if far else up)
                after = [to_left]
                if not far:
                    break
            acc, *kept = more(acc, [right, left], around, after=after, keep=k < peers - 1)
            keeps += kept
            places.append(around)
            if k < peers - 1:
                right, left = following
    lesser = band(acc, own, back_left, back_right, energies, paired)

    recv = lax.all_to_all(lesser, "energy", split_axis=0, concat_axis=0, tiled=True)
    spread = scatter(recv, where, mix, factors, pairs)
    result = lax.all_to_all(spread, "energy", split_axis=0, concat_axis=0, tiled=True)
    return result.reshape(1, atoms * degree, 2 * W * W)


def solution(mesh):
    return jax.shard_map(
        per_device,
        mesh=mesh,
        in_specs=(
            P("energy", None, "orb", None),
            P("energy", "orb", None, None, None),
            P("orb", None),
            P(),
            P(),
            P("orb", None, None, None),
        ),
        out_specs=P("energy", "orb", None),
        check_vma=False,
    )
```

```python
import functools

import jax
import jax.numpy as jnp
from jax import lax
from jax.experimental import pallas as pl
from jax.experimental.pallas import tpu as pltpu
from jax.sharding import PartitionSpec as P

W = 8
BS = 128
REACH = 8
MARGIN = REACH * W
HALF = MARGIN // 2
TILE = 128
LANES = 128
F32, BF16 = jnp.float32, jnp.bfloat16

NT = (((1,), (1,)), ((), ()))
NN = (((1,), (0,)), ((), ()))


def halves(x):
    hi = x.astype(BF16)
    return hi, (x - hi.astype(F32)).astype(BF16)


def dot(a, b, dims):
    return lax.dot_general(a, b, dims, preferred_element_type=F32)


def dot3(a, b, dims):
    left = jnp.concatenate([a[0], a[0], a[1]], axis=1)
    right = jnp.concatenate([b[0], b[1], b[0]], axis=dims[0][1][0])
    return dot(left, right, dims)


def blocks_at_once(held):
    return 2 if held % 2 == 0 else 1


def some_blocks(lane, weights, hi_ref, lo_ref, acc_ref, edges, active):
    rows = hi_ref.shape[0] - 2 * MARGIN
    wide = 2 * BS
    split, products = [], []
    for n, (real, imag) in enumerate(weights):
        top = jnp.concatenate([real, imag], axis=1)
        weight = halves(jnp.concatenate([top, jnp.concatenate([-imag, real], axis=1)], axis=0))
        cols = pl.ds(lane + n * wide, wide)
        own = [ref[MARGIN : MARGIN + rows, cols] for ref in (hi_ref, lo_ref)]
        product = halves(dot3(own, weight, NN))
        for ref, part in zip(edges, product):
            ref[n, :MARGIN, :] = part[:MARGIN]
            ref[n, 3 * MARGIN :, :] = part[rows - MARGIN :]
        split.append(weight)
        products.append(product)
    cols = pl.ds(lane, len(weights) * wide)
    for t in range(rows // TILE):
        both = []
        for part in zip(*products):
            lanes = []
            for x in part:
                x = x[t * TILE : (t + 1) * TILE]
                turned = jnp.concatenate([x[:, BS:], -x[:, :BS]], axis=1)
                lanes.append(jnp.concatenate([x, turned], axis=0))
            both.append(jnp.concatenate(lanes, axis=1))
        near = pl.ds(t * TILE, TILE + 2 * MARGIN)
        acc_ref[t] = acc_ref[t] + dot3(both, (hi_ref[near, cols], lo_ref[near, cols]), NT)

    if not edges:
        return

    @pl.when(active)
    def _():
        for n, weight in enumerate(split):
            one = pl.ds(lane + n * wide, wide)
            outer = [
                jnp.concatenate(
                    [ref[MARGIN : 2 * MARGIN, one], ref[rows : rows + MARGIN, one]], axis=0
                )
                for ref in (hi_ref, lo_ref)
            ]
            for ref, part in zip(edges, halves(dot3(outer, weight, NT))):
                ref[n, MARGIN : 3 * MARGIN, :] = part


def shard_loop(first_block, self_ref, hi_ref, lo_ref, acc_ref, keeps, slot, active):
    held = self_ref.shape[1]
    once = blocks_at_once(held)

    def step(g, carry):
        lane = pl.multiple_of((first_block + g * once) * 2 * BS, 2 * BS)
        weights = [
            (self_ref[0, g * once + n, 0], self_ref[0, g * once + n, 1]) for n in range(once)
        ]
        slots = pl.ds(slot + g * once, once)
        kept = tuple(ref.at[slots] for ref in keeps)
        some_blocks(lane, weights, hi_ref, lo_ref, acc_ref, kept, active)
        return carry

    lax.fori_loop(0, held // once, step, 0)


def is_far(peers):
    return peers >= 4


def is_inner():
    z, peers = lax.axis_index("orb"), lax.axis_size("orb")
    if is_far(peers):
        return jnp.logical_and(z > 0, z < peers - 1)
    return z >= 0


def neighbour(distance):
    def place():
        z, peers = lax.axis_index("orb"), lax.axis_size("orb")
        number = z + distance
        return jnp.clip(number, 0, peers - 1), jnp.logical_and(number >= 0, number < peers)

    return place


def reflected(offset, inner):
    def place():
        z = lax.axis_index("orb")
        is_inner_one = jnp.logical_or(z == 1, z == 2)
        valid = z >= 0 if inner is None else is_inner_one == inner
        return lax.rem(offset + 4 - z, 4), valid

    return place


def beside():
    z = lax.axis_index("orb")
    return jnp.where(lax.rem(z, 2) == 0, z + 1, z - 1), z >= 0


def two_off(inner):
    def place():
        z = lax.axis_index("orb")
        return lax.rem(z + 2, 4), jnp.logical_or(z == 1, z == 2) == inner

    return place


def own_kernel(wanted, extra, green_ref, sigma_ref, *rest):
    acc_ref, keep_hi_ref, keep_lo_ref, hi_ref, lo_ref, *rest = rest[extra:]
    *sent, buf, self_ref, sem, sent_sem = rest
    rows, held = green_ref.shape[2], sigma_ref.shape[1]
    blocks = green_ref.shape[3] // BS
    begin, active = lax.axis_index("orb") * held, is_inner()

    def block_of(s):
        return lax.rem(begin + s, blocks)

    def fetch(s):
        col = pl.multiple_of(block_of(s) * BS, BS)
        return pltpu.make_async_copy(
            green_ref.at[0, :, :, pl.ds(col, BS)], buf.at[s], sem.at[s]
        )

    def store(s, carry):
        fetch(s).wait()
        lanes = pl.ds(pl.multiple_of(block_of(s) * 2 * BS, 2 * BS), 2 * BS)
        parts = halves(jnp.concatenate([buf[s, 0], buf[s, 1]], axis=1))
        for ref, part in zip((hi_ref, lo_ref), parts):
            ref[MARGIN : MARGIN + rows, lanes] = part
        return carry

    load = pltpu.make_async_copy(sigma_ref, self_ref, sem.at[blocks])
    load.start()
    for s in range(blocks):
        fetch(s).start()
    copies = []
    for n, ((size, start), out) in enumerate(zip(wanted, sent)):
        row = pl.multiple_of(start(lax.axis_index("orb"), rows), HALF)
        copies.append(
            pltpu.make_async_copy(green_ref.at[0, :, pl.ds(row, size), :], out, sent_sem.at[n])
        )
    for copy in copies:
        copy.start()
    acc_ref[...] = jnp.zeros_like(acc_ref)
    for ref in (hi_ref, lo_ref):
        ref[:MARGIN, :] = jnp.zeros((MARGIN, ref.shape[1]), BF16)
        ref[MARGIN + rows :, :] = jnp.zeros((MARGIN, ref.shape[1]), BF16)
    lax.fori_loop(0, held, store, 0)
    load.wait()
    shard_loop(begin, self_ref, hi_ref, lo_ref, acc_ref, (keep_hi_ref, keep_lo_ref), 0, active)
    lax.fori_loop(held, blocks, store, 0)
    for copy in copies:
        copy.wait()


def own_part(green, sigma, wanted, after):
    rows, held = green.shape[2], sigma.shape[1]
    tiles, blocks = rows // TILE, green.shape[3] // BS
    vmem = pl.BlockSpec(memory_space=pltpu.VMEM)
    hbm = pl.BlockSpec(memory_space=pl.ANY)
    keep = jax.ShapeDtypeStruct((held, 4 * MARGIN, 2 * BS), BF16)
    whole = jax.ShapeDtypeStruct((rows + 2 * MARGIN, blocks * 2 * BS), BF16)
    return pl.pallas_call(
        functools.partial(own_kernel, wanted, len(after)),
        out_shape=(
            jax.ShapeDtypeStruct((tiles, 2 * TILE, TILE + 2 * MARGIN), F32),
            keep,
            keep,
            whole,
            whole,
            *[jax.ShapeDtypeStruct((2, size, green.shape[3]), F32) for size, _ in wanted],
        ),
        in_specs=[hbm] * (2 + len(after)),
        out_specs=(vmem,) * (5 + len(wanted)),
        scratch_shapes=[
            pltpu.VMEM((blocks, 2, rows, BS), F32),
            pltpu.VMEM(sigma.shape, F32),
            pltpu.SemaphoreType.DMA((blocks + 1,)),
            pltpu.SemaphoreType.DMA((len(wanted),)),
        ],
        compiler_params=pltpu.CompilerParams(vmem_limit_bytes=40 << 20),
        cost_estimate=pl.CostEstimate(
            flops=held * rows * BS * BS,
            bytes_accessed=blocks * rows * BS,
            transcendentals=0,
        ),
        name="lesser_own",
    )(green, sigma, *after)


def lesser_kernel(places, held, extra, hi_ref, lo_ref, before_ref, *rest):
    sigmas, rest = rest[: len(places)], rest[len(places) :]
    rest = rest[extra:]
    acc_ref, keeps = rest[0], rest[1:]
    acc_ref[...] = before_ref[...]
    slot = 0
    for place, self_ref in zip(places, sigmas):
        number, valid = place()

        @pl.when(valid)
        def _():
            shard_loop(
                number * held, self_ref, hi_ref, lo_ref, acc_ref, keeps, slot, is_inner()
            )

        slot += self_ref.shape[1]


def lesser_part(hi, lo, before, shards, places, held, after=(), keep=True):
    vmem = pl.BlockSpec(memory_space=pltpu.VMEM)
    count = sum(x.shape[1] for x in shards)
    kept = jax.ShapeDtypeStruct((count, 4 * MARGIN, 2 * BS), BF16)
    outs = [jax.ShapeDtypeStruct(before.shape, F32)] + ([kept, kept] if keep else [])
    return pl.pallas_call(
        functools.partial(lesser_kernel, places, held, len(after)),
        out_shape=outs,
        in_specs=[vmem] * (3 + len(shards)) + [pl.BlockSpec(memory_space=pl.ANY)] * len(after),
        out_specs=[vmem] * len(outs),
        input_output_aliases={2: 0},
        compiler_params=pltpu.CompilerParams(vmem_limit_bytes=26 << 20),
        cost_estimate=pl.CostEstimate(
            flops=count * hi.shape[0] * BS * BS,
            bytes_accessed=before.size,
            transcendentals=0,
        ),
        name="lesser_more",
    )(hi, lo, before, *shards, *after)


def gate_kernel(*refs):
    del refs


def gate(arrays, after):
    hbm = pl.BlockSpec(memory_space=pl.ANY)
    return pl.pallas_call(
        gate_kernel,
        out_shape=[jax.ShapeDtypeStruct(x.shape, x.dtype) for x in arrays],
        in_specs=[hbm] * (len(arrays) + len(after)),
        out_specs=[hbm] * len(arrays),
        input_output_aliases={n: n for n in range(len(arrays))},
        compiler_params=pltpu.CompilerParams(vmem_limit_bytes=1 << 20),
        cost_estimate=pl.CostEstimate(flops=0, bytes_accessed=0, transcendentals=0),
        name="gate",
    )(*arrays, *after)


def edge_kernel(places, held, *refs):
    halos, refs = refs[:3], refs[3:]
    keeps = refs[: 2 * len(places)]
    left_ref, right_ref, own_ref, acc_ref = refs[2 * len(places) :]
    z, peers = lax.axis_index("orb"), lax.axis_size("orb")
    if is_far(peers):
        from_left, from_right = z == 1, z == peers - 2
    else:
        from_left = from_right = z < 0
    limit = jnp.where(from_right, MARGIN, HALF)
    acc_ref[...] = jnp.zeros_like(acc_ref)

    def rows_of(part, cols):
        return [ref[part, :, cols] for ref in halos]

    def add(number, hi, lo, at):
        cols = pl.ds(pl.multiple_of(number * held * BS, BS), held * BS)
        wide = [rows_of(part, cols) for part in range(2)]
        for side in range(2):
            fields = []
            for part in range(2):
                outer = jnp.where(from_left if side == 0 else from_right, wide[part][0], 0.0)
                inner = wide[part][1 + side]
                rows = [outer, inner] if side == 0 else [inner, outer]
                fields.append(halves(jnp.concatenate(rows, axis=0)))
            halo = []
            for real, imag in zip(*fields):
                lanes = []
                for s in range(held):
                    one = slice(s * BS, (s + 1) * BS)
                    lanes += [
                        jnp.concatenate([real[:, one], -imag[:, one]], axis=0),
                        jnp.concatenate([imag[:, one], real[:, one]], axis=0),
                    ]
                halo.append(jnp.concatenate(lanes, axis=1))
            rows = slice(side * TILE, (side + 1) * TILE)
            kept = [
                jnp.concatenate([ref[at + s, rows, :] for s in range(held)], axis=1)
                for ref in (hi, lo)
            ]
            acc_ref[side] = acc_ref[side] + dot3(halo, kept, NT)

    @pl.when(is_inner())
    def _():
        for k, shards in enumerate(places):
            for n, place in enumerate(shards):
                number, valid = place()

                @pl.when(valid)
                def _():
                    add(number, keeps[2 * k], keeps[2 * k + 1], n * held)

    lane = lax.broadcasted_iota(jnp.int32, (MARGIN, LANES), 1)
    row = lax.broadcasted_iota(jnp.int32, (MARGIN, LANES), 0)
    low = lane < MARGIN
    left, right = acc_ref[0], acc_ref[1]
    turned_left, turned_right = left.T[:MARGIN], right.T[MARGIN:]
    for part in range(2):
        rows = slice(part * MARGIN, (part + 1) * MARGIN)
        sign = 1.0 - 2.0 * part
        to_left = jnp.where(low, 0.0, sign * left[rows])
        to_right = jnp.where(lane < limit, sign * right[rows], 0.0)
        left_ref[part] = to_left
        right_ref[part] = to_right
    own_ref[0, 0] = jnp.where(low, turned_left, 0.0)
    own_ref[0, 1] = jnp.where(low, pltpu.roll(turned_left, MARGIN, 1), 0.0)
    mine = jnp.logical_and(row < limit, lane >= MARGIN)
    own_ref[1, 0] = jnp.where(mine, pltpu.roll(turned_right, MARGIN, 1), 0.0)
    own_ref[1, 1] = jnp.where(mine, turned_right, 0.0)


def edge_part(halos, keeps, places, held):
    vmem = pl.BlockSpec(memory_space=pltpu.VMEM)
    side = jax.ShapeDtypeStruct((2, MARGIN, LANES), F32)
    return pl.pallas_call(
        functools.partial(edge_kernel, places, held),
        out_shape=(side, side, jax.ShapeDtypeStruct((2, 2, MARGIN, LANES), F32)),
        in_specs=[vmem] * (len(halos) + len(keeps)),
        out_specs=(vmem, vmem, vmem),
        scratch_shapes=[pltpu.VMEM((2, TILE, TILE), F32)],
        compiler_params=pltpu.CompilerParams(vmem_limit_bytes=20 << 20),
        cost_estimate=pl.CostEstimate(
            flops=1 << 31, bytes_accessed=8 << 20, transcendentals=0
        ),
        name="edges",
    )(*halos, *keeps)


def pair_edge_kernel(middle, shards, held, *refs):
    halo_ref, keeps, refs = refs[0], refs[1 : 1 + 2 * len(shards)], refs[1 + 2 * len(shards) :]
    if middle:
        before_ref, refs = refs[0], refs[1:]
    send_ref, own_ref, acc_ref = refs
    z = lax.axis_index("orb")
    on_left = (z == 2) if middle else (z == 1)
    count = halo_ref.shape[1]
    begin = pl.multiple_of(jnp.where(on_left, 0, TILE), TILE)
    acc_ref[...] = jnp.zeros_like(acc_ref)

    @pl.when(is_inner())
    def _():
        for k, group in enumerate(shards):
            for n, place in enumerate(group):
                number, _ = place()
                cols = pl.ds(pl.multiple_of(number * held * BS, BS), held * BS)
                fields = [halves(halo_ref[part, :, cols]) for part in range(2)]
                halo = []
                for real, imag in zip(*fields):
                    lanes = []
                    for s in range(held):
                        one = slice(s * BS, (s + 1) * BS)
                        lanes += [
                            jnp.concatenate([real[:, one], -imag[:, one]], axis=0),
                            jnp.concatenate([imag[:, one], real[:, one]], axis=0),
                        ]
                    halo.append(jnp.concatenate(lanes, axis=1))
                kept = [
                    jnp.concatenate(
                        [ref[n * held + s, pl.ds(begin, TILE), :] for s in range(held)], axis=1
                    )
                    for ref in keeps[2 * k : 2 * k + 2]
                ]
                acc_ref[...] = acc_ref[...] + dot3(halo, kept, NT)

    limit = HALF if middle else MARGIN
    lane = lax.broadcasted_iota(jnp.int32, (MARGIN, LANES), 1)
    row = lax.broadcasted_iota(jnp.int32, (MARGIN, LANES), 0)
    low = lane < MARGIN
    mine = jnp.logical_and(row < limit, lane >= MARGIN)
    parts = [acc_ref[part * count : (part + 1) * count, :] for part in range(2)]
    if middle:
        none = jnp.zeros((MARGIN - count, LANES), F32)
        parts = [
            jnp.where(
                on_left,
                jnp.concatenate([none, x], axis=0),
                jnp.concatenate([x, none], axis=0),
            )
            for x in parts
        ]
    for part, sign in enumerate((1.0, -1.0)):
        x = sign * parts[part]
        send_ref[part] = jnp.where(
            on_left, jnp.where(low, 0.0, x), jnp.where(lane < limit, x, 0.0)
        )
    turned = jnp.concatenate(parts, axis=0).T
    left, right = turned[:MARGIN], turned[MARGIN:]
    lefts = left, pltpu.roll(left, MARGIN, 1)
    rights = pltpu.roll(right, MARGIN, 1), right
    for part in range(2):
        own = [
            jnp.where(on_left, jnp.where(low, lefts[part], 0.0), 0.0),
            jnp.where(on_left, 0.0, jnp.where(mine, rights[part], 0.0)),
        ]
        for side in range(2):
            own_ref[side, part] = own[side] + (before_ref[side, part] if middle else 0.0)


def pair_edge_part(halo, keeps, shards, held, before=None):
    vmem = pl.BlockSpec(memory_space=pltpu.VMEM)
    middle = before is not None
    args = [halo, *keeps] + ([before] if middle else [])
    return pl.pallas_call(
        functools.partial(pair_edge_kernel, middle, shards, held),
        out_shape=(
            jax.ShapeDtypeStruct((2, MARGIN, LANES), F32),
            jax.ShapeDtypeStruct((2, 2, MARGIN, LANES), F32),
        ),
        in_specs=[vmem] * len(args),
        out_specs=(vmem, vmem),
        scratch_shapes=[pltpu.VMEM((2 * halo.shape[1], TILE), F32)],
        compiler_params=pltpu.CompilerParams(vmem_limit_bytes=20 << 20),
        cost_estimate=pl.CostEstimate(flops=1 << 30, bytes_accessed=4 << 20, transcendentals=0),
        name="edge_middle" if middle else "edge_end",
    )(*args)


def band_kernel(paired, acc_ref, own_ref, from_left_ref, from_right_ref, out_ref, rows_ref):
    tiles = acc_ref.shape[0]
    returned = [[ref[part] for part in range(2)] for ref in (from_left_ref, from_right_ref)]
    if paired:
        either = [x + y for x, y in zip(*returned)]
        high = lax.axis_index("orb") >= 2
        returned = [
            [jnp.where(high, x, 0.0) for x in either],
            [jnp.where(high, 0.0, x) for x in either],
        ]
    group = out_ref.shape[2]
    per_tile = TILE // W
    for t in range(tiles):
        for part in range(2):
            base = part * TILE
            x = acc_ref[t, base : base + TILE, :]
            rows_ref[t, part] = x
            if t == 0:
                extra = own_ref[0, part] + returned[0][part]
                rows_ref[t, part, :MARGIN, :LANES] = x[:MARGIN, :LANES] + extra
            if t == tiles - 1:
                extra = own_ref[1, part] + returned[1][part]
                rows_ref[t, part, MARGIN:, LANES:] = x[MARGIN:, LANES:] + extra
    low = lax.broadcasted_iota(jnp.int32, (W, LANES), 1) < MARGIN
    width = TILE + 2 * MARGIN
    for a in range(per_tile):
        for t in range(tiles):
            atom = t * per_tile + a
            for part in range(2):
                x = rows_ref[t, part, a * W : (a + 1) * W, :]
                before = pltpu.roll(x, (width - a * W) % width, 1)[:, :LANES]
                after = pltpu.roll(x, (width - (a + 1) * W) % width, 1)[:, :LANES]
                out_ref[atom // group, part, atom % group] = jnp.where(low, before, after)


def band(acc, own, from_left, from_right, energies, paired):
    tiles = acc.shape[0]
    atoms = tiles * TILE // W
    vmem = pl.BlockSpec(memory_space=pltpu.VMEM)
    return pl.pallas_call(
        functools.partial(band_kernel, paired),
        out_shape=jax.ShapeDtypeStruct((energies, 2, atoms // energies, W, LANES), F32),
        in_specs=[vmem] * 4,
        out_specs=vmem,
        scratch_shapes=[pltpu.VMEM((tiles, 2, TILE, TILE + 2 * MARGIN), F32)],
        compiler_params=pltpu.CompilerParams(vmem_limit_bytes=16 << 20),
        name="band",
    )(acc, own, from_left, from_right)


def scatter_kernel(
    recv_ref, where_ref, mix_ref, dham_ref, out_ref, smeared_ref, result_ref, factor_ref
):
    energies, _, group, _, _ = recv_ref.shape
    padded = dham_ref.shape[1]
    pairs = out_ref.shape[1]
    columns = [
        recv_ref[:, :, a, :, :].reshape(energies * 2 * W, LANES) for a in range(group)
    ]
    received = halves(jnp.concatenate(columns, axis=1))
    mixed = jnp.concatenate(halves(dot3(halves(mix_ref[...]), received, NN)), axis=0)
    rows = smeared_ref.shape[0]
    entry = lax.broadcasted_iota(jnp.int32, (group * LANES, padded), 0)
    offset = entry - where_ref[...] * W
    for j in range(0, W, 2):
        pick = jnp.concatenate(
            [jnp.where(offset == j + n, 1.0, 0.0).astype(BF16) for n in range(2)], axis=1
        )
        both = dot(mixed, pick, NN)
        smeared_ref[:, j * padded : (j + 2) * padded] = both[:rows] + both[rows:]
    for row in range(dham_ref.shape[0]):
        factor_ref[row] = jnp.broadcast_to(dham_ref[row : row + 1, :], (energies, padded))

    def block(part, j, k):
        row = (part * W + j) * energies
        return smeared_ref[row : row + energies, k * padded : (k + 1) * padded]

    for part in range(2):
        for i in range(W):
            total = [None] * W
            for c in range(3):
                factors = [factor_ref[(c * W + i) * W + j] for j in range(W)]
                for k in range(W):
                    t = None
                    for j in range(W):
                        term = factors[j] * block(part, j, k)
                        t = term if t is None else t + term
                    for l in range(W):
                        term = t * factor_ref[(c * W + l) * W + k]
                        total[l] = term if total[l] is None else total[l] + term
            for l in range(W):
                row = ((part * W + i) * W + l) * energies
                result_ref[row : row + energies, :] = total[l]
    for e in range(energies):
        one = result_ref[pl.ds(e, 2 * W * W, stride=energies), :]
        out_ref[e] = one.T[:pairs, :]


def scatter(recv, where, mix, dham, pairs):
    energies, _, group, _, _ = recv.shape
    padded = dham.shape[1]
    vmem = pl.BlockSpec(memory_space=pltpu.VMEM)
    return pl.pallas_call(
        scatter_kernel,
        out_shape=jax.ShapeDtypeStruct((energies, pairs, 2 * W * W), F32),
        in_specs=[vmem] * 4,
        out_specs=vmem,
        scratch_shapes=[
            pltpu.VMEM((2 * W * energies, W * padded), F32),
            pltpu.VMEM((2 * W * W * energies, padded), F32),
            pltpu.VMEM((dham.shape[0], energies, padded), F32),
        ],
        compiler_params=pltpu.CompilerParams(vmem_limit_bytes=24 << 20),
        name="scatter",
    )(recv, where, mix, dham)


def build_kernel(phonon_shift, phonon_weight, energies):
    rows_e = jnp.arange(energies, dtype=jnp.int32)[None, :, None]
    cols_f = jnp.arange(energies, dtype=jnp.int32)[None, None, :]
    shifts = phonon_shift[:, None, None]
    emission = (cols_f == rows_e + shifts).astype(F32)
    absorption = (cols_f == rows_e - shifts).astype(F32)
    terms = (
        phonon_weight[0][:, None, None] * emission + phonon_weight[1][:, None, None] * absorption
    )
    return jnp.sum(terms, axis=0)


def build_mix(phonon_shift, phonon_weight, energies):
    kernel = build_kernel(phonon_shift, phonon_weight, energies)
    same = jnp.eye(2 * W, dtype=F32)
    mix = same[:, None, None, :] * kernel[None, :, :, None]
    return mix.reshape(2 * W * energies, energies * 2 * W)


def send(x, pairs):
    return lax.ppermute(x, "orb", pairs)


def per_device(green, sigma, neighbours, phonon_shift, phonon_weight, dham):
    energies = lax.axis_size("energy")
    peers = lax.axis_size("orb")
    e, z = lax.axis_index("energy"), lax.axis_index("orb")
    rows = green.shape[2]
    atoms = rows // W
    degree = neighbours.shape[1]
    group = atoms // energies
    pairs = group * degree
    padded = -(-pairs // LANES) * LANES
    held = sigma.shape[1]

    far, paired = is_far(peers), peers == 4
    up = [(i, i + 1) for i in range(peers - 1)]
    down = [(i + 1, i) for i in range(peers - 1)]
    fixed = pltpu.with_memory_space_constraint(green, pltpu.HBM)
    if paired:
        ends, middle, outward = [(0, 1), (3, 2)], [(1, 2), (2, 1)], [(1, 0), (2, 3)]
        aside, across = send(sigma, ends + outward), send(sigma, middle)
        wanted = [
            (MARGIN, lambda z, rows: jnp.where(z == 0, rows - MARGIN, 0)),
            (HALF, lambda z, rows: jnp.where(z == 1, rows - HALF, 0)),
        ]
    else:
        right, left = send(sigma, up), send(sigma, down)
        wanted = [
            (HALF, lambda z, rows: jnp.where(z == 0, rows - MARGIN, HALF)),
            (HALF, lambda z, rows: rows - HALF),
            (HALF, lambda z, rows: 0 * z),
        ]

    mine = lax.dynamic_slice_in_dim(neighbours, e * group, group, axis=0)
    first = z * atoms + e * group
    offset = mine - (first + jnp.arange(group, dtype=jnp.int32))[:, None]
    column = jnp.where(offset < 0, offset + REACH, offset + REACH - 1)
    where = column + 2 * REACH * jnp.arange(group, dtype=jnp.int32)[:, None]
    where = jnp.pad(where.reshape(1, pairs), ((0, 0), (0, padded - pairs)), constant_values=-1)
    mix = build_mix(phonon_shift, phonon_weight, energies)
    factors = lax.dynamic_slice_in_dim(
        dham.transpose(1, 2, 3, 0).reshape(3 * W * W, -1), e * pairs, pairs, axis=1
    )
    factors = jnp.pad(factors, ((0, 0), (0, padded - pairs)))


    acc, keep_hi, keep_lo, hi, lo, outer, near, *nearer = own_part(
        fixed,
        pltpu.with_memory_space_constraint(sigma, pltpu.HBM),
        wanted,
        [where, mix, factors],
    )
    keeps = [keep_hi, keep_lo]
    more = functools.partial(lesser_part, hi, lo, held=held)
    places = [[neighbour(0)]]
    if paired:
        (aside,) = gate([aside], [keeps[-1]])
        (across,) = gate([across], [aside])
        second_across, second_aside = send(aside, middle), send(across, outward)
        halos = [send(outer, ends), send(near, middle)]
        places.append([beside, reflected(3, True)])
        acc, *kept = more(acc, [aside, across], places[-1])
        keeps += kept
        (second_across,) = gate([second_across], [kept[-1]])
        third_aside = send(second_across, outward)
        places.append([two_off(True), two_off(False)])
        acc, *kept = more(acc, [second_across, second_aside], places[-1])
        keeps += kept
        shards = [*places[:-1], places[-1][:1]]
        to_end, own = pair_edge_part(halos[0], keeps, shards, held)
        back_left = send(to_end, outward)
        to_middle, own = pair_edge_part(halos[1], keeps, shards, held, own)
        back_right = send(to_middle, middle)
        (acc,) = more(acc, [third_aside], [reflected(3, False)], after=[to_middle], keep=False)
    else:
        near_right = send(near, up[:-1] if far else up)
        near_left = send(nearer[0], down[1:] if far else down)
        if far:
            other = send(outer, [(0, 1), (peers - 1, peers - 2)])
        else:
            other = jnp.zeros_like(near_left)
        for k in range(1, peers):
            around = [neighbour(-k), neighbour(k)]
            if k < peers - 1:
                right, left = gate([right, left], [keeps[-1], outer if k == 1 else other])
                following = send(right, up[k:]), send(left, down[: peers - 1 - k])
                after = []
            else:
                if not far:
                    acc, *kept = more(acc, [right, left], around)
                    keeps += kept
                    places.append(around)
                to_left, to_right, own = edge_part(
                    [other, near_right, near_left], keeps, places, held
                )
                back_right = send(to_left, down[:-1] if far else down)
                back_left = send(to_right, up[1:] if far else up)
                after = [to_left]
                if not far:
                    break
            acc, *kept = more(acc, [right, left], around, after=after, keep=k < peers - 1)
            keeps += kept
            places.append(around)
            if k < peers - 1:
                right, left = following
    lesser = band(acc, own, back_left, back_right, energies, paired)

    recv = lax.all_to_all(lesser, "energy", split_axis=0, concat_axis=0, tiled=True)
    spread = scatter(recv, where, mix, factors, pairs)
    result = lax.all_to_all(spread, "energy", split_axis=0, concat_axis=0, tiled=True)
    return result.reshape(1, atoms * degree, 2 * W * W)


def solution(mesh):
    return jax.shard_map(
        per_device,
        mesh=mesh,
        in_specs=(
            P("energy", None, "orb", None),
            P("energy", "orb", None, None, None),
            P("orb", None),
            P(),
            P(),
            P("orb", None, None, None),
        ),
        out_specs=P("energy", "orb", None),
        check_vma=False,
    )
```

```python
import functools

import jax
import jax.numpy as jnp
from jax import lax
from jax.experimental import pallas as pl
from jax.experimental.pallas import tpu as pltpu
from jax.sharding import PartitionSpec as P

W = 8
BS = 128
REACH = 8
MARGIN = REACH * W
HALF = MARGIN // 2
TILE = 128
LANES = 128
F32, BF16 = jnp.float32, jnp.bfloat16

NT = (((1,), (1,)), ((), ()))
NN = (((1,), (0,)), ((), ()))


def halves(x):
    hi = x.astype(BF16)
    return hi, (x - hi.astype(F32)).astype(BF16)


def dot(a, b, dims):
    return lax.dot_general(a, b, dims, preferred_element_type=F32)


def dot3(a, b, dims):
    left = jnp.concatenate([a[0], a[0], a[1]], axis=1)
    right = jnp.concatenate([b[0], b[1], b[0]], axis=dims[0][1][0])
    return dot(left, right, dims)


def blocks_at_once(held):
    return 2 if held % 2 == 0 else 1


def some_blocks(lane, weights, hi_ref, lo_ref, acc_ref, edges, active):
    rows = hi_ref.shape[0] - 2 * MARGIN
    wide = 2 * BS
    split, products = [], []
    for n, (real, imag) in enumerate(weights):
        top = jnp.concatenate([real, imag], axis=1)
        weight = halves(jnp.concatenate([top, jnp.concatenate([-imag, real], axis=1)], axis=0))
        cols = pl.ds(lane + n * wide, wide)
        own = [ref[MARGIN : MARGIN + rows, cols] for ref in (hi_ref, lo_ref)]
        product = halves(dot3(own, weight, NN))
        for ref, part in zip(edges, product):
            ref[n, :MARGIN, :] = part[:MARGIN]
            ref[n, 3 * MARGIN :, :] = part[rows - MARGIN :]
        split.append(weight)
        products.append(product)
    cols = pl.ds(lane, len(weights) * wide)
    for t in range(rows // TILE):
        both = []
        for part in zip(*products):
            lanes = []
            for x in part:
                x = x[t * TILE : (t + 1) * TILE]
                turned = jnp.concatenate([x[:, BS:], -x[:, :BS]], axis=1)
                lanes.append(jnp.concatenate([x, turned], axis=0))
            both.append(jnp.concatenate(lanes, axis=1))
        near = pl.ds(t * TILE, TILE + 2 * MARGIN)
        acc_ref[t] = acc_ref[t] + dot3(both, (hi_ref[near, cols], lo_ref[near, cols]), NT)

    if not edges:
        return

    @pl.when(active)
    def _():
        for n, weight in enumerate(split):
            one = pl.ds(lane + n * wide, wide)
            outer = [
                jnp.concatenate(
                    [ref[MARGIN : 2 * MARGIN, one], ref[rows : rows + MARGIN, one]], axis=0
                )
                for ref in (hi_ref, lo_ref)
            ]
            for ref, part in zip(edges, halves(dot3(outer, weight, NT))):
                ref[n, MARGIN : 3 * MARGIN, :] = part


def shard_loop(first_block, self_ref, hi_ref, lo_ref, acc_ref, keeps, slot, active):
    held = self_ref.shape[1]
    once = blocks_at_once(held)

    def step(g, carry):
        lane = pl.multiple_of((first_block + g * once) * 2 * BS, 2 * BS)
        weights = [
            (self_ref[0, g * once + n, 0], self_ref[0, g * once + n, 1]) for n in range(once)
        ]
        slots = pl.ds(slot + g * once, once)
        kept = tuple(ref.at[slots] for ref in keeps)
        some_blocks(lane, weights, hi_ref, lo_ref, acc_ref, kept, active)
        return carry

    lax.fori_loop(0, held // once, step, 0)


def is_far(peers):
    return peers >= 4


def is_inner():
    z, peers = lax.axis_index("orb"), lax.axis_size("orb")
    if is_far(peers):
        return jnp.logical_and(z > 0, z < peers - 1)
    return z >= 0


def neighbour(distance):
    def place():
        z, peers = lax.axis_index("orb"), lax.axis_size("orb")
        number = z + distance
        return jnp.clip(number, 0, peers - 1), jnp.logical_and(number >= 0, number < peers)

    return place


def reflected(offset, inner):
    def place():
        z = lax.axis_index("orb")
        is_inner_one = jnp.logical_or(z == 1, z == 2)
        valid = z >= 0 if inner is None else is_inner_one == inner
        return lax.rem(offset + 4 - z, 4), valid

    return place


def beside():
    z = lax.axis_index("orb")
    return jnp.where(lax.rem(z, 2) == 0, z + 1, z - 1), z >= 0


def two_off(inner):
    def place():
        z = lax.axis_index("orb")
        return lax.rem(z + 2, 4), jnp.logical_or(z == 1, z == 2) == inner

    return place


def own_kernel(wanted, extra, green_ref, sigma_ref, *rest):
    acc_ref, keep_hi_ref, keep_lo_ref, hi_ref, lo_ref, *rest = rest[extra:]
    *sent, buf, self_ref, sem, sent_sem = rest
    rows, held = green_ref.shape[2], sigma_ref.shape[1]
    blocks = green_ref.shape[3] // BS
    begin, active = lax.axis_index("orb") * held, is_inner()

    def block_of(s):
        return lax.rem(begin + s, blocks)

    def fetch(s):
        col = pl.multiple_of(block_of(s) * BS, BS)
        return pltpu.make_async_copy(
            green_ref.at[0, :, :, pl.ds(col, BS)], buf.at[s], sem.at[s]
        )

    def store(s, carry):
        fetch(s).wait()
        lanes = pl.ds(pl.multiple_of(block_of(s) * 2 * BS, 2 * BS), 2 * BS)
        parts = halves(jnp.concatenate([buf[s, 0], buf[s, 1]], axis=1))
        for ref, part in zip((hi_ref, lo_ref), parts):
            ref[MARGIN : MARGIN + rows, lanes] = part
        return carry

    load = pltpu.make_async_copy(sigma_ref, self_ref, sem.at[blocks])
    load.start()
    for s in range(blocks):
        fetch(s).start()
    copies = []
    for n, ((size, start), out) in enumerate(zip(wanted, sent)):
        row = pl.multiple_of(start(lax.axis_index("orb"), rows), HALF)
        copies.append(
            pltpu.make_async_copy(green_ref.at[0, :, pl.ds(row, size), :], out, sent_sem.at[n])
        )
    for copy in copies:
        copy.start()
    acc_ref[...] = jnp.zeros_like(acc_ref)
    for ref in (hi_ref, lo_ref):
        ref[:MARGIN, :] = jnp.zeros((MARGIN, ref.shape[1]), BF16)
        ref[MARGIN + rows :, :] = jnp.zeros((MARGIN, ref.shape[1]), BF16)
    lax.fori_loop(0, held, store, 0)
    load.wait()
    shard_loop(begin, self_ref, hi_ref, lo_ref, acc_ref, (keep_hi_ref, keep_lo_ref), 0, active)
    lax.fori_loop(held, blocks, store, 0)
    for copy in copies:
        copy.wait()


def own_part(green, sigma, wanted, after):
    rows, held = green.shape[2], sigma.shape[1]
    tiles, blocks = rows // TILE, green.shape[3] // BS
    vmem = pl.BlockSpec(memory_space=pltpu.VMEM)
    hbm = pl.BlockSpec(memory_space=pl.ANY)
    keep = jax.ShapeDtypeStruct((held, 4 * MARGIN, 2 * BS), BF16)
    whole = jax.ShapeDtypeStruct((rows + 2 * MARGIN, blocks * 2 * BS), BF16)
    return pl.pallas_call(
        functools.partial(own_kernel, wanted, len(after)),
        out_shape=(
            jax.ShapeDtypeStruct((tiles, 2 * TILE, TILE + 2 * MARGIN), F32),
            keep,
            keep,
            whole,
            whole,
            *[jax.ShapeDtypeStruct((2, size, green.shape[3]), F32) for size, _ in wanted],
        ),
        in_specs=[hbm] * (2 + len(after)),
        out_specs=(vmem,) * (5 + len(wanted)),
        scratch_shapes=[
            pltpu.VMEM((blocks, 2, rows, BS), F32),
            pltpu.VMEM(sigma.shape, F32),
            pltpu.SemaphoreType.DMA((blocks + 1,)),
            pltpu.SemaphoreType.DMA((len(wanted),)),
        ],
        compiler_params=pltpu.CompilerParams(vmem_limit_bytes=40 << 20),
        cost_estimate=pl.CostEstimate(
            flops=held * rows * BS * BS,
            bytes_accessed=blocks * rows * BS,
            transcendentals=0,
        ),
        name="lesser_own",
    )(green, sigma, *after)


def lesser_kernel(places, held, extra, hi_ref, lo_ref, before_ref, *rest):
    sigmas, rest = rest[: len(places)], rest[len(places) :]
    rest = rest[extra:]
    acc_ref, keeps = rest[0], rest[1:]
    acc_ref[...] = before_ref[...]
    slot = 0
    for place, self_ref in zip(places, sigmas):
        number, valid = place()

        @pl.when(valid)
        def _():
            shard_loop(
                number * held, self_ref, hi_ref, lo_ref, acc_ref, keeps, slot, is_inner()
            )

        slot += self_ref.shape[1]


def lesser_part(hi, lo, before, shards, places, held, after=(), keep=True):
    vmem = pl.BlockSpec(memory_space=pltpu.VMEM)
    count = sum(x.shape[1] for x in shards)
    kept = jax.ShapeDtypeStruct((count, 4 * MARGIN, 2 * BS), BF16)
    outs = [jax.ShapeDtypeStruct(before.shape, F32)] + ([kept, kept] if keep else [])
    return pl.pallas_call(
        functools.partial(lesser_kernel, places, held, len(after)),
        out_shape=outs,
        in_specs=[vmem] * (3 + len(shards)) + [pl.BlockSpec(memory_space=pl.ANY)] * len(after),
        out_specs=[vmem] * len(outs),
        input_output_aliases={2: 0},
        compiler_params=pltpu.CompilerParams(vmem_limit_bytes=26 << 20),
        cost_estimate=pl.CostEstimate(
            flops=count * hi.shape[0] * BS * BS,
            bytes_accessed=before.size,
            transcendentals=0,
        ),
        name="lesser_more",
    )(hi, lo, before, *shards, *after)


def gate_kernel(*refs):
    del refs


def gate(arrays, after):
    hbm = pl.BlockSpec(memory_space=pl.ANY)
    return pl.pallas_call(
        gate_kernel,
        out_shape=[jax.ShapeDtypeStruct(x.shape, x.dtype) for x in arrays],
        in_specs=[hbm] * (len(arrays) + len(after)),
        out_specs=[hbm] * len(arrays),
        input_output_aliases={n: n for n in range(len(arrays))},
        compiler_params=pltpu.CompilerParams(vmem_limit_bytes=1 << 20),
        cost_estimate=pl.CostEstimate(flops=0, bytes_accessed=0, transcendentals=0),
        name="gate",
    )(*arrays, *after)


def edge_kernel(places, held, *refs):
    halos, refs = refs[:3], refs[3:]
    keeps = refs[: 2 * len(places)]
    left_ref, right_ref, own_ref, acc_ref = refs[2 * len(places) :]
    z, peers = lax.axis_index("orb"), lax.axis_size("orb")
    if is_far(peers):
        from_left, from_right = z == 1, z == peers - 2
    else:
        from_left = from_right = z < 0
    limit = jnp.where(from_right, MARGIN, HALF)
    acc_ref[...] = jnp.zeros_like(acc_ref)

    def rows_of(part, cols):
        return [ref[part, :, cols] for ref in halos]

    def add(number, hi, lo, at):
        cols = pl.ds(pl.multiple_of(number * held * BS, BS), held * BS)
        wide = [rows_of(part, cols) for part in range(2)]
        for side in range(2):
            fields = []
            for part in range(2):
                outer = jnp.where(from_left if side == 0 else from_right, wide[part][0], 0.0)
                inner = wide[part][1 + side]
                rows = [outer, inner] if side == 0 else [inner, outer]
                fields.append(halves(jnp.concatenate(rows, axis=0)))
            halo = []
            for real, imag in zip(*fields):
                lanes = []
                for s in range(held):
                    one = slice(s * BS, (s + 1) * BS)
                    lanes += [
                        jnp.concatenate([real[:, one], -imag[:, one]], axis=0),
                        jnp.concatenate([imag[:, one], real[:, one]], axis=0),
                    ]
                halo.append(jnp.concatenate(lanes, axis=1))
            rows = slice(side * TILE, (side + 1) * TILE)
            kept = [
                jnp.concatenate([ref[at + s, rows, :] for s in range(held)], axis=1)
                for ref in (hi, lo)
            ]
            acc_ref[side] = acc_ref[side] + dot3(halo, kept, NT)

    @pl.when(is_inner())
    def _():
        for k, shards in enumerate(places):
            for n, place in enumerate(shards):
                number, valid = place()

                @pl.when(valid)
                def _():
                    add(number, keeps[2 * k], keeps[2 * k + 1], n * held)

    lane = lax.broadcasted_iota(jnp.int32, (MARGIN, LANES), 1)
    row = lax.broadcasted_iota(jnp.int32, (MARGIN, LANES), 0)
    low = lane < MARGIN
    left, right = acc_ref[0], acc_ref[1]
    turned_left, turned_right = left.T[:MARGIN], right.T[MARGIN:]
    for part in range(2):
        rows = slice(part * MARGIN, (part + 1) * MARGIN)
        sign = 1.0 - 2.0 * part
        to_left = jnp.where(low, 0.0, sign * left[rows])
        to_right = jnp.where(lane < limit, sign * right[rows], 0.0)
        left_ref[part] = to_left
        right_ref[part] = to_right
    own_ref[0, 0] = jnp.where(low, turned_left, 0.0)
    own_ref[0, 1] = jnp.where(low, pltpu.roll(turned_left, MARGIN, 1), 0.0)
    mine = jnp.logical_and(row < limit, lane >= MARGIN)
    own_ref[1, 0] = jnp.where(mine, pltpu.roll(turned_right, MARGIN, 1), 0.0)
    own_ref[1, 1] = jnp.where(mine, turned_right, 0.0)


def edge_part(halos, keeps, places, held):
    vmem = pl.BlockSpec(memory_space=pltpu.VMEM)
    side = jax.ShapeDtypeStruct((2, MARGIN, LANES), F32)
    return pl.pallas_call(
        functools.partial(edge_kernel, places, held),
        out_shape=(side, side, jax.ShapeDtypeStruct((2, 2, MARGIN, LANES), F32)),
        in_specs=[vmem] * (len(halos) + len(keeps)),
        out_specs=(vmem, vmem, vmem),
        scratch_shapes=[pltpu.VMEM((2, TILE, TILE), F32)],
        compiler_params=pltpu.CompilerParams(vmem_limit_bytes=20 << 20),
        cost_estimate=pl.CostEstimate(
            flops=1 << 31, bytes_accessed=8 << 20, transcendentals=0
        ),
        name="edges",
    )(*halos, *keeps)


def pair_edge_kernel(middle, shards, held, *refs):
    halo_ref, keeps, refs = refs[0], refs[1 : 1 + 2 * len(shards)], refs[1 + 2 * len(shards) :]
    if middle:
        before_ref, refs = refs[0], refs[1:]
    send_ref, own_ref, acc_ref = refs
    z = lax.axis_index("orb")
    on_left = (z == 2) if middle else (z == 1)
    count = halo_ref.shape[1]
    begin = pl.multiple_of(jnp.where(on_left, 0, TILE), TILE)
    acc_ref[...] = jnp.zeros_like(acc_ref)

    @pl.when(is_inner())
    def _():
        for k, group in enumerate(shards):
            for n, place in enumerate(group):
                number, _ = place()
                cols = pl.ds(pl.multiple_of(number * held * BS, BS), held * BS)
                fields = [halves(halo_ref[part, :, cols]) for part in range(2)]
                halo = []
                for real, imag in zip(*fields):
                    lanes = []
                    for s in range(held):
                        one = slice(s * BS, (s + 1) * BS)
                        lanes += [
                            jnp.concatenate([real[:, one], -imag[:, one]], axis=0),
                            jnp.concatenate([imag[:, one], real[:, one]], axis=0),
                        ]
                    halo.append(jnp.concatenate(lanes, axis=1))
                kept = [
                    jnp.concatenate(
                        [ref[n * held + s, pl.ds(begin, TILE), :] for s in range(held)], axis=1
                    )
                    for ref in keeps[2 * k : 2 * k + 2]
                ]
                acc_ref[...] = acc_ref[...] + dot3(halo, kept, NT)

    limit = HALF if middle else MARGIN
    lane = lax.broadcasted_iota(jnp.int32, (MARGIN, LANES), 1)
    row = lax.broadcasted_iota(jnp.int32, (MARGIN, LANES), 0)
    low = lane < MARGIN
    mine = jnp.logical_and(row < limit, lane >= MARGIN)
    parts = [acc_ref[part * count : (part + 1) * count, :] for part in range(2)]
    if middle:
        none = jnp.zeros((MARGIN - count, LANES), F32)
        parts = [
            jnp.where(
                on_left,
                jnp.concatenate([none, x], axis=0),
                jnp.concatenate([x, none], axis=0),
            )
            for x in parts
        ]
    for part, sign in enumerate((1.0, -1.0)):
        x = sign * parts[part]
        send_ref[part] = jnp.where(
            on_left, jnp.where(low, 0.0, x), jnp.where(lane < limit, x, 0.0)
        )
    turned = jnp.concatenate(parts, axis=0).T
    left, right = turned[:MARGIN], turned[MARGIN:]
    lefts = left, pltpu.roll(left, MARGIN, 1)
    rights = pltpu.roll(right, MARGIN, 1), right
    for part in range(2):
        own = [
            jnp.where(on_left, jnp.where(low, lefts[part], 0.0), 0.0),
            jnp.where(on_left, 0.0, jnp.where(mine, rights[part], 0.0)),
        ]
        for side in range(2):
            own_ref[side, part] = own[side] + (before_ref[side, part] if middle else 0.0)


def pair_edge_part(halo, keeps, shards, held, before=None):
    vmem = pl.BlockSpec(memory_space=pltpu.VMEM)
    middle = before is not None
    args = [halo, *keeps] + ([before] if middle else [])
    return pl.pallas_call(
        functools.partial(pair_edge_kernel, middle, shards, held),
        out_shape=(
            jax.ShapeDtypeStruct((2, MARGIN, LANES), F32),
            jax.ShapeDtypeStruct((2, 2, MARGIN, LANES), F32),
        ),
        in_specs=[vmem] * len(args),
        out_specs=(vmem, vmem),
        scratch_shapes=[pltpu.VMEM((2 * halo.shape[1], TILE), F32)],
        compiler_params=pltpu.CompilerParams(vmem_limit_bytes=20 << 20),
        cost_estimate=pl.CostEstimate(flops=1 << 30, bytes_accessed=4 << 20, transcendentals=0),
        name="edge_middle" if middle else "edge_end",
    )(*args)


def band_kernel(paired, acc_ref, own_ref, from_left_ref, from_right_ref, out_ref, rows_ref):
    tiles = acc_ref.shape[0]
    returned = [[ref[part] for part in range(2)] for ref in (from_left_ref, from_right_ref)]
    if paired:
        either = [x + y for x, y in zip(*returned)]
        high = lax.axis_index("orb") >= 2
        returned = [
            [jnp.where(high, x, 0.0) for x in either],
            [jnp.where(high, 0.0, x) for x in either],
        ]
    group = out_ref.shape[2]
    per_tile = TILE // W
    for t in range(tiles):
        for part in range(2):
            base = part * TILE
            x = acc_ref[t, base : base + TILE, :]
            rows_ref[t, part] = x
            if t == 0:
                extra = own_ref[0, part] + returned[0][part]
                rows_ref[t, part, :MARGIN, :LANES] = x[:MARGIN, :LANES] + extra
            if t == tiles - 1:
                extra = own_ref[1, part] + returned[1][part]
                rows_ref[t, part, MARGIN:, LANES:] = x[MARGIN:, LANES:] + extra
    low = lax.broadcasted_iota(jnp.int32, (W, LANES), 1) < MARGIN
    width = TILE + 2 * MARGIN
    for a in range(per_tile):
        for t in range(tiles):
            atom = t * per_tile + a
            for part in range(2):
                x = rows_ref[t, part, a * W : (a + 1) * W, :]
                before = pltpu.roll(x, (width - a * W) % width, 1)[:, :LANES]
                after = pltpu.roll(x, (width - (a + 1) * W) % width, 1)[:, :LANES]
                out_ref[atom // group, part, atom % group] = jnp.where(low, before, after)


def band(acc, own, from_left, from_right, energies, paired):
    tiles = acc.shape[0]
    atoms = tiles * TILE // W
    vmem = pl.BlockSpec(memory_space=pltpu.VMEM)
    return pl.pallas_call(
        functools.partial(band_kernel, paired),
        out_shape=jax.ShapeDtypeStruct((energies, 2, atoms // energies, W, LANES), F32),
        in_specs=[vmem] * 4,
        out_specs=vmem,
        scratch_shapes=[pltpu.VMEM((tiles, 2, TILE, TILE + 2 * MARGIN), F32)],
        compiler_params=pltpu.CompilerParams(vmem_limit_bytes=16 << 20),
        name="band",
    )(acc, own, from_left, from_right)


def scatter_kernel(
    recv_ref, where_ref, mix_ref, dham_ref, out_ref, smeared_ref, result_ref, factor_ref
):
    energies, _, group, _, _ = recv_ref.shape
    padded = dham_ref.shape[1]
    pairs = out_ref.shape[1]
    columns = [
        recv_ref[:, :, a, :, :].reshape(energies * 2 * W, LANES) for a in range(group)
    ]
    received = halves(jnp.concatenate(columns, axis=1))
    mixed = jnp.concatenate(halves(dot3(halves(mix_ref[...]), received, NN)), axis=0)
    rows = smeared_ref.shape[0]
    entry = lax.broadcasted_iota(jnp.int32, (group * LANES, padded), 0)
    offset = entry - where_ref[...] * W
    for j in range(0, W, 2):
        pick = jnp.concatenate(
            [jnp.where(offset == j + n, 1.0, 0.0).astype(BF16) for n in range(2)], axis=1
        )
        both = dot(mixed, pick, NN)
        smeared_ref[:, j * padded : (j + 2) * padded] = both[:rows] + both[rows:]
    for row in range(dham_ref.shape[0]):
        factor_ref[row] = jnp.broadcast_to(dham_ref[row : row + 1, :], (energies, padded))

    def block(part, j, k):
        row = (part * W + j) * energies
        return smeared_ref[row : row + energies, k * padded : (k + 1) * padded]

    for part in range(2):
        for i in range(W):
            total = [None] * W
            for c in range(3):
                factors = [factor_ref[(c * W + i) * W + j] for j in range(W)]
                for k in range(W):
                    t = None
                    for j in range(W):
                        term = factors[j] * block(part, j, k)
                        t = term if t is None else t + term
                    for l in range(W):
                        term = t * factor_ref[(c * W + l) * W + k]
                        total[l] = term if total[l] is None else total[l] + term
            for l in range(W):
                row = ((part * W + i) * W + l) * energies
                result_ref[row : row + energies, :] = total[l]
    for e in range(energies):
        one = result_ref[pl.ds(e, 2 * W * W, stride=energies), :]
        out_ref[e] = one.T[:pairs, :]


def scatter(recv, where, mix, dham, pairs):
    energies, _, group, _, _ = recv.shape
    padded = dham.shape[1]
    vmem = pl.BlockSpec(memory_space=pltpu.VMEM)
    return pl.pallas_call(
        scatter_kernel,
        out_shape=jax.ShapeDtypeStruct((energies, pairs, 2 * W * W), F32),
        in_specs=[vmem] * 4,
        out_specs=vmem,
        scratch_shapes=[
            pltpu.VMEM((2 * W * energies, W * padded), F32),
            pltpu.VMEM((2 * W * W * energies, padded), F32),
            pltpu.VMEM((dham.shape[0], energies, padded), F32),
        ],
        compiler_params=pltpu.CompilerParams(vmem_limit_bytes=24 << 20),
        name="scatter",
    )(recv, where, mix, dham)


def build_kernel(phonon_shift, phonon_weight, energies):
    rows_e = jnp.arange(energies, dtype=jnp.int32)[None, :, None]
    cols_f = jnp.arange(energies, dtype=jnp.int32)[None, None, :]
    shifts = phonon_shift[:, None, None]
    emission = (cols_f == rows_e + shifts).astype(F32)
    absorption = (cols_f == rows_e - shifts).astype(F32)
    terms = (
        phonon_weight[0][:, None, None] * emission + phonon_weight[1][:, None, None] * absorption
    )
    return jnp.sum(terms, axis=0)


def build_mix(phonon_shift, phonon_weight, energies):
    kernel = build_kernel(phonon_shift, phonon_weight, energies)
    same = jnp.eye(2 * W, dtype=F32)
    mix = same[:, None, None, :] * kernel[None, :, :, None]
    return mix.reshape(2 * W * energies, energies * 2 * W)


def send(x, pairs):
    return lax.ppermute(x, "orb", pairs)


def per_device(green, sigma, neighbours, phonon_shift, phonon_weight, dham):
    energies = lax.axis_size("energy")
    peers = lax.axis_size("orb")
    e, z = lax.axis_index("energy"), lax.axis_index("orb")
    rows = green.shape[2]
    atoms = rows // W
    degree = neighbours.shape[1]
    group = atoms // energies
    pairs = group * degree
    padded = -(-pairs // LANES) * LANES
    held = sigma.shape[1]

    far, paired = is_far(peers), peers == 4
    up = [(i, i + 1) for i in range(peers - 1)]
    down = [(i + 1, i) for i in range(peers - 1)]
    fixed = pltpu.with_memory_space_constraint(green, pltpu.HBM)
    if paired:
        ends, middle, outward = [(0, 1), (3, 2)], [(1, 2), (2, 1)], [(1, 0), (2, 3)]
        aside, across = send(sigma, ends + outward), send(sigma, middle)
        wanted = [
            (MARGIN, lambda z, rows: jnp.where(z == 0, rows - MARGIN, 0)),
            (HALF, lambda z, rows: jnp.where(z == 1, rows - HALF, 0)),
        ]
    else:
        right, left = send(sigma, up), send(sigma, down)
        wanted = [
            (HALF, lambda z, rows: jnp.where(z == 0, rows - MARGIN, HALF)),
            (HALF, lambda z, rows: rows - HALF),
            (HALF, lambda z, rows: 0 * z),
        ]

    mine = lax.dynamic_slice_in_dim(neighbours, e * group, group, axis=0)
    first = z * atoms + e * group
    offset = mine - (first + jnp.arange(group, dtype=jnp.int32))[:, None]
    column = jnp.where(offset < 0, offset + REACH, offset + REACH - 1)
    where = column + 2 * REACH * jnp.arange(group, dtype=jnp.int32)[:, None]
    where = jnp.pad(where.reshape(1, pairs), ((0, 0), (0, padded - pairs)), constant_values=-1)
    mix = build_mix(phonon_shift, phonon_weight, energies)
    factors = lax.dynamic_slice_in_dim(
        dham.transpose(1, 2, 3, 0).reshape(3 * W * W, -1), e * pairs, pairs, axis=1
    )
    factors = jnp.pad(factors, ((0, 0), (0, padded - pairs)))


    acc, keep_hi, keep_lo, hi, lo, outer, near, *nearer = own_part(
        fixed,
        pltpu.with_memory_space_constraint(sigma, pltpu.HBM),
        wanted,
        [where, mix, factors],
    )
    keeps = [keep_hi, keep_lo]
    more = functools.partial(lesser_part, hi, lo, held=held)
    places = [[neighbour(0)]]
    if paired:
        (aside,) = gate([aside], [keeps[-1]])
        (across,) = gate([across], [aside])
        second_across, second_aside = send(aside, middle), send(across, outward)
        halos = [send(outer, ends), send(near, middle)]
        places.append([beside, reflected(3, True)])
        acc, *kept = more(acc, [aside, across], places[-1])
        keeps += kept
        (second_across,) = gate([second_across], [kept[-1]])
        third_aside = send(second_across, outward)
        places.append([two_off(True), two_off(False)])
        acc, *kept = more(acc, [second_across, second_aside], places[-1])
        keeps += kept
        shards = [*places[:-1], places[-1][:1]]
        to_end, own = pair_edge_part(halos[0], keeps, shards, held)
        back_left = send(to_end, outward)
        to_middle, own = pair_edge_part(halos[1], keeps, shards, held, own)
        back_right = send(to_middle, middle)
        (acc,) = more(acc, [third_aside], [reflected(3, False)], after=[to_middle, back_left], keep=False)
    else:
        near_right = send(near, up[:-1] if far else up)
        near_left = send(nearer[0], down[1:] if far else down)
        if far:
            other = send(outer, [(0, 1), (peers - 1, peers - 2)])
        else:
            other = jnp.zeros_like(near_left)
        for k in range(1, peers):
            around = [neighbour(-k), neighbour(k)]
            if k < peers - 1:
                right, left = gate([right, left], [keeps[-1], outer if k == 1 else other])
                following = send(right, up[k:]), send(left, down[: peers - 1 - k])
                after = []
            else:
                if not far:
                    acc, *kept = more(acc, [right, left], around)
                    keeps += kept
                    places.append(around)
                to_left, to_right, own = edge_part(
                    [other, near_right, near_left], keeps, places, held
                )
                back_right = send(to_left, down[:-1] if far else down)
                back_left = send(to_right, up[1:] if far else up)
                after = [to_left]
                if not far:
                    break
            acc, *kept = more(acc, [right, left], around, after=after, keep=k < peers - 1)
            keeps += kept
            places.append(around)
            if k < peers - 1:
                right, left = following
    lesser = band(acc, own, back_left, back_right, energies, paired)

    recv = lax.all_to_all(lesser, "energy", split_axis=0, concat_axis=0, tiled=True)
    spread = scatter(recv, where, mix, factors, pairs)
    result = lax.all_to_all(spread, "energy", split_axis=0, concat_axis=0, tiled=True)
    return result.reshape(1, atoms * degree, 2 * W * W)


def solution(mesh):
    return jax.shard_map(
        per_device,
        mesh=mesh,
        in_specs=(
            P("energy", None, "orb", None),
            P("energy", "orb", None, None, None),
            P("orb", None),
            P(),
            P(),
            P("orb", None, None, None),
        ),
        out_specs=P("energy", "orb", None),
        check_vma=False,
    )
```

```python
import functools

import jax
import jax.numpy as jnp
from jax import lax
from jax.experimental import pallas as pl
from jax.experimental.pallas import tpu as pltpu
from jax.sharding import PartitionSpec as P

W = 8
BS = 128
REACH = 8
MARGIN = REACH * W
HALF = MARGIN // 2
TILE = 128
LANES = 128
F32, BF16 = jnp.float32, jnp.bfloat16

NT = (((1,), (1,)), ((), ()))
NN = (((1,), (0,)), ((), ()))


def halves(x):
    hi = x.astype(BF16)
    return hi, (x - hi.astype(F32)).astype(BF16)


def dot(a, b, dims):
    return lax.dot_general(a, b, dims, preferred_element_type=F32)


def dot3(a, b, dims):
    left = jnp.concatenate([a[0], a[0], a[1]], axis=1)
    right = jnp.concatenate([b[0], b[1], b[0]], axis=dims[0][1][0])
    return dot(left, right, dims)


def blocks_at_once(held):
    return 2 if held % 2 == 0 else 1


def some_blocks(lane, weights, hi_ref, lo_ref, acc_ref, edges, active):
    rows = hi_ref.shape[0] - 2 * MARGIN
    wide = 2 * BS
    split, products = [], []
    for n, (real, imag) in enumerate(weights):
        top = jnp.concatenate([real, imag], axis=1)
        weight = halves(jnp.concatenate([top, jnp.concatenate([-imag, real], axis=1)], axis=0))
        cols = pl.ds(lane + n * wide, wide)
        own = [ref[MARGIN : MARGIN + rows, cols] for ref in (hi_ref, lo_ref)]
        product = halves(dot3(own, weight, NN))
        for ref, part in zip(edges, product):
            ref[n, :MARGIN, :] = part[:MARGIN]
            ref[n, 3 * MARGIN :, :] = part[rows - MARGIN :]
        split.append(weight)
        products.append(product)
    cols = pl.ds(lane, len(weights) * wide)
    for t in range(rows // TILE):
        both = []
        for part in zip(*products):
            lanes = []
            for x in part:
                x = x[t * TILE : (t + 1) * TILE]
                turned = jnp.concatenate([x[:, BS:], -x[:, :BS]], axis=1)
                lanes.append(jnp.concatenate([x, turned], axis=0))
            both.append(jnp.concatenate(lanes, axis=1))
        near = pl.ds(t * TILE, TILE + 2 * MARGIN)
        acc_ref[t] = acc_ref[t] + dot3(both, (hi_ref[near, cols], lo_ref[near, cols]), NT)

    if not edges:
        return

    @pl.when(active)
    def _():
        for n, weight in enumerate(split):
            one = pl.ds(lane + n * wide, wide)
            outer = [
                jnp.concatenate(
                    [ref[MARGIN : 2 * MARGIN, one], ref[rows : rows + MARGIN, one]], axis=0
                )
                for ref in (hi_ref, lo_ref)
            ]
            for ref, part in zip(edges, halves(dot3(outer, weight, NT))):
                ref[n, MARGIN : 3 * MARGIN, :] = part


def shard_loop(first_block, self_ref, hi_ref, lo_ref, acc_ref, keeps, slot, active):
    held = self_ref.shape[1]
    once = blocks_at_once(held)

    def step(g, carry):
        lane = pl.multiple_of((first_block + g * once) * 2 * BS, 2 * BS)
        weights = [
            (self_ref[0, g * once + n, 0], self_ref[0, g * once + n, 1]) for n in range(once)
        ]
        slots = pl.ds(slot + g * once, once)
        kept = tuple(ref.at[slots] for ref in keeps)
        some_blocks(lane, weights, hi_ref, lo_ref, acc_ref, kept, active)
        return carry

    lax.fori_loop(0, held // once, step, 0)


def is_far(peers):
    return peers >= 4


def is_inner():
    z, peers = lax.axis_index("orb"), lax.axis_size("orb")
    if is_far(peers):
        return jnp.logical_and(z > 0, z < peers - 1)
    return z >= 0


def neighbour(distance):
    def place():
        z, peers = lax.axis_index("orb"), lax.axis_size("orb")
        number = z + distance
        return jnp.clip(number, 0, peers - 1), jnp.logical_and(number >= 0, number < peers)

    return place


def reflected(offset, inner):
    def place():
        z = lax.axis_index("orb")
        is_inner_one = jnp.logical_or(z == 1, z == 2)
        valid = z >= 0 if inner is None else is_inner_one == inner
        return lax.rem(offset + 4 - z, 4), valid

    return place


def beside():
    z = lax.axis_index("orb")
    return jnp.where(lax.rem(z, 2) == 0, z + 1, z - 1), z >= 0


def two_off(inner):
    def place():
        z = lax.axis_index("orb")
        return lax.rem(z + 2, 4), jnp.logical_or(z == 1, z == 2) == inner

    return place


def own_kernel(wanted, extra, green_ref, sigma_ref, *rest):
    acc_ref, keep_hi_ref, keep_lo_ref, hi_ref, lo_ref, *rest = rest[extra:]
    *sent, buf, self_ref, sem, sent_sem = rest
    rows, held = green_ref.shape[2], sigma_ref.shape[1]
    blocks = green_ref.shape[3] // BS
    begin, active = lax.axis_index("orb") * held, is_inner()

    def block_of(s):
        return lax.rem(begin + s, blocks)

    def fetch(s):
        col = pl.multiple_of(block_of(s) * BS, BS)
        return pltpu.make_async_copy(
            green_ref.at[0, :, :, pl.ds(col, BS)], buf.at[s], sem.at[s]
        )

    def store(s, carry):
        fetch(s).wait()
        lanes = pl.ds(pl.multiple_of(block_of(s) * 2 * BS, 2 * BS), 2 * BS)
        parts = halves(jnp.concatenate([buf[s, 0], buf[s, 1]], axis=1))
        for ref, part in zip((hi_ref, lo_ref), parts):
            ref[MARGIN : MARGIN + rows, lanes] = part
        return carry

    load = pltpu.make_async_copy(sigma_ref, self_ref, sem.at[blocks])
    load.start()
    for s in range(blocks):
        fetch(s).start()
    copies = []
    for n, ((size, start), out) in enumerate(zip(wanted, sent)):
        row = pl.multiple_of(start(lax.axis_index("orb"), rows), HALF)
        copies.append(
            pltpu.make_async_copy(green_ref.at[0, :, pl.ds(row, size), :], out, sent_sem.at[n])
        )
    for copy in copies:
        copy.start()
    acc_ref[...] = jnp.zeros_like(acc_ref)
    for ref in (hi_ref, lo_ref):
        ref[:MARGIN, :] = jnp.zeros((MARGIN, ref.shape[1]), BF16)
        ref[MARGIN + rows :, :] = jnp.zeros((MARGIN, ref.shape[1]), BF16)
    lax.fori_loop(0, held, store, 0)
    load.wait()
    shard_loop(begin, self_ref, hi_ref, lo_ref, acc_ref, (keep_hi_ref, keep_lo_ref), 0, active)
    lax.fori_loop(held, blocks, store, 0)
    for copy in copies:
        copy.wait()


def own_part(green, sigma, wanted, after):
    rows, held = green.shape[2], sigma.shape[1]
    tiles, blocks = rows // TILE, green.shape[3] // BS
    vmem = pl.BlockSpec(memory_space=pltpu.VMEM)
    hbm = pl.BlockSpec(memory_space=pl.ANY)
    keep = jax.ShapeDtypeStruct((held, 4 * MARGIN, 2 * BS), BF16)
    whole = jax.ShapeDtypeStruct((rows + 2 * MARGIN, blocks * 2 * BS), BF16)
    return pl.pallas_call(
        functools.partial(own_kernel, wanted, len(after)),
        out_shape=(
            jax.ShapeDtypeStruct((tiles, 2 * TILE, TILE + 2 * MARGIN), F32),
            keep,
            keep,
            whole,
            whole,
            *[jax.ShapeDtypeStruct((2, size, green.shape[3]), F32) for size, _ in wanted],
        ),
        in_specs=[hbm] * (2 + len(after)),
        out_specs=(vmem,) * (5 + len(wanted)),
        scratch_shapes=[
            pltpu.VMEM((blocks, 2, rows, BS), F32),
            pltpu.VMEM(sigma.shape, F32),
            pltpu.SemaphoreType.DMA((blocks + 1,)),
            pltpu.SemaphoreType.DMA((len(wanted),)),
        ],
        compiler_params=pltpu.CompilerParams(vmem_limit_bytes=40 << 20),
        cost_estimate=pl.CostEstimate(
            flops=held * rows * BS * BS,
            bytes_accessed=blocks * rows * BS,
            transcendentals=0,
        ),
        name="lesser_own",
    )(green, sigma, *after)


def lesser_kernel(places, held, extra, hi_ref, lo_ref, before_ref, *rest):
    sigmas, rest = rest[: len(places)], rest[len(places) :]
    rest = rest[extra:]
    acc_ref, keeps = rest[0], rest[1:]
    acc_ref[...] = before_ref[...]
    slot = 0
    for place, self_ref in zip(places, sigmas):
        number, valid = place()

        @pl.when(valid)
        def _():
            shard_loop(
                number * held, self_ref, hi_ref, lo_ref, acc_ref, keeps, slot, is_inner()
            )

        slot += self_ref.shape[1]


def lesser_part(hi, lo, before, shards, places, held, after=(), keep=True):
    vmem = pl.BlockSpec(memory_space=pltpu.VMEM)
    count = sum(x.shape[1] for x in shards)
    kept = jax.ShapeDtypeStruct((count, 4 * MARGIN, 2 * BS), BF16)
    outs = [jax.ShapeDtypeStruct(before.shape, F32)] + ([kept, kept] if keep else [])
    return pl.pallas_call(
        functools.partial(lesser_kernel, places, held, len(after)),
        out_shape=outs,
        in_specs=[vmem] * (3 + len(shards)) + [pl.BlockSpec(memory_space=pl.ANY)] * len(after),
        out_specs=[vmem] * len(outs),
        input_output_aliases={2: 0},
        compiler_params=pltpu.CompilerParams(vmem_limit_bytes=26 << 20),
        cost_estimate=pl.CostEstimate(
            flops=count * hi.shape[0] * BS * BS,
            bytes_accessed=before.size,
            transcendentals=0,
        ),
        name="lesser_more",
    )(hi, lo, before, *shards, *after)


def gate_kernel(*refs):
    del refs


def gate(arrays, after):
    hbm = pl.BlockSpec(memory_space=pl.ANY)
    return pl.pallas_call(
        gate_kernel,
        out_shape=[jax.ShapeDtypeStruct(x.shape, x.dtype) for x in arrays],
        in_specs=[hbm] * (len(arrays) + len(after)),
        out_specs=[hbm] * len(arrays),
        input_output_aliases={n: n for n in range(len(arrays))},
        compiler_params=pltpu.CompilerParams(vmem_limit_bytes=1 << 20),
        cost_estimate=pl.CostEstimate(flops=0, bytes_accessed=0, transcendentals=0),
        name="gate",
    )(*arrays, *after)


def edge_kernel(places, held, *refs):
    halos, refs = refs[:3], refs[3:]
    keeps = refs[: 2 * len(places)]
    left_ref, right_ref, own_ref, acc_ref = refs[2 * len(places) :]
    z, peers = lax.axis_index("orb"), lax.axis_size("orb")
    if is_far(peers):
        from_left, from_right = z == 1, z == peers - 2
    else:
        from_left = from_right = z < 0
    limit = jnp.where(from_right, MARGIN, HALF)
    acc_ref[...] = jnp.zeros_like(acc_ref)

    def rows_of(part, cols):
        return [ref[part, :, cols] for ref in halos]

    def add(number, hi, lo, at):
        cols = pl.ds(pl.multiple_of(number * held * BS, BS), held * BS)
        wide = [rows_of(part, cols) for part in range(2)]
        for side in range(2):
            fields = []
            for part in range(2):
                outer = jnp.where(from_left if side == 0 else from_right, wide[part][0], 0.0)
                inner = wide[part][1 + side]
                rows = [outer, inner] if side == 0 else [inner, outer]
                fields.append(halves(jnp.concatenate(rows, axis=0)))
            halo = []
            for real, imag in zip(*fields):
                lanes = []
                for s in range(held):
                    one = slice(s * BS, (s + 1) * BS)
                    lanes += [
                        jnp.concatenate([real[:, one], -imag[:, one]], axis=0),
                        jnp.concatenate([imag[:, one], real[:, one]], axis=0),
                    ]
                halo.append(jnp.concatenate(lanes, axis=1))
            rows = slice(side * TILE, (side + 1) * TILE)
            kept = [
                jnp.concatenate([ref[at + s, rows, :] for s in range(held)], axis=1)
                for ref in (hi, lo)
            ]
            acc_ref[side] = acc_ref[side] + dot3(halo, kept, NT)

    @pl.when(is_inner())
    def _():
        for k, shards in enumerate(places):
            for n, place in enumerate(shards):
                number, valid = place()

                @pl.when(valid)
                def _():
                    add(number, keeps[2 * k], keeps[2 * k + 1], n * held)

    lane = lax.broadcasted_iota(jnp.int32, (MARGIN, LANES), 1)
    row = lax.broadcasted_iota(jnp.int32, (MARGIN, LANES), 0)
    low = lane < MARGIN
    left, right = acc_ref[0], acc_ref[1]
    turned_left, turned_right = left.T[:MARGIN], right.T[MARGIN:]
    for part in range(2):
        rows = slice(part * MARGIN, (part + 1) * MARGIN)
        sign = 1.0 - 2.0 * part
        to_left = jnp.where(low, 0.0, sign * left[rows])
        to_right = jnp.where(lane < limit, sign * right[rows], 0.0)
        left_ref[part] = to_left
        right_ref[part] = to_right
    own_ref[0, 0] = jnp.where(low, turned_left, 0.0)
    own_ref[0, 1] = jnp.where(low, pltpu.roll(turned_left, MARGIN, 1), 0.0)
    mine = jnp.logical_and(row < limit, lane >= MARGIN)
    own_ref[1, 0] = jnp.where(mine, pltpu.roll(turned_right, MARGIN, 1), 0.0)
    own_ref[1, 1] = jnp.where(mine, turned_right, 0.0)


def edge_part(halos, keeps, places, held):
    vmem = pl.BlockSpec(memory_space=pltpu.VMEM)
    side = jax.ShapeDtypeStruct((2, MARGIN, LANES), F32)
    return pl.pallas_call(
        functools.partial(edge_kernel, places, held),
        out_shape=(side, side, jax.ShapeDtypeStruct((2, 2, MARGIN, LANES), F32)),
        in_specs=[vmem] * (len(halos) + len(keeps)),
        out_specs=(vmem, vmem, vmem),
        scratch_shapes=[pltpu.VMEM((2, TILE, TILE), F32)],
        compiler_params=pltpu.CompilerParams(vmem_limit_bytes=20 << 20),
        cost_estimate=pl.CostEstimate(
            flops=1 << 31, bytes_accessed=8 << 20, transcendentals=0
        ),
        name="edges",
    )(*halos, *keeps)


def pair_edge_kernel(middle, shards, held, *refs):
    halo_ref, keeps, refs = refs[0], refs[1 : 1 + 2 * len(shards)], refs[1 + 2 * len(shards) :]
    if middle:
        before_ref, refs = refs[0], refs[1:]
    send_ref, own_ref, acc_ref = refs
    z = lax.axis_index("orb")
    on_left = (z == 2) if middle else (z == 1)
    count = halo_ref.shape[1]
    begin = pl.multiple_of(jnp.where(on_left, 0, TILE), TILE)
    acc_ref[...] = jnp.zeros_like(acc_ref)

    @pl.when(is_inner())
    def _():
        for k, group in enumerate(shards):
            for n, place in enumerate(group):
                number, _ = place()
                cols = pl.ds(pl.multiple_of(number * held * BS, BS), held * BS)
                fields = [halves(halo_ref[part, :, cols]) for part in range(2)]
                halo = []
                for real, imag in zip(*fields):
                    lanes = []
                    for s in range(held):
                        one = slice(s * BS, (s + 1) * BS)
                        lanes += [
                            jnp.concatenate([real[:, one], -imag[:, one]], axis=0),
                            jnp.concatenate([imag[:, one], real[:, one]], axis=0),
                        ]
                    halo.append(jnp.concatenate(lanes, axis=1))
                kept = [
                    jnp.concatenate(
                        [ref[n * held + s, pl.ds(begin, TILE), :] for s in range(held)], axis=1
                    )
                    for ref in keeps[2 * k : 2 * k + 2]
                ]
                acc_ref[...] = acc_ref[...] + dot3(halo, kept, NT)

    limit = HALF if middle else MARGIN
    lane = lax.broadcasted_iota(jnp.int32, (MARGIN, LANES), 1)
    row = lax.broadcasted_iota(jnp.int32, (MARGIN, LANES), 0)
    low = lane < MARGIN
    mine = jnp.logical_and(row < limit, lane >= MARGIN)
    parts = [acc_ref[part * count : (part + 1) * count, :] for part in range(2)]
    if middle:
        none = jnp.zeros((MARGIN - count, LANES), F32)
        parts = [
            jnp.where(
                on_left,
                jnp.concatenate([none, x], axis=0),
                jnp.concatenate([x, none], axis=0),
            )
            for x in parts
        ]
    for part, sign in enumerate((1.0, -1.0)):
        x = sign * parts[part]
        send_ref[part] = jnp.where(
            on_left, jnp.where(low, 0.0, x), jnp.where(lane < limit, x, 0.0)
        )
    turned = jnp.concatenate(parts, axis=0).T
    left, right = turned[:MARGIN], turned[MARGIN:]
    lefts = left, pltpu.roll(left, MARGIN, 1)
    rights = pltpu.roll(right, MARGIN, 1), right
    for part in range(2):
        own = [
            jnp.where(on_left, jnp.where(low, lefts[part], 0.0), 0.0),
            jnp.where(on_left, 0.0, jnp.where(mine, rights[part], 0.0)),
        ]
        for side in range(2):
            own_ref[side, part] = own[side] + (before_ref[side, part] if middle else 0.0)


def pair_edge_part(halo, keeps, shards, held, before=None):
    vmem = pl.BlockSpec(memory_space=pltpu.VMEM)
    middle = before is not None
    args = [halo, *keeps] + ([before] if middle else [])
    return pl.pallas_call(
        functools.partial(pair_edge_kernel, middle, shards, held),
        out_shape=(
            jax.ShapeDtypeStruct((2, MARGIN, LANES), F32),
            jax.ShapeDtypeStruct((2, 2, MARGIN, LANES), F32),
        ),
        in_specs=[vmem] * len(args),
        out_specs=(vmem, vmem),
        scratch_shapes=[pltpu.VMEM((2 * halo.shape[1], TILE), F32)],
        compiler_params=pltpu.CompilerParams(vmem_limit_bytes=20 << 20),
        cost_estimate=pl.CostEstimate(flops=1 << 30, bytes_accessed=4 << 20, transcendentals=0),
        name="edge_middle" if middle else "edge_end",
    )(*args)


def band_kernel(paired, acc_ref, own_ref, from_left_ref, from_right_ref, out_ref, rows_ref):
    tiles = acc_ref.shape[0]
    returned = [[ref[part] for part in range(2)] for ref in (from_left_ref, from_right_ref)]
    if paired:
        either = [x + y for x, y in zip(*returned)]
        high = lax.axis_index("orb") >= 2
        returned = [
            [jnp.where(high, x, 0.0) for x in either],
            [jnp.where(high, 0.0, x) for x in either],
        ]
    group = out_ref.shape[2]
    per_tile = TILE // W
    for t in range(tiles):
        for part in range(2):
            base = part * TILE
            x = acc_ref[t, base : base + TILE, :]
            rows_ref[t, part] = x
            if t == 0:
                extra = own_ref[0, part] + returned[0][part]
                rows_ref[t, part, :MARGIN, :LANES] = x[:MARGIN, :LANES] + extra
            if t == tiles - 1:
                extra = own_ref[1, part] + returned[1][part]
                rows_ref[t, part, MARGIN:, LANES:] = x[MARGIN:, LANES:] + extra
    low = lax.broadcasted_iota(jnp.int32, (W, LANES), 1) < MARGIN
    width = TILE + 2 * MARGIN
    for a in range(per_tile):
        for t in range(tiles):
            atom = t * per_tile + a
            for part in range(2):
                x = rows_ref[t, part, a * W : (a + 1) * W, :]
                before = pltpu.roll(x, (width - a * W) % width, 1)[:, :LANES]
                after = pltpu.roll(x, (width - (a + 1) * W) % width, 1)[:, :LANES]
                out_ref[atom // group, part, atom % group] = jnp.where(low, before, after)


def band(acc, own, from_left, from_right, energies, paired):
    tiles = acc.shape[0]
    atoms = tiles * TILE // W
    vmem = pl.BlockSpec(memory_space=pltpu.VMEM)
    return pl.pallas_call(
        functools.partial(band_kernel, paired),
        out_shape=jax.ShapeDtypeStruct((energies, 2, atoms // energies, W, LANES), F32),
        in_specs=[vmem] * 4,
        out_specs=vmem,
        scratch_shapes=[pltpu.VMEM((tiles, 2, TILE, TILE + 2 * MARGIN), F32)],
        compiler_params=pltpu.CompilerParams(vmem_limit_bytes=16 << 20),
        name="band",
    )(acc, own, from_left, from_right)


def scatter_kernel(
    recv_ref, where_ref, mix_ref, dham_ref, out_ref, smeared_ref, result_ref, factor_ref
):
    energies, _, group, _, _ = recv_ref.shape
    padded = dham_ref.shape[1]
    pairs = out_ref.shape[1]
    columns = [
        recv_ref[:, :, a, :, :].reshape(energies * 2 * W, LANES) for a in range(group)
    ]
    received = halves(jnp.concatenate(columns, axis=1))
    mixed = jnp.concatenate(halves(dot3(halves(mix_ref[...]), received, NN)), axis=0)
    rows = smeared_ref.shape[0]
    entry = lax.broadcasted_iota(jnp.int32, (group * LANES, padded), 0)
    offset = entry - where_ref[...] * W
    for j in range(0, W, 2):
        pick = jnp.concatenate(
            [jnp.where(offset == j + n, 1.0, 0.0).astype(BF16) for n in range(2)], axis=1
        )
        both = dot(mixed, pick, NN)
        smeared_ref[:, j * padded : (j + 2) * padded] = both[:rows] + both[rows:]
    for row in range(dham_ref.shape[0]):
        factor_ref[row] = jnp.broadcast_to(dham_ref[row : row + 1, :], (energies, padded))

    def block(part, j, k):
        row = (part * W + j) * energies
        return smeared_ref[row : row + energies, k * padded : (k + 1) * padded]

    for part in range(2):
        for i in range(W):
            total = [None] * W
            for c in range(3):
                factors = [factor_ref[(c * W + i) * W + j] for j in range(W)]
                for k in range(W):
                    t = None
                    for j in range(W):
                        term = factors[j] * block(part, j, k)
                        t = term if t is None else t + term
                    for l in range(W):
                        term = t * factor_ref[(c * W + l) * W + k]
                        total[l] = term if total[l] is None else total[l] + term
            for l in range(W):
                row = ((part * W + i) * W + l) * energies
                result_ref[row : row + energies, :] = total[l]
    for e in range(energies):
        one = result_ref[pl.ds(e, 2 * W * W, stride=energies), :]
        out_ref[e] = one.T[:pairs, :]


def scatter(recv, where, mix, dham, pairs):
    energies, _, group, _, _ = recv.shape
    padded = dham.shape[1]
    vmem = pl.BlockSpec(memory_space=pltpu.VMEM)
    return pl.pallas_call(
        scatter_kernel,
        out_shape=jax.ShapeDtypeStruct((energies, pairs, 2 * W * W), F32),
        in_specs=[vmem] * 4,
        out_specs=vmem,
        scratch_shapes=[
            pltpu.VMEM((2 * W * energies, W * padded), F32),
            pltpu.VMEM((2 * W * W * energies, padded), F32),
            pltpu.VMEM((dham.shape[0], energies, padded), F32),
        ],
        compiler_params=pltpu.CompilerParams(vmem_limit_bytes=24 << 20),
        name="scatter",
    )(recv, where, mix, dham)


def build_kernel(phonon_shift, phonon_weight, energies):
    rows_e = jnp.arange(energies, dtype=jnp.int32)[None, :, None]
    cols_f = jnp.arange(energies, dtype=jnp.int32)[None, None, :]
    shifts = phonon_shift[:, None, None]
    emission = (cols_f == rows_e + shifts).astype(F32)
    absorption = (cols_f == rows_e - shifts).astype(F32)
    terms = (
        phonon_weight[0][:, None, None] * emission + phonon_weight[1][:, None, None] * absorption
    )
    return jnp.sum(terms, axis=0)


def build_mix(phonon_shift, phonon_weight, energies):
    kernel = build_kernel(phonon_shift, phonon_weight, energies)
    same = jnp.eye(2 * W, dtype=F32)
    mix = same[:, None, None, :] * kernel[None, :, :, None]
    return mix.reshape(2 * W * energies, energies * 2 * W)


def send(x, pairs):
    return lax.ppermute(x, "orb", pairs)


def per_device(green, sigma, neighbours, phonon_shift, phonon_weight, dham):
    energies = lax.axis_size("energy")
    peers = lax.axis_size("orb")
    e, z = lax.axis_index("energy"), lax.axis_index("orb")
    rows = green.shape[2]
    atoms = rows // W
    degree = neighbours.shape[1]
    group = atoms // energies
    pairs = group * degree
    padded = -(-pairs // LANES) * LANES
    held = sigma.shape[1]

    far, paired = is_far(peers), peers == 4
    up = [(i, i + 1) for i in range(peers - 1)]
    down = [(i + 1, i) for i in range(peers - 1)]
    fixed = pltpu.with_memory_space_constraint(green, pltpu.HBM)
    if paired:
        ends, middle, outward = [(0, 1), (3, 2)], [(1, 2), (2, 1)], [(1, 0), (2, 3)]
        aside, across = send(sigma, ends + outward), send(sigma, middle)
        wanted = [
            (MARGIN, lambda z, rows: jnp.where(z == 0, rows - MARGIN, 0)),
            (HALF, lambda z, rows: jnp.where(z == 1, rows - HALF, 0)),
        ]
    else:
        right, left = send(sigma, up), send(sigma, down)
        wanted = [
            (HALF, lambda z, rows: jnp.where(z == 0, rows - MARGIN, HALF)),
            (HALF, lambda z, rows: rows - HALF),
            (HALF, lambda z, rows: 0 * z),
        ]

    mine = lax.dynamic_slice_in_dim(neighbours, e * group, group, axis=0)
    first = z * atoms + e * group
    offset = mine - (first + jnp.arange(group, dtype=jnp.int32))[:, None]
    column = jnp.where(offset < 0, offset + REACH, offset + REACH - 1)
    where = column + 2 * REACH * jnp.arange(group, dtype=jnp.int32)[:, None]
    where = jnp.pad(where.reshape(1, pairs), ((0, 0), (0, padded - pairs)), constant_values=-1)
    mix = build_mix(phonon_shift, phonon_weight, energies)
    factors = lax.dynamic_slice_in_dim(
        dham.transpose(1, 2, 3, 0).reshape(3 * W * W, -1), e * pairs, pairs, axis=1
    )
    factors = jnp.pad(factors, ((0, 0), (0, padded - pairs)))


    acc, keep_hi, keep_lo, hi, lo, outer, near, *nearer = own_part(
        fixed,
        pltpu.with_memory_space_constraint(sigma, pltpu.HBM),
        wanted,
        [where, mix, factors],
    )
    keeps = [keep_hi, keep_lo]
    more = functools.partial(lesser_part, hi, lo, held=held)
    places = [[neighbour(0)]]
    if paired:
        (aside,) = gate([aside], [keeps[-1]])
        (across,) = gate([across], [aside])
        second_across, second_aside = send(aside, middle), send(across, outward)
        halos = [send(outer, ends), send(near, middle)]
        places.append([beside, reflected(3, True)])
        acc, *kept = more(acc, [aside, across], places[-1])
        keeps += kept
        (second_across,) = gate([second_across], [kept[-1]])
        third_aside = send(second_across, outward)
        places.append([two_off(True), two_off(False)])
        acc, *kept = more(acc, [second_across, second_aside], places[-1])
        keeps += kept
        shards = [*places[:-1], places[-1][:1]]
        to_end, own = pair_edge_part(halos[0], keeps, shards, held)
        back_right = send(to_end, outward)
        to_middle, own = pair_edge_part(halos[1], keeps, shards, held, own)
        back_left = send(to_middle, middle)
        (acc,) = more(acc, [third_aside], [reflected(3, False)], after=[to_middle], keep=False)
        (back_right,) = gate([back_right], [acc])
    else:
        near_right = send(near, up[:-1] if far else up)
        near_left = send(nearer[0], down[1:] if far else down)
        if far:
            other = send(outer, [(0, 1), (peers - 1, peers - 2)])
        else:
            other = jnp.zeros_like(near_left)
        for k in range(1, peers):
            around = [neighbour(-k), neighbour(k)]
            if k < peers - 1:
                right, left = gate([right, left], [keeps[-1], outer if k == 1 else other])
                following = send(right, up[k:]), send(left, down[: peers - 1 - k])
                after = []
            else:
                if not far:
                    acc, *kept = more(acc, [right, left], around)
                    keeps += kept
                    places.append(around)
                to_left, to_right, own = edge_part(
                    [other, near_right, near_left], keeps, places, held
                )
                back_right = send(to_left, down[:-1] if far else down)
                back_left = send(to_right, up[1:] if far else up)
                after = [to_left]
                if not far:
                    break
            acc, *kept = more(acc, [right, left], around, after=after, keep=k < peers - 1)
            keeps += kept
            places.append(around)
            if k < peers - 1:
                right, left = following
    lesser = band(acc, own, back_left, back_right, energies, paired)

    recv = lax.all_to_all(lesser, "energy", split_axis=0, concat_axis=0, tiled=True)
    spread = scatter(recv, where, mix, factors, pairs)
    result = lax.all_to_all(spread, "energy", split_axis=0, concat_axis=0, tiled=True)
    return result.reshape(1, atoms * degree, 2 * W * W)


def solution(mesh):
    return jax.shard_map(
        per_device,
        mesh=mesh,
        in_specs=(
            P("energy", None, "orb", None),
            P("energy", "orb", None, None, None),
            P("orb", None),
            P(),
            P(),
            P("orb", None, None, None),
        ),
        out_specs=P("energy", "orb", None),
        check_vma=False,
    )
```
